32 devices in a mesh: chan: 4 (over z), tm: 8 (over y, x, core).
Axes of the slice: x: 2, y: 2, z: 4, core: 2. Of those that a mesh axis runs over, the one named last changes fastest.
Arguments:
- strain_rate: float32 [1024, 4096], P('chan', 'tm'), may hold values from -64 to 64
Outputs:
- stacks: float32 [32, 2, 13056], P('chan', None, 'tm')
The draws below stay inside these ranges and needn't reach their ends.
All inputs are finite; a program needn't handle non-finite values.
Results may differ from the reference program's by a relative error of at most 0.0041.
Values may be sent and summed in bfloat16 or wider, within the bound.
No kernel may reach another device: no remote copies, remote signals or barrier semaphores. Data moves between devices by JAX's collectives and lax.ppermute only.
A program may use at most 64 MiB of HBM per device.

```python
import math
import jax
import jax.numpy as jnp
from jax import lax

CB = 256
SRC = 8
TS = 512
MAXLAG = 25
W2 = 64
LAGS = 51
N_CHAN = 4
N_TM = 8


def draw_strain_rate(key, part):
    key_chan, key_seg, key_noise = jax.random.split(key, 3)
    channels = CB * N_CHAN
    samples = TS * N_TM
    chan_gain = jnp.exp(jax.random.uniform(key_chan, (channels, 1), jnp.float32, 0.0, math.log(4.0)))
    seg_gain = jnp.exp(jax.random.uniform(key_seg, (channels, samples // 32), jnp.float32, math.log(0.5), math.log(4.0)))
    noise = jax.random.truncated_normal(key_noise, -4.0, 4.0, (channels, samples), jnp.float32)
    seg_gain = jnp.repeat(seg_gain, 32, axis=1)
    return (noise * chan_gain * seg_gain).astype(jnp.float32)


def setup_inputs(seed: int = 0) -> dict:
    keys = jax.random.split(jax.random.key(seed), 2)
    strain_rate = draw_strain_rate(jax.random.fold_in(keys[1], 71), 0)
    return {"strain_rate": strain_rate}


def running_level(strain_rate):
    magnitude = jnp.abs(strain_rate)
    window_sums = lax.reduce_window(magnitude, jnp.zeros((), magnitude.dtype), lax.add, (1, 2 * W2 + 1), (1, 1), ((0, 0), (W2, W2)))
    return window_sums / (2 * W2 + 1) + 1e-05

def lag_sources(source_shards):
    padded = jnp.pad(source_shards, ((0, 0), (0, 0), (MAXLAG, MAXLAG)))
    windows = [padded[:, :, 2 * MAXLAG - position:2 * MAXLAG - position + TS] for position in range(LAGS)]
    return jnp.stack(windows, axis=1)

def block_stack(source_rows, receivers):
    source_shards = source_rows.reshape(SRC, N_TM, TS).astype(jnp.float32)
    receiver_shards = receivers.reshape(CB, N_TM, TS).astype(jnp.float32)
    lagged = lag_sources(source_shards)
    product = jnp.einsum('slku,bku->ksbl', lagged, receiver_shards)
    partial_value = product * (1.0 / math.sqrt(TS * N_TM))
    return lax.optimization_barrier(jnp.sum(partial_value, axis=0)).reshape(SRC, CB * LAGS)

def reference(strain_rate):
    normed = (strain_rate / running_level(strain_rate)).astype(jnp.bfloat16)
    blocks = normed.reshape(N_CHAN, CB, TS * N_TM)
    sources = blocks[:, ::CB // SRC, :]
    reach_steps = N_CHAN // 4
    offsets = list(range(-reach_steps, 0)) + list(range(1, reach_steps + 1))
    per_offset = []
    for offset in offsets:
        rolled = jnp.roll(blocks, -offset, axis=0)
        per_offset.append(lax.map(lambda pieces: block_stack(pieces[0], pieces[1]), (sources, rolled)))
    stacks = jnp.stack(per_offset, axis=1)
    return jnp.transpose(stacks, (0, 2, 1, 3)).reshape(N_CHAN * SRC, 2 * reach_steps, CB * LAGS)
```

```python
import functools
import math

import jax
import jax.numpy as jnp
from jax import lax
from jax.experimental import pallas as pl
from jax.experimental.pallas import tpu as pltpu
from jax.sharding import PartitionSpec as P

SRC = 8
MAXLAG = 25
W2 = 64
LAGS = 51
FINE = 8
COARSE = -(-LAGS // FINE)
LANES = 128
PAD = 128


def passed_along(block, axis, distance):
    devices = range(lax.axis_size(axis))
    route = [((i - distance) % len(devices), i) for i in devices]
    return lax.ppermute(block, axis, route)


def window_band(inner):
    shape = (inner + 2 * LANES, inner)
    p = lax.broadcasted_iota(jnp.int32, shape, 0) - LANES
    t = lax.broadcasted_iota(jnp.int32, shape, 1)
    return jnp.where(jnp.abs(p - t) <= W2, 1.0, 0.0).astype(jnp.bfloat16)


def normalised(rows_ref, k, shards, band):
    x = rows_ref[k]
    height, length = x.shape
    inner = band.shape[1]
    before = jnp.abs(rows_ref[max(k - 1, 0), :, length - LANES :])
    after = jnp.abs(rows_ref[min(k + 1, shards - 1), :, :LANES])
    if k == 0:
        before = jnp.zeros_like(before)
    if k == shards - 1:
        after = jnp.zeros_like(after)
    magnitude = jnp.concatenate([before, jnp.abs(x), after], axis=1)
    high = magnitude.astype(jnp.bfloat16)
    low = (magnitude - high.astype(jnp.float32)).astype(jnp.bfloat16)
    pieces = []
    for part in (high, low):
        for start in range(0, length, inner):
            pieces.append(part[:, start : start + inner + 2 * LANES])
    sums = jnp.dot(
        jnp.concatenate(pieces, axis=0), band, preferred_element_type=jnp.float32
    )
    chunks = length // inner
    window_sums = jnp.concatenate(
        [
            sums[c * height : (c + 1) * height]
            + sums[(chunks + c) * height : (chunks + c + 1) * height]
            for c in range(chunks)
        ],
        axis=1,
    )
    return x / (window_sums / (2 * W2 + 1) + 1e-05)


def correlate_kernel(shards, group, offsets, scale, rows_ref, *refs):
    outs, (mixed, table) = refs[:offsets], refs[offsets:]
    sources = offsets * SRC
    length = rows_ref.shape[2]
    band = window_band(min(256, length))
    product = None
    for k in range(shards):
        normed = normalised(rows_ref, k, shards, band)
        wide = jnp.concatenate(
            [normed, jnp.zeros((normed.shape[0], PAD), jnp.float32)], axis=1
        )
        receivers, senders = wide[:group], wide[group:]
        coarse = [
            pltpu.roll(senders, FINE * i, 1) if i else senders for i in range(COARSE)
        ]
        fine = [pltpu.roll(receivers, MAXLAG - j, 1) for j in range(FINE)]
        term = lax.dot_general(
            jnp.concatenate(fine, axis=0).astype(jnp.bfloat16),
            jnp.concatenate(coarse, axis=0).astype(jnp.bfloat16),
            (((1,), (1,)), ((), ())),
            preferred_element_type=jnp.float32,
        )
        product = term if product is None else product + term
    product = product * scale
    for h in range(mixed.shape[0]):
        first, last = h * LANES, min((h + 1) * LANES, COARSE * sources)
        for j in range(FINE):
            mixed[h, pl.ds(j, group, stride=FINE), : last - first] = product[
                j * group : (j + 1) * group, first:last
            ]
        table[h * LANES : (h + 1) * LANES] = mixed[h].T
    lane = lax.broadcasted_iota(jnp.int32, (sources, LANES), 1)
    width = group * LAGS
    tiles = [None] * -(-width // LANES)

    def place(tile, piece, low, high):
        if tiles[tile] is None:
            tiles[tile] = piece
        elif low == 0:
            tiles[tile] = jnp.where(lane < high, piece, tiles[tile])
        else:
            tiles[tile] = jnp.where(lane >= low, piece, tiles[tile])

    for b in range(group):
        column = b * FINE
        for i in range(COARSE):
            piece = table[
                i * sources : (i + 1) * sources,
                column // LANES * LANES : (column // LANES + 1) * LANES,
            ]
            start = b * LAGS + i * FINE
            shift = (start - column) % LANES
            if shift:
                piece = pltpu.roll(piece, shift, 1)
            count = min(FINE, LAGS - i * FINE)
            tile, low = start // LANES, start % LANES
            place(tile, piece, low, LANES)
            if low + count > LANES:
                tiles[tile + 1] = piece
    for tile, value in enumerate(tiles):
        first = tile * LANES
        last = min(first + LANES, width)
        for o in range(offsets):
            outs[o][:, first:last] = value[o * SRC : (o + 1) * SRC, : last - first]


def correlated(rows, group, offsets, scale):
    shards, _, length = rows.shape
    sources = offsets * SRC
    columns = -(-group * FINE // LANES) * LANES
    heights = -(-COARSE * sources // LANES) * LANES
    flops = 2 * shards * (length + PAD) * group * FINE * COARSE * sources
    width = group * LAGS
    return pl.pallas_call(
        functools.partial(correlate_kernel, shards, group, offsets, scale),
        out_shape=[jax.ShapeDtypeStruct((SRC, width), jnp.float32)] * offsets,
        in_specs=[pl.BlockSpec(memory_space=pltpu.VMEM)],
        out_specs=[pl.BlockSpec(memory_space=pltpu.VMEM)] * offsets,
        scratch_shapes=[
            pltpu.VMEM((heights // LANES, columns, LANES), jnp.float32),
            pltpu.VMEM((heights, columns), jnp.float32),
        ],
        compiler_params=pltpu.CompilerParams(vmem_limit_bytes=48 * 1024 * 1024),
        cost_estimate=pl.CostEstimate(
            flops=flops, bytes_accessed=rows.size * 4, transcendentals=0
        ),
    )(rows)


def body(strain_rate):
    channels, length = strain_rate.shape
    shards = lax.axis_size("tm")
    reach = lax.axis_size("chan") // 4
    group = channels // shards
    steps = list(range(-reach, 0)) + list(range(1, reach + 1))
    scale = 1.0 / math.sqrt(length * shards)
    own_sources = strain_rate[:: channels // SRC]
    sources = jnp.concatenate([passed_along(own_sources, "chan", d) for d in steps])
    outgoing = jnp.concatenate(
        [
            strain_rate.reshape(shards, group, length),
            jnp.broadcast_to(sources[None], (shards,) + sources.shape),
        ],
        axis=1,
    )
    rows = lax.all_to_all(outgoing, "tm", 0, 0, tiled=True)
    results = correlated(rows, group, len(steps), scale)
    return jnp.stack(
        [passed_along(r, "chan", -d) for r, d in zip(results, steps)], axis=1
    )


def solution(mesh):
    placed = (P("chan", "tm"),)
    return jax.shard_map(
        body, mesh=mesh, in_specs=placed, out_specs=P("chan", None, "tm"), check_vma=False
    )
```

```python
import functools
import math

import jax
import jax.numpy as jnp
from jax import lax
from jax.experimental import pallas as pl
from jax.experimental.pallas import tpu as pltpu
from jax.sharding import PartitionSpec as P

SRC = 8
MAXLAG = 25
W2 = 64
LAGS = 51
FINE = 8
COARSE = -(-LAGS // FINE)
LANES = 128
PAD = 128


def passed_along(block, axis, distance):
    devices = range(lax.axis_size(axis))
    route = [((i - distance) % len(devices), i) for i in devices]
    return lax.ppermute(block, axis, route)


def window_band(inner):
    shape = (inner + 2 * LANES, inner)
    p = lax.broadcasted_iota(jnp.int32, shape, 0) - LANES
    t = lax.broadcasted_iota(jnp.int32, shape, 1)
    return jnp.where(jnp.abs(p - t) <= W2, 1.0, 0.0).astype(jnp.bfloat16)


def normalised(blocks, m, first, last, band):
    shards = len(blocks)
    x = blocks[m][...]
    height, length = x.shape
    inner = band.shape[1]
    before = jnp.abs(blocks[(m - 1) % shards][:, length - LANES :])
    after = jnp.abs(blocks[(m + 1) % shards][:, :LANES])
    before = jnp.where(first, jnp.zeros_like(before), before)
    after = jnp.where(last, jnp.zeros_like(after), after)
    magnitude = jnp.concatenate([before, jnp.abs(x), after], axis=1)
    high = magnitude.astype(jnp.bfloat16)
    low = (magnitude - high.astype(jnp.float32)).astype(jnp.bfloat16)
    pieces = []
    for part in (high, low):
        for start in range(0, length, inner):
            pieces.append(part[:, start : start + inner + 2 * LANES])
    sums = jnp.dot(
        jnp.concatenate(pieces, axis=0), band, preferred_element_type=jnp.float32
    )
    chunks = length // inner
    window_sums = jnp.concatenate(
        [
            sums[c * height : (c + 1) * height]
            + sums[(chunks + c) * height : (chunks + c + 1) * height]
            for c in range(chunks)
        ],
        axis=1,
    )
    return x / (window_sums / (2 * W2 + 1) + 1e-05)


def correlate_kernel(shards, group, offsets, scale, *refs):
    receiver_refs, refs = refs[:shards], refs[shards:]
    sender_refs, refs = refs[:shards], refs[shards:]
    outs, (mixed, table) = refs[:offsets], refs[offsets:]
    sources = offsets * SRC
    length = receiver_refs[0].shape[1]
    band = window_band(min(256, length))
    me = lax.axis_index("tm")
    product = None
    for m in range(shards):
        shard = lax.rem(me + m, shards)
        wides = []
        for blocks in (receiver_refs, sender_refs):
            normed = normalised(blocks, m, shard == 0, shard == shards - 1, band)
            wides.append(
                jnp.concatenate(
                    [normed, jnp.zeros((normed.shape[0], PAD), jnp.float32)], axis=1
                )
            )
        receivers, senders = wides
        coarse = [
            pltpu.roll(senders, FINE * i, 1) if i else senders for i in range(COARSE)
        ]
        fine = [pltpu.roll(receivers, MAXLAG - j, 1) for j in range(FINE)]
        term = lax.dot_general(
            jnp.concatenate(fine, axis=0).astype(jnp.bfloat16),
            jnp.concatenate(coarse, axis=0).astype(jnp.bfloat16),
            (((1,), (1,)), ((), ())),
            preferred_element_type=jnp.float32,
        )
        product = term if product is None else product + term
    product = product * scale
    for h in range(mixed.shape[0]):
        first, last = h * LANES, min((h + 1) * LANES, COARSE * sources)
        for j in range(FINE):
            mixed[h, pl.ds(j, group, stride=FINE), : last - first] = product[
                j * group : (j + 1) * group, first:last
            ]
        table[h * LANES : (h + 1) * LANES] = mixed[h].T
    lane = lax.broadcasted_iota(jnp.int32, (sources, LANES), 1)
    width = group * LAGS
    tiles = [None] * -(-width // LANES)

    def place(tile, piece, low, high):
        if tiles[tile] is None:
            tiles[tile] = piece
        elif low == 0:
            tiles[tile] = jnp.where(lane < high, piece, tiles[tile])
        else:
            tiles[tile] = jnp.where(lane >= low, piece, tiles[tile])

    for b in range(group):
        column = b * FINE
        for i in range(COARSE):
            piece = table[
                i * sources : (i + 1) * sources,
                column // LANES * LANES : (column // LANES + 1) * LANES,
            ]
            start = b * LAGS + i * FINE
            shift = (start - column) % LANES
            if shift:
                piece = pltpu.roll(piece, shift, 1)
            count = min(FINE, LAGS - i * FINE)
            tile, low = start // LANES, start % LANES
            place(tile, piece, low, LANES)
            if low + count > LANES:
                tiles[tile + 1] = piece
    for tile, value in enumerate(tiles):
        first = tile * LANES
        last = min(first + LANES, width)
        for o in range(offsets):
            outs[o][:, first:last] = value[o * SRC : (o + 1) * SRC, : last - first]


def pack_kernel(shards, group, x_ref, *refs):
    blocks, (sources, held, sems) = refs[:shards], refs[shards:]
    me = lax.axis_index("tm")
    every = x_ref.shape[0] // SRC
    copies = [
        pltpu.make_async_copy(
            x_ref.at[pl.ds(q * every, SRC)], held.at[q], sems.at[shards + q]
        )
        for q in range(SRC)
    ]
    for m in range(shards):
        start = pl.multiple_of(lax.rem(me - m + shards, shards) * group, group)
        copies.append(
            pltpu.make_async_copy(x_ref.at[pl.ds(start, group)], blocks[m], sems.at[m])
        )
    for copy in copies:
        copy.start()
    for copy in copies:
        copy.wait()
    for q in range(SRC):
        sources[q : q + 1] = held[q, 0:1]


def packed(x, shards, group):
    length = x.shape[1]
    block = jax.ShapeDtypeStruct((group, length), x.dtype)
    out = pl.pallas_call(
        functools.partial(pack_kernel, shards, group),
        out_shape=[block] * shards + [jax.ShapeDtypeStruct((SRC, length), x.dtype)],
        in_specs=[pl.BlockSpec(memory_space=pl.ANY)],
        out_specs=[pl.BlockSpec(memory_space=pltpu.VMEM)] * (shards + 1),
        scratch_shapes=[
            pltpu.VMEM((SRC, SRC, length), x.dtype),
            pltpu.SemaphoreType.DMA((shards + SRC,)),
        ],
        cost_estimate=pl.CostEstimate(
            flops=0, bytes_accessed=x.size * 8, transcendentals=0
        ),
    )(x)
    return out[:shards], out[shards]


def correlated(receivers, senders, offsets, scale):
    shards = len(receivers)
    group, length = receivers[0].shape
    sources = offsets * SRC
    columns = -(-group * FINE // LANES) * LANES
    heights = -(-COARSE * sources // LANES) * LANES
    flops = 2 * shards * (length + PAD) * group * FINE * COARSE * sources
    width = group * LAGS
    return pl.pallas_call(
        functools.partial(correlate_kernel, shards, group, offsets, scale),
        out_shape=[jax.ShapeDtypeStruct((SRC, width), jnp.float32)] * offsets,
        in_specs=[pl.BlockSpec(memory_space=pltpu.VMEM)] * (2 * shards),
        out_specs=[pl.BlockSpec(memory_space=pltpu.VMEM)] * offsets,
        scratch_shapes=[
            pltpu.VMEM((heights // LANES, columns, LANES), jnp.float32),
            pltpu.VMEM((heights, columns), jnp.float32),
        ],
        compiler_params=pltpu.CompilerParams(vmem_limit_bytes=40 * 1024 * 1024),
        cost_estimate=pl.CostEstimate(
            flops=flops,
            bytes_accessed=shards * (group + sources) * length * 4,
            transcendentals=0,
        ),
    )(*receivers, *senders)


def body(strain_rate):
    channels, length = strain_rate.shape
    shards = lax.axis_size("tm")
    reach = lax.axis_size("chan") // 4
    group = channels // shards
    steps = list(range(-reach, 0)) + list(range(1, reach + 1))
    scale = 1.0 / math.sqrt(length * shards)
    blocks, own_sources = packed(strain_rate, shards, group)
    arrived = [passed_along(own_sources, "chan", d) for d in steps]
    receivers = [blocks[0]]
    for m in range(1, shards):
        receivers.append(passed_along(blocks[m], "tm", -m))
    sources = jnp.concatenate(arrived)
    senders = [sources] + [passed_along(sources, "tm", -m) for m in range(1, shards)]
    results = correlated(receivers, senders, len(steps), scale)
    return jnp.stack(
        [passed_along(r, "chan", -d) for r, d in zip(results, steps)], axis=1
    )


def solution(mesh):
    placed = (P("chan", "tm"),)
    return jax.shard_map(
        body, mesh=mesh, in_specs=placed, out_specs=P("chan", None, "tm"), check_vma=False
    )
```

```python
import functools
import math

import jax
import jax.numpy as jnp
from jax import lax
from jax.experimental import pallas as pl
from jax.experimental.pallas import tpu as pltpu
from jax.sharding import PartitionSpec as P

SRC = 8
MAXLAG = 25
W2 = 64
LAGS = 51
FINE = 8
COARSE = -(-LAGS // FINE)
LANES = 128
PAD = 128


def passed_along(block, axis, distance):
    devices = range(lax.axis_size(axis))
    route = [((i - distance) % len(devices), i) for i in devices]
    return lax.ppermute(block, axis, route)


def window_band(inner):
    shape = (inner + 2 * LANES, inner)
    p = lax.broadcasted_iota(jnp.int32, shape, 0) - LANES
    t = lax.broadcasted_iota(jnp.int32, shape, 1)
    return jnp.where(jnp.abs(p - t) <= W2, 1.0, 0.0).astype(jnp.bfloat16)


def normalised(rows_ref, k, band):
    x = rows_ref[k]
    shards = rows_ref.shape[0]
    height, length = x.shape
    inner = band.shape[1]
    before = jnp.abs(rows_ref[max(k - 1, 0), :, length - LANES :])
    after = jnp.abs(rows_ref[min(k + 1, shards - 1), :, :LANES])
    if k == 0:
        before = jnp.zeros_like(before)
    if k == shards - 1:
        after = jnp.zeros_like(after)
    magnitude = jnp.concatenate([before, jnp.abs(x), after], axis=1)
    high = magnitude.astype(jnp.bfloat16)
    low = (magnitude - high.astype(jnp.float32)).astype(jnp.bfloat16)
    pieces = []
    for part in (high, low):
        for start in range(0, length, inner):
            pieces.append(part[:, start : start + inner + 2 * LANES])
    sums = jnp.dot(
        jnp.concatenate(pieces, axis=0), band, preferred_element_type=jnp.float32
    )
    chunks = length // inner
    window_sums = jnp.concatenate(
        [
            sums[c * height : (c + 1) * height]
            + sums[(chunks + c) * height : (chunks + c + 1) * height]
            for c in range(chunks)
        ],
        axis=1,
    )
    return x / (window_sums / (2 * W2 + 1) + 1e-05)


def correlate_kernel(offsets, scale, receivers_ref, senders_ref, *refs):
    outs, (mixed, table) = refs[:offsets], refs[offsets:]
    sources = offsets * SRC
    shards, group, length = receivers_ref.shape
    band = window_band(min(256, length))
    product = None
    for k in range(shards):
        receivers, senders = [
            jnp.concatenate(
                [normed, jnp.zeros((normed.shape[0], PAD), jnp.float32)], axis=1
            )
            for normed in (
                normalised(receivers_ref, k, band),
                normalised(senders_ref, k, band),
            )
        ]
        coarse = [
            pltpu.roll(senders, FINE * i, 1) if i else senders for i in range(COARSE)
        ]
        fine = [pltpu.roll(receivers, MAXLAG - j, 1) for j in range(FINE)]
        term = lax.dot_general(
            jnp.concatenate(fine, axis=0).astype(jnp.bfloat16),
            jnp.concatenate(coarse, axis=0).astype(jnp.bfloat16),
            (((1,), (1,)), ((), ())),
            preferred_element_type=jnp.float32,
        )
        product = term if product is None else product + term
    product = product * scale
    for h in range(mixed.shape[0]):
        first, last = h * LANES, min((h + 1) * LANES, COARSE * sources)
        for j in range(FINE):
            mixed[h, pl.ds(j, group, stride=FINE), : last - first] = product[
                j * group : (j + 1) * group, first:last
            ]
        table[h * LANES : (h + 1) * LANES] = mixed[h].T
    lane = lax.broadcasted_iota(jnp.int32, (sources, LANES), 1)
    width = group * LAGS
    tiles = [None] * -(-width // LANES)

    def place(tile, piece, low, high):
        if tiles[tile] is None:
            tiles[tile] = piece
        elif low == 0:
            tiles[tile] = jnp.where(lane < high, piece, tiles[tile])
        else:
            tiles[tile] = jnp.where(lane >= low, piece, tiles[tile])

    for b in range(group):
        column = b * FINE
        for i in range(COARSE):
            piece = table[
                i * sources : (i + 1) * sources,
                column // LANES * LANES : (column // LANES + 1) * LANES,
            ]
            start = b * LAGS + i * FINE
            shift = (start - column) % LANES
            if shift:
                piece = pltpu.roll(piece, shift, 1)
            count = min(FINE, LAGS - i * FINE)
            tile, low = start // LANES, start % LANES
            place(tile, piece, low, LANES)
            if low + count > LANES:
                tiles[tile + 1] = piece
    for tile, value in enumerate(tiles):
        first = tile * LANES
        last = min(first + LANES, width)
        for o in range(offsets):
            outs[o][:, first:last] = value[o * SRC : (o + 1) * SRC, : last - first]


def correlated(receivers, senders, offsets, scale):
    shards, group, length = receivers.shape
    sources = offsets * SRC
    columns = -(-group * FINE // LANES) * LANES
    heights = -(-COARSE * sources // LANES) * LANES
    flops = 2 * shards * (length + PAD) * group * FINE * COARSE * sources
    width = group * LAGS
    return pl.pallas_call(
        functools.partial(correlate_kernel, offsets, scale),
        out_shape=[jax.ShapeDtypeStruct((SRC, width), jnp.float32)] * offsets,
        in_specs=[pl.BlockSpec(memory_space=pltpu.VMEM)] * 2,
        out_specs=[pl.BlockSpec(memory_space=pltpu.VMEM)] * offsets,
        scratch_shapes=[
            pltpu.VMEM((heights // LANES, columns, LANES), jnp.float32),
            pltpu.VMEM((heights, columns), jnp.float32),
        ],
        compiler_params=pltpu.CompilerParams(vmem_limit_bytes=40 * 1024 * 1024),
        cost_estimate=pl.CostEstimate(
            flops=flops,
            bytes_accessed=(receivers.size + senders.size) * 4,
            transcendentals=0,
        ),
    )(receivers, senders)


def body(strain_rate):
    channels, length = strain_rate.shape
    shards = lax.axis_size("tm")
    reach = lax.axis_size("chan") // 4
    group = channels // shards
    steps = list(range(-reach, 0)) + list(range(1, reach + 1))
    scale = 1.0 / math.sqrt(length * shards)
    own_sources = strain_rate[:: channels // SRC]
    sources = jnp.concatenate([passed_along(own_sources, "chan", d) for d in steps])
    receivers = lax.all_to_all(
        strain_rate.reshape(shards, group, length), "tm", 0, 0, tiled=True
    )
    senders = lax.all_to_all(
        jnp.broadcast_to(sources[None], (shards,) + sources.shape),
        "tm",
        0,
        0,
        tiled=True,
    )
    results = correlated(receivers, senders, len(steps), scale)
    return jnp.stack(
        [passed_along(r, "chan", -d) for r, d in zip(results, steps)], axis=1
    )


def solution(mesh):
    placed = (P("chan", "tm"),)
    return jax.shard_map(
        body, mesh=mesh, in_specs=placed, out_specs=P("chan", None, "tm"), check_vma=False
    )
```

```python
import functools
import math

import jax
import jax.numpy as jnp
from jax import lax
from jax.experimental import pallas as pl
from jax.experimental.pallas import tpu as pltpu
from jax.sharding import PartitionSpec as P

SRC = 8
MAXLAG = 25
W2 = 64
LAGS = 51
FINE = 8
COARSE = -(-LAGS // FINE)
LANES = 128
PAD = 128


def passed_along(block, axis, distance):
    devices = range(lax.axis_size(axis))
    route = [((i - distance) % len(devices), i) for i in devices]
    return lax.ppermute(block, axis, route)


def window_band(inner):
    shape = (inner + 2 * LANES, inner)
    p = lax.broadcasted_iota(jnp.int32, shape, 0) - LANES
    t = lax.broadcasted_iota(jnp.int32, shape, 1)
    return jnp.where(jnp.abs(p - t) <= W2, 1.0, 0.0).astype(jnp.bfloat16)


def normalised(rows_ref, k, band):
    x = rows_ref[k]
    shards = rows_ref.shape[0]
    height, length = x.shape
    inner = band.shape[1]
    before = jnp.abs(rows_ref[max(k - 1, 0), :, length - LANES :])
    after = jnp.abs(rows_ref[min(k + 1, shards - 1), :, :LANES])
    if k == 0:
        before = jnp.zeros_like(before)
    if k == shards - 1:
        after = jnp.zeros_like(after)
    magnitude = jnp.concatenate([before, jnp.abs(x), after], axis=1)
    high = magnitude.astype(jnp.bfloat16)
    low = (magnitude - high.astype(jnp.float32)).astype(jnp.bfloat16)
    pieces = []
    for part in (high, low):
        for start in range(0, length, inner):
            pieces.append(part[:, start : start + inner + 2 * LANES])
    sums = jnp.dot(
        jnp.concatenate(pieces, axis=0), band, preferred_element_type=jnp.float32
    )
    chunks = length // inner
    window_sums = jnp.concatenate(
        [
            sums[c * height : (c + 1) * height]
            + sums[(chunks + c) * height : (chunks + c + 1) * height]
            for c in range(chunks)
        ],
        axis=1,
    )
    return x / (window_sums / (2 * W2 + 1) + 1e-05)


def correlate_kernel(shards, offsets, scale, senders_ref, *refs):
    blocks, refs = refs[:shards], refs[shards:]
    outs, (receivers_all, senders_all, mixed, table) = refs[:offsets], refs[offsets:]
    sources = offsets * SRC
    group, length = blocks[0].shape
    me = lax.axis_index("tm")
    for m in range(shards):
        receivers_all[me ^ m] = blocks[m][...]
        senders_all[me ^ m] = senders_ref[m]
    band = window_band(min(256, length))
    product = None
    for k in range(shards):
        receivers, senders = [
            jnp.concatenate(
                [normed, jnp.zeros((normed.shape[0], PAD), jnp.float32)], axis=1
            )
            for normed in (
                normalised(receivers_all, k, band),
                normalised(senders_all, k, band),
            )
        ]
        coarse = [
            pltpu.roll(senders, FINE * i, 1) if i else senders for i in range(COARSE)
        ]
        fine = [pltpu.roll(receivers, MAXLAG - j, 1) for j in range(FINE)]
        term = lax.dot_general(
            jnp.concatenate(fine, axis=0).astype(jnp.bfloat16),
            jnp.concatenate(coarse, axis=0).astype(jnp.bfloat16),
            (((1,), (1,)), ((), ())),
            preferred_element_type=jnp.float32,
        )
        product = term if product is None else product + term
    product = product * scale
    for h in range(mixed.shape[0]):
        first, last = h * LANES, min((h + 1) * LANES, COARSE * sources)
        for j in range(FINE):
            mixed[h, pl.ds(j, group, stride=FINE), : last - first] = product[
                j * group : (j + 1) * group, first:last
            ]
        table[h * LANES : (h + 1) * LANES] = mixed[h].T
    lane = lax.broadcasted_iota(jnp.int32, (sources, LANES), 1)
    width = group * LAGS
    tiles = [None] * -(-width // LANES)

    def place(tile, piece, low, high):
        if tiles[tile] is None:
            tiles[tile] = piece
        elif low == 0:
            tiles[tile] = jnp.where(lane < high, piece, tiles[tile])
        else:
            tiles[tile] = jnp.where(lane >= low, piece, tiles[tile])

    for b in range(group):
        column = b * FINE
        for i in range(COARSE):
            piece = table[
                i * sources : (i + 1) * sources,
                column // LANES * LANES : (column // LANES + 1) * LANES,
            ]
            start = b * LAGS + i * FINE
            shift = (start - column) % LANES
            if shift:
                piece = pltpu.roll(piece, shift, 1)
            count = min(FINE, LAGS - i * FINE)
            tile, low = start // LANES, start % LANES
            place(tile, piece, low, LANES)
            if low + count > LANES:
                tiles[tile + 1] = piece
    for tile, value in enumerate(tiles):
        first = tile * LANES
        last = min(first + LANES, width)
        for o in range(offsets):
            outs[o][:, first:last] = value[o * SRC : (o + 1) * SRC, : last - first]


def pack_kernel(shards, group, x_ref, *refs):
    blocks, (sources, held, sems) = refs[:shards], refs[shards:]
    me = lax.axis_index("tm")
    every = x_ref.shape[0] // SRC
    copies = [
        pltpu.make_async_copy(
            x_ref.at[pl.ds(q * every, SRC)], held.at[q], sems.at[shards + q]
        )
        for q in range(SRC)
    ]
    for m in range(shards):
        start = pl.multiple_of((me ^ m) * group, group)
        copies.append(
            pltpu.make_async_copy(x_ref.at[pl.ds(start, group)], blocks[m], sems.at[m])
        )
    for copy in copies:
        copy.start()
    for copy in copies:
        copy.wait()
    for q in range(SRC):
        sources[q : q + 1] = held[q, 0:1]


def packed(x, shards, group):
    length = x.shape[1]
    block = jax.ShapeDtypeStruct((group, length), x.dtype)
    out = pl.pallas_call(
        functools.partial(pack_kernel, shards, group),
        out_shape=[block] * shards + [jax.ShapeDtypeStruct((SRC, length), x.dtype)],
        in_specs=[pl.BlockSpec(memory_space=pl.ANY)],
        out_specs=[pl.BlockSpec(memory_space=pltpu.VMEM)] * (shards + 1),
        scratch_shapes=[
            pltpu.VMEM((SRC, SRC, length), x.dtype),
            pltpu.SemaphoreType.DMA((shards + SRC,)),
        ],
        cost_estimate=pl.CostEstimate(
            flops=0, bytes_accessed=x.size * 8, transcendentals=0
        ),
    )(x)
    return out[:shards], out[shards]


def correlated(receivers, senders, offsets, scale):
    shards, sources, length = senders.shape
    group = receivers[0].shape[0]
    columns = -(-group * FINE // LANES) * LANES
    heights = -(-COARSE * sources // LANES) * LANES
    flops = 2 * shards * (length + PAD) * group * FINE * COARSE * sources
    width = group * LAGS
    return pl.pallas_call(
        functools.partial(correlate_kernel, shards, offsets, scale),
        out_shape=[jax.ShapeDtypeStruct((SRC, width), jnp.float32)] * offsets,
        in_specs=[pl.BlockSpec(memory_space=pltpu.VMEM)] * (1 + shards),
        out_specs=[pl.BlockSpec(memory_space=pltpu.VMEM)] * offsets,
        scratch_shapes=[
            pltpu.VMEM((shards, group, length), jnp.float32),
            pltpu.VMEM((shards, sources, length), jnp.float32),
            pltpu.VMEM((heights // LANES, columns, LANES), jnp.float32),
            pltpu.VMEM((heights, columns), jnp.float32),
        ],
        compiler_params=pltpu.CompilerParams(vmem_limit_bytes=40 * 1024 * 1024),
        cost_estimate=pl.CostEstimate(
            flops=flops,
            bytes_accessed=shards * (group + sources) * length * 4,
            transcendentals=0,
        ),
    )(senders, *receivers)


def swapped(block, axis, m):
    devices = range(lax.axis_size(axis))
    return lax.ppermute(block, axis, [(k, k ^ m) for k in devices])


def body(strain_rate):
    channels, length = strain_rate.shape
    shards = lax.axis_size("tm")
    reach = lax.axis_size("chan") // 4
    group = channels // shards
    steps = list(range(-reach, 0)) + list(range(1, reach + 1))
    scale = 1.0 / math.sqrt(length * shards)
    blocks, own_sources = packed(strain_rate, shards, group)
    senders = jnp.concatenate([passed_along(own_sources, "chan", d) for d in steps])[None]
    receivers = [blocks[0]] + [swapped(blocks[m], "tm", m) for m in range(1, shards)]
    while senders.shape[0] < shards:
        senders = jnp.concatenate([senders, swapped(senders, "tm", senders.shape[0])])
    results = correlated(receivers, senders, len(steps), scale)
    return jnp.stack(
        [passed_along(r, "chan", -d) for r, d in zip(results, steps)], axis=1
    )


def solution(mesh):
    placed = (P("chan", "tm"),)
    return jax.shard_map(
        body, mesh=mesh, in_specs=placed, out_specs=P("chan", None, "tm"), check_vma=False
    )
```

```python
import functools
import math

import jax
import jax.numpy as jnp
from jax import lax
from jax.experimental import pallas as pl
from jax.experimental.pallas import tpu as pltpu
from jax.sharding import PartitionSpec as P

SRC = 8
MAXLAG = 25
W2 = 64
LAGS = 51
FINE = 8
COARSE = -(-LAGS // FINE)
LANES = 128
PAD = 128


def passed_along(block, axis, distance):
    devices = range(lax.axis_size(axis))
    route = [((i - distance) % len(devices), i) for i in devices]
    return lax.ppermute(block, axis, route)


def window_band(inner):
    shape = (inner + 2 * LANES, inner)
    p = lax.broadcasted_iota(jnp.int32, shape, 0) - LANES
    t = lax.broadcasted_iota(jnp.int32, shape, 1)
    return jnp.where(jnp.abs(p - t) <= W2, 1.0, 0.0).astype(jnp.bfloat16)


def normalised(rows_ref, k, rows, band):
    shards, _, length = rows_ref.shape
    x = rows_ref[k, rows]
    height = x.shape[0]
    inner = band.shape[1]
    before = jnp.abs(rows_ref[max(k - 1, 0), rows, length - LANES :])
    after = jnp.abs(rows_ref[min(k + 1, shards - 1), rows, :LANES])
    if k == 0:
        before = jnp.zeros_like(before)
    if k == shards - 1:
        after = jnp.zeros_like(after)
    magnitude = jnp.concatenate([before, jnp.abs(x), after], axis=1)
    high = magnitude.astype(jnp.bfloat16)
    low = (magnitude - high.astype(jnp.float32)).astype(jnp.bfloat16)
    pieces = []
    for part in (high, low):
        for start in range(0, length, inner):
            pieces.append(part[:, start : start + inner + 2 * LANES])
    sums = jnp.dot(
        jnp.concatenate(pieces, axis=0), band, preferred_element_type=jnp.float32
    )
    chunks = length // inner
    window_sums = jnp.concatenate(
        [
            sums[c * height : (c + 1) * height]
            + sums[(chunks + c) * height : (chunks + c + 1) * height]
            for c in range(chunks)
        ],
        axis=1,
    )
    return x / (window_sums / (2 * W2 + 1) + 1e-05)


def source_kernel(group, rows_ref, out_ref):
    shards, _, length = rows_ref.shape
    band = window_band(min(256, length))
    rows = slice(group, group + SRC)
    out_ref[...] = jnp.concatenate(
        [normalised(rows_ref, k, rows, band) for k in range(shards)], axis=0
    ).astype(jnp.bfloat16)


def receiver_kernel(group, rows_ref, out_ref):
    shards, _, length = rows_ref.shape
    band = window_band(min(256, length))
    for k in range(shards):
        normed = normalised(rows_ref, k, slice(0, group), band)
        wide = jnp.concatenate([normed, jnp.zeros((group, PAD), jnp.float32)], axis=1)
        fine = [pltpu.roll(wide, MAXLAG - j, 1) for j in range(FINE)]
        out_ref[k] = jnp.concatenate(fine, axis=0).astype(jnp.bfloat16)


def correlate_kernel(offsets, scale, receivers_ref, *refs):
    sender_refs, refs = refs[:offsets], refs[offsets:]
    outs, (mixed, table) = refs[:offsets], refs[offsets:]
    sources = offsets * SRC
    shards = receivers_ref.shape[0]
    group = receivers_ref.shape[1] // FINE
    held = [ref[...].astype(jnp.float32) for ref in sender_refs]
    product = None
    for k in range(shards):
        senders = jnp.concatenate([h[k * SRC : (k + 1) * SRC] for h in held], axis=0)
        senders = jnp.concatenate(
            [senders, jnp.zeros((sources, PAD), jnp.float32)], axis=1
        )
        coarse = [
            pltpu.roll(senders, FINE * i, 1) if i else senders for i in range(COARSE)
        ]
        term = lax.dot_general(
            receivers_ref[k],
            jnp.concatenate(coarse, axis=0).astype(jnp.bfloat16),
            (((1,), (1,)), ((), ())),
            preferred_element_type=jnp.float32,
        )
        product = term if product is None else product + term
    product = product * scale
    for h in range(mixed.shape[0]):
        first, last = h * LANES, min((h + 1) * LANES, COARSE * sources)
        for j in range(FINE):
            mixed[h, pl.ds(j, group, stride=FINE), : last - first] = product[
                j * group : (j + 1) * group, first:last
            ]
        table[h * LANES : (h + 1) * LANES] = mixed[h].T
    lane = lax.broadcasted_iota(jnp.int32, (sources, LANES), 1)
    width = group * LAGS
    tiles = [None] * -(-width // LANES)

    def place(tile, piece, low, high):
        if tiles[tile] is None:
            tiles[tile] = piece
        elif low == 0:
            tiles[tile] = jnp.where(lane < high, piece, tiles[tile])
        else:
            tiles[tile] = jnp.where(lane >= low, piece, tiles[tile])

    for b in range(group):
        column = b * FINE
        for i in range(COARSE):
            piece = table[
                i * sources : (i + 1) * sources,
                column // LANES * LANES : (column // LANES + 1) * LANES,
            ]
            start = b * LAGS + i * FINE
            shift = (start - column) % LANES
            if shift:
                piece = pltpu.roll(piece, shift, 1)
            count = min(FINE, LAGS - i * FINE)
            tile, low = start // LANES, start % LANES
            place(tile, piece, low, LANES)
            if low + count > LANES:
                tiles[tile + 1] = piece
    for tile, value in enumerate(tiles):
        first = tile * LANES
        last = min(first + LANES, width)
        for o in range(offsets):
            outs[o][:, first:last] = value[o * SRC : (o + 1) * SRC, : last - first]


def call(kernel, out_shape, inputs, scratch=(), flops=0):
    spec = pl.BlockSpec(memory_space=pltpu.VMEM)
    single = not isinstance(out_shape, list)
    moved = sum(v.size * v.dtype.itemsize for v in inputs)
    return pl.pallas_call(
        kernel,
        out_shape=out_shape,
        in_specs=[spec] * len(inputs),
        out_specs=spec if single else [spec] * len(out_shape),
        scratch_shapes=list(scratch),
        compiler_params=pltpu.CompilerParams(vmem_limit_bytes=32 * 1024 * 1024),
        cost_estimate=pl.CostEstimate(
            flops=flops, bytes_accessed=moved, transcendentals=0
        ),
    )(*inputs)


def body(strain_rate):
    channels, length = strain_rate.shape
    shards = lax.axis_size("tm")
    reach = lax.axis_size("chan") // 4
    group = channels // shards
    steps = list(range(-reach, 0)) + list(range(1, reach + 1))
    offsets = len(steps)
    scale = 1.0 / math.sqrt(length * shards)
    own_sources = strain_rate[:: channels // SRC]
    outgoing = jnp.concatenate(
        [
            strain_rate.reshape(shards, group, length),
            jnp.broadcast_to(own_sources[None], (shards, SRC, length)),
        ],
        axis=1,
    )
    rows = lax.all_to_all(outgoing, "tm", 0, 0, tiled=True)
    band_flops = 4 * (length + 4 * LANES) * length * shards
    sources = call(
        functools.partial(source_kernel, group),
        jax.ShapeDtypeStruct((shards * SRC, length), jnp.bfloat16),
        [rows],
        flops=band_flops * SRC,
    )
    arrived = [passed_along(sources, "chan", d) for d in steps]
    receivers = call(
        functools.partial(receiver_kernel, group),
        jax.ShapeDtypeStruct((shards, FINE * group, length + PAD), jnp.bfloat16),
        [rows],
        flops=band_flops * group,
    )
    width = group * LAGS
    columns = -(-group * FINE // LANES) * LANES
    heights = -(-COARSE * offsets * SRC // LANES) * LANES
    results = call(
        functools.partial(correlate_kernel, offsets, scale),
        [jax.ShapeDtypeStruct((SRC, width), jnp.float32)] * offsets,
        [receivers] + arrived,
        scratch=[
            pltpu.VMEM((heights // LANES, columns, LANES), jnp.float32),
            pltpu.VMEM((heights, columns), jnp.float32),
        ],
        flops=2 * receivers.size * COARSE * offsets * SRC,
    )
    return jnp.stack(
        [passed_along(r, "chan", -d) for r, d in zip(results, steps)], axis=1
    )


def solution(mesh):
    placed = (P("chan", "tm"),)
    return jax.shard_map(
        body, mesh=mesh, in_specs=placed, out_specs=P("chan", None, "tm"), check_vma=False
    )
```

```python
import functools
import math

import jax
import jax.numpy as jnp
from jax import lax
from jax.experimental import pallas as pl
from jax.experimental.pallas import tpu as pltpu
from jax.sharding import PartitionSpec as P

SRC = 8
MAXLAG = 25
W2 = 64
LAGS = 51
FINE = 8
COARSE = -(-LAGS // FINE)
LANES = 128
PAD = 128
CORES = 2


def passed_along(block, axis, distance):
    devices = range(lax.axis_size(axis))
    route = [((i - distance) % len(devices), i) for i in devices]
    return lax.ppermute(block, axis, route)


def pack_kernel(group, core_flip, x_ref, out_ref, held, sems):
    me = lax.axis_index("tm") ^ core_flip
    chips = sems.shape[0] - SRC
    every = x_ref.shape[0] // SRC
    copies = [
        pltpu.make_async_copy(
            x_ref.at[pl.ds(q * every, SRC)], held.at[q], sems.at[chips + q]
        )
        for q in range(SRC)
    ]
    for m in range(chips):
        start = pl.multiple_of((me ^ (CORES * m)) * group, group)
        copies.append(
            pltpu.make_async_copy(
                x_ref.at[pl.ds(start, group)],
                out_ref.at[pl.ds(m * group, group)],
                sems.at[m],
            )
        )
    for copy in copies:
        copy.start()
    for copy in copies:
        copy.wait()
    for q in range(SRC):
        row = chips * group + q
        out_ref[row : row + 1] = held[q, 0:1]


def band_matrix(rows, columns, related):
    p = lax.broadcasted_iota(jnp.int32, (rows, columns), 0)
    t = lax.broadcasted_iota(jnp.int32, (rows, columns), 1)
    return jnp.where(related(p, t), 1.0, 0.0).astype(jnp.bfloat16)


def halves(values):
    high = values.astype(jnp.bfloat16).astype(jnp.float32)
    return high, values - high


def banded_sums(pieces, band):
    height = pieces[0].shape[0]
    parts = [halves(piece) for piece in pieces]
    stacked = jnp.concatenate([p[0] for p in parts] + [p[1] for p in parts], axis=0)
    sums = jnp.dot(
        stacked.astype(jnp.bfloat16), band, preferred_element_type=jnp.float32
    )
    count = len(pieces)
    return [
        sums[c * height : (c + 1) * height]
        + sums[(count + c) * height : (count + c + 1) * height]
        for c in range(count)
    ]


def level(window_sums):
    return window_sums / (2 * W2 + 1) + 1e-05


def code_kernel(group, own_ref, other_ref, *outs):
    blocks, sources_ref = outs[:-1], outs[-1]
    first_core = lax.rem(lax.axis_index("tm"), CORES) == 0
    own, other = own_ref[...], other_ref[...]
    x = jnp.concatenate(
        [jnp.where(first_core, own, other), jnp.where(first_core, other, own)], axis=1
    )
    height, length = x.shape
    border = jnp.zeros((height, LANES), jnp.float32)
    magnitude = jnp.concatenate([border, jnp.abs(x), border], axis=1)
    inner = min(256, length)
    band = band_matrix(
        inner + 2 * LANES, inner, lambda p, t: jnp.abs(p - LANES - t) <= W2
    )
    sums = jnp.concatenate(
        banded_sums(
            [
                magnitude[:, start : start + inner + 2 * LANES]
                for start in range(0, length, inner)
            ],
            band,
        ),
        axis=1,
    )
    normed = x / level(sums)
    left = lax.broadcasted_iota(jnp.int32, (height, LANES), 1) < W2
    tail = length - LANES
    x_high, x_low = halves(jnp.where(left, x[:, :LANES], x[:, tail:]))
    s_high, s_low = halves(jnp.where(left, sums[:, :LANES], sums[:, tail:]))
    coded = jnp.concatenate(
        [
            jnp.where(left, x_high, normed[:, :LANES]),
            normed[:, LANES:tail],
            jnp.where(left, normed[:, tail:], x_high),
            x_low,
            s_high,
            s_low,
        ],
        axis=1,
    ).astype(jnp.bfloat16)
    for m, block in enumerate(blocks):
        block[...] = coded[m * group : (m + 1) * group]
    sources_ref[...] = coded[len(blocks) * group :]


def correlate_kernel(offsets, scale, *refs):
    chips = len(refs) - offsets - 3
    blocks, refs = refs[:chips], refs[chips:]
    outs, (held, mixed, table) = refs[:offsets], refs[offsets:]
    sources = offsets * SRC
    height, width = held.shape[1:]
    group = height - sources
    length = width - 3 * LANES
    chip = lax.div(lax.axis_index("tm"), CORES)
    for m in range(chips):
        held[chip ^ m] = blocks[m][...].astype(jnp.float32)
    left = lax.broadcasted_iota(jnp.int32, (height, LANES), 1) < W2
    tail = length - LANES
    nothing = jnp.zeros((height, LANES), jnp.float32)
    x_ends, s_ends = [], []
    for c in range(chips):
        x_ends.append(
            jnp.where(left, held[c, :, :LANES], held[c, :, tail:length])
            + held[c, :, length : length + LANES]
        )
        s_ends.append(
            held[c, :, length + LANES : length + 2 * LANES]
            + held[c, :, length + 2 * LANES :]
        )

    def meeting(ends):
        return [
            jnp.where(left, after, before)
            for before, after in zip([nothing] + ends, ends + [nothing])
        ]

    def across(p, t):
        at_p, at_t = jnp.where(p < W2, p, p - LANES), jnp.where(t < W2, t, t - LANES)
        return ((p < W2) != (t < W2)) & (jnp.abs(at_p - at_t) <= W2)

    x_meet = meeting(x_ends)
    added = banded_sums(
        [jnp.abs(x) for x in x_meet], band_matrix(LANES, LANES, across)
    )
    ends = [x / level(s + a) for x, s, a in zip(x_meet, meeting(s_ends), added)]
    shard = length // CORES
    padding = jnp.zeros((height, PAD), jnp.float32)
    product = None
    for k in range(chips * CORES):
        c, part = k // CORES, k % CORES
        pieces = [held[c, :, part * shard : (part + 1) * shard], padding]
        if part == 0:
            head = jnp.where(left, ends[c], held[c, :, :LANES])
            pieces = [head, held[c, :, LANES:shard], padding]
        if part == CORES - 1:
            last = jnp.where(left, held[c, :, tail:length], ends[c + 1])
            pieces = [held[c, :, part * shard : tail], last, padding]
        wide = jnp.concatenate(pieces, axis=1)
        receivers, senders = wide[:group], wide[group:]
        fine = [pltpu.roll(receivers, MAXLAG - j, 1) for j in range(FINE)]
        coarse = [
            pltpu.roll(senders, FINE * i, 1) if i else senders for i in range(COARSE)
        ]
        term = lax.dot_general(
            jnp.concatenate(fine, axis=0).astype(jnp.bfloat16),
            jnp.concatenate(coarse, axis=0).astype(jnp.bfloat16),
            (((1,), (1,)), ((), ())),
            preferred_element_type=jnp.float32,
        )
        product = term if product is None else product + term
    product = product * scale
    for h in range(mixed.shape[0]):
        first, last = h * LANES, min((h + 1) * LANES, COARSE * sources)
        for j in range(FINE):
            mixed[h, pl.ds(j, group, stride=FINE), : last - first] = product[
                j * group : (j + 1) * group, first:last
            ]
        table[h * LANES : (h + 1) * LANES] = mixed[h].T
    lane = lax.broadcasted_iota(jnp.int32, (sources, LANES), 1)
    width = group * LAGS
    tiles = [None] * -(-width // LANES)

    def place(tile, piece, low, high):
        if tiles[tile] is None:
            tiles[tile] = piece
        elif low == 0:
            tiles[tile] = jnp.where(lane < high, piece, tiles[tile])
        else:
            tiles[tile] = jnp.where(lane >= low, piece, tiles[tile])

    for b in range(group):
        column = b * FINE
        for i in range(COARSE):
            piece = table[
                i * sources : (i + 1) * sources,
                column // LANES * LANES : (column // LANES + 1) * LANES,
            ]
            start = b * LAGS + i * FINE
            shift = (start - column) % LANES
            if shift:
                piece = pltpu.roll(piece, shift, 1)
            count = min(FINE, LAGS - i * FINE)
            tile, low = start // LANES, start % LANES
            place(tile, piece, low, LANES)
            if low + count > LANES:
                tiles[tile + 1] = piece
    for tile, value in enumerate(tiles):
        first = tile * LANES
        last = min(first + LANES, width)
        for o in range(offsets):
            outs[o][:, first:last] = value[o * SRC : (o + 1) * SRC, : last - first]


def call(kernel, out_shape, inputs, scratch=(), flops=0, space=pltpu.VMEM):
    single = not isinstance(out_shape, list)
    spec = pl.BlockSpec(memory_space=pltpu.VMEM)
    moved = sum(v.size * v.dtype.itemsize for v in inputs)
    return pl.pallas_call(
        kernel,
        out_shape=out_shape,
        in_specs=[pl.BlockSpec(memory_space=space)] * len(inputs),
        out_specs=spec if single else [spec] * len(out_shape),
        scratch_shapes=list(scratch),
        compiler_params=pltpu.CompilerParams(vmem_limit_bytes=32 * 1024 * 1024),
        cost_estimate=pl.CostEstimate(
            flops=flops, bytes_accessed=moved, transcendentals=0
        ),
    )(*inputs)


def swapped(block, axis, m):
    devices = range(lax.axis_size(axis))
    return lax.ppermute(block, axis, [(k, k ^ m) for k in devices])


def body(strain_rate):
    channels, length = strain_rate.shape
    shards = lax.axis_size("tm")
    chips = shards // CORES
    reach = lax.axis_size("chan") // 4
    group = channels // shards
    steps = list(range(-reach, 0)) + list(range(1, reach + 1))
    offsets = len(steps)
    sources = offsets * SRC
    scale = 1.0 / math.sqrt(length * shards)
    run = CORES * length
    coded = run + 3 * LANES

    def packed(core_flip):
        return call(
            functools.partial(pack_kernel, group, core_flip),
            jax.ShapeDtypeStruct((chips * group + SRC, length), jnp.float32),
            [strain_rate],
            scratch=[
                pltpu.VMEM((SRC, SRC, length), jnp.float32),
                pltpu.SemaphoreType.DMA((chips + SRC,)),
            ],
            space=pl.ANY,
        )

    other = swapped(packed(1), "tm", 1)
    *blocks, own_sources = call(
        functools.partial(code_kernel, group),
        [jax.ShapeDtypeStruct((group, coded), jnp.bfloat16)] * chips
        + [jax.ShapeDtypeStruct((SRC, coded), jnp.bfloat16)],
        [packed(0), other],
        flops=8 * (chips * group + SRC) * run * (256 + 2 * LANES),
    )
    arrived = [passed_along(own_sources, "chan", d) for d in steps]
    blocks = [jnp.concatenate([block] + arrived) for block in blocks]
    blocks = blocks[:1] + [swapped(blocks[m], "tm", CORES * m) for m in range(1, chips)]
    columns = -(-group * FINE // LANES) * LANES
    heights = -(-COARSE * sources // LANES) * LANES
    results = call(
        functools.partial(correlate_kernel, offsets, scale),
        [jax.ShapeDtypeStruct((SRC, group * LAGS), jnp.float32)] * offsets,
        blocks,
        scratch=[
            pltpu.VMEM((chips, group + sources, coded), jnp.float32),
            pltpu.VMEM((heights // LANES, columns, LANES), jnp.float32),
            pltpu.VMEM((heights, columns), jnp.float32),
        ],
        flops=2 * shards * (length + PAD) * group * FINE * COARSE * sources,
    )
    return jnp.stack(
        [passed_along(r, "chan", -d) for r, d in zip(results, steps)], axis=1
    )


def solution(mesh):
    placed = (P("chan", "tm"),)
    return jax.shard_map(
        body, mesh=mesh, in_specs=placed, out_specs=P("chan", None, "tm"), check_vma=False
    )
```

```python
import functools
import math

import jax
import jax.numpy as jnp
from jax import lax
from jax.experimental import pallas as pl
from jax.experimental.pallas import tpu as pltpu
from jax.sharding import PartitionSpec as P

SRC = 8
MAXLAG = 25
W2 = 64
LAGS = 51
FINE = 8
COARSE = -(-LAGS // FINE)
LANES = 128
PAD = 128
CORES = 2


def passed_along(block, axis, distance):
    devices = range(lax.axis_size(axis))
    route = [((i - distance) % len(devices), i) for i in devices]
    return lax.ppermute(block, axis, route)


def band_matrix(rows, columns, related):
    p = lax.broadcasted_iota(jnp.int32, (rows, columns), 0)
    t = lax.broadcasted_iota(jnp.int32, (rows, columns), 1)
    return jnp.where(related(p, t), 1.0, 0.0).astype(jnp.bfloat16)


def halves(values):
    high = values.astype(jnp.bfloat16).astype(jnp.float32)
    return high, values - high


def banded_sums(pieces, band):
    height = pieces[0].shape[0]
    parts = [halves(piece) for piece in pieces]
    stacked = jnp.concatenate([p[0] for p in parts] + [p[1] for p in parts], axis=0)
    sums = jnp.dot(
        stacked.astype(jnp.bfloat16), band, preferred_element_type=jnp.float32
    )
    count = len(pieces)
    return [
        sums[c * height : (c + 1) * height]
        + sums[(count + c) * height : (count + c + 1) * height]
        for c in range(count)
    ]


def level(window_sums):
    return window_sums / (2 * W2 + 1) + 1e-05


def rows_for_here(ref, group, chips):
    me = lax.axis_index("tm")
    every = ref.shape[0] // SRC
    pieces = []
    for m in range(chips):
        start = pl.multiple_of((me ^ (CORES * m)) * group, group)
        pieces.append(ref[pl.ds(start, group)])
    pieces += [ref[q * every : q * every + 1] for q in range(SRC)]
    return jnp.concatenate(pieces, axis=0)


def pack_kernel(group, chips, x_ref, out_ref):
    out_ref[...] = rows_for_here(x_ref, group, chips)


def code_kernel(group, own_ref, other_ref, *outs):
    blocks, sources_ref = outs[:-1], outs[-1]
    first_core = lax.rem(lax.axis_index("tm"), CORES) == 0
    own = own_ref[...]
    other = rows_for_here(other_ref, group, len(blocks))
    x = jnp.concatenate(
        [jnp.where(first_core, own, other), jnp.where(first_core, other, own)], axis=1
    )
    height, length = x.shape
    border = jnp.zeros((height, LANES), jnp.float32)
    magnitude = jnp.concatenate([border, jnp.abs(x), border], axis=1)
    inner = min(256, length)
    band = band_matrix(
        inner + 2 * LANES, inner, lambda p, t: jnp.abs(p - LANES - t) <= W2
    )
    sums = jnp.concatenate(
        banded_sums(
            [
                magnitude[:, start : start + inner + 2 * LANES]
                for start in range(0, length, inner)
            ],
            band,
        ),
        axis=1,
    )
    normed = x / level(sums)
    left = lax.broadcasted_iota(jnp.int32, (height, LANES), 1) < W2
    tail = length - LANES
    x_high, x_low = halves(jnp.where(left, x[:, :LANES], x[:, tail:]))
    s_high, s_low = halves(jnp.where(left, sums[:, :LANES], sums[:, tail:]))
    coded = jnp.concatenate(
        [
            jnp.where(left, x_high, normed[:, :LANES]),
            normed[:, LANES:tail],
            jnp.where(left, normed[:, tail:], x_high),
            x_low,
            s_high,
            s_low,
        ],
        axis=1,
    ).astype(jnp.bfloat16)
    for m, block in enumerate(blocks):
        block[...] = coded[m * group : (m + 1) * group]
    sources_ref[...] = coded[len(blocks) * group :]


def correlate_kernel(offsets, scale, *refs):
    chips = len(refs) - offsets - 3
    blocks, refs = refs[:chips], refs[chips:]
    outs, (held, mixed, table) = refs[:offsets], refs[offsets:]
    sources = offsets * SRC
    height, width = held.shape[1:]
    group = height - sources
    length = width - 3 * LANES
    chip = lax.div(lax.axis_index("tm"), CORES)
    for m in range(chips):
        held[chip ^ m] = blocks[m][...].astype(jnp.float32)
    left = lax.broadcasted_iota(jnp.int32, (height, LANES), 1) < W2
    tail = length - LANES
    nothing = jnp.zeros((height, LANES), jnp.float32)
    x_ends, s_ends = [], []
    for c in range(chips):
        x_ends.append(
            jnp.where(left, held[c, :, :LANES], held[c, :, tail:length])
            + held[c, :, length : length + LANES]
        )
        s_ends.append(
            held[c, :, length + LANES : length + 2 * LANES]
            + held[c, :, length + 2 * LANES :]
        )

    def meeting(ends):
        return [
            jnp.where(left, after, before)
            for before, after in zip([nothing] + ends, ends + [nothing])
        ]

    def across(p, t):
        at_p, at_t = jnp.where(p < W2, p, p - LANES), jnp.where(t < W2, t, t - LANES)
        return ((p < W2) != (t < W2)) & (jnp.abs(at_p - at_t) <= W2)

    x_meet = meeting(x_ends)
    added = banded_sums(
        [jnp.abs(x) for x in x_meet], band_matrix(LANES, LANES, across)
    )
    ends = [x / level(s + a) for x, s, a in zip(x_meet, meeting(s_ends), added)]
    shard = length // CORES
    padding = jnp.zeros((height, PAD), jnp.float32)
    product = None
    for k in range(chips * CORES):
        c, part = k // CORES, k % CORES
        pieces = [held[c, :, part * shard : (part + 1) * shard], padding]
        if part == 0:
            head = jnp.where(left, ends[c], held[c, :, :LANES])
            pieces = [head, held[c, :, LANES:shard], padding]
        if part == CORES - 1:
            last = jnp.where(left, held[c, :, tail:length], ends[c + 1])
            pieces = [held[c, :, part * shard : tail], last, padding]
        wide = jnp.concatenate(pieces, axis=1)
        receivers, senders = wide[:group], wide[group:]
        fine = [pltpu.roll(receivers, MAXLAG - j, 1) for j in range(FINE)]
        coarse = [
            pltpu.roll(senders, FINE * i, 1) if i else senders for i in range(COARSE)
        ]
        term = lax.dot_general(
            jnp.concatenate(fine, axis=0).astype(jnp.bfloat16),
            jnp.concatenate(coarse, axis=0).astype(jnp.bfloat16),
            (((1,), (1,)), ((), ())),
            preferred_element_type=jnp.float32,
        )
        product = term if product is None else product + term
    product = product * scale
    for h in range(mixed.shape[0]):
        first, last = h * LANES, min((h + 1) * LANES, COARSE * sources)
        for j in range(FINE):
            mixed[h, pl.ds(j, group, stride=FINE), : last - first] = product[
                j * group : (j + 1) * group, first:last
            ]
        table[h * LANES : (h + 1) * LANES] = mixed[h].T
    lane = lax.broadcasted_iota(jnp.int32, (sources, LANES), 1)
    width = group * LAGS
    tiles = [None] * -(-width // LANES)

    def place(tile, piece, low, high):
        if tiles[tile] is None:
            tiles[tile] = piece
        elif low == 0:
            tiles[tile] = jnp.where(lane < high, piece, tiles[tile])
        else:
            tiles[tile] = jnp.where(lane >= low, piece, tiles[tile])

    for b in range(group):
        column = b * FINE
        for i in range(COARSE):
            piece = table[
                i * sources : (i + 1) * sources,
                column // LANES * LANES : (column // LANES + 1) * LANES,
            ]
            start = b * LAGS + i * FINE
            shift = (start - column) % LANES
            if shift:
                piece = pltpu.roll(piece, shift, 1)
            count = min(FINE, LAGS - i * FINE)
            tile, low = start // LANES, start % LANES
            place(tile, piece, low, LANES)
            if low + count > LANES:
                tiles[tile + 1] = piece
    for tile, value in enumerate(tiles):
        first = tile * LANES
        last = min(first + LANES, width)
        for o in range(offsets):
            rows = value[o * SRC : (o + 1) * SRC, : last - first]
            outs[o][:, first:last] = rows.astype(jnp.bfloat16)


def call(kernel, out_shape, inputs, scratch=(), flops=0):
    single = not isinstance(out_shape, list)
    spec = pl.BlockSpec(memory_space=pltpu.VMEM)
    moved = sum(v.size * v.dtype.itemsize for v in inputs)
    return pl.pallas_call(
        kernel,
        out_shape=out_shape,
        in_specs=[spec] * len(inputs),
        out_specs=spec if single else [spec] * len(out_shape),
        scratch_shapes=list(scratch),
        compiler_params=pltpu.CompilerParams(vmem_limit_bytes=32 * 1024 * 1024),
        cost_estimate=pl.CostEstimate(
            flops=flops, bytes_accessed=moved, transcendentals=0
        ),
    )(*inputs)


def swapped(block, axis, m):
    devices = range(lax.axis_size(axis))
    return lax.ppermute(block, axis, [(k, k ^ m) for k in devices])


def body(strain_rate):
    channels, length = strain_rate.shape
    shards = lax.axis_size("tm")
    chips = shards // CORES
    reach = lax.axis_size("chan") // 4
    group = channels // shards
    steps = list(range(-reach, 0)) + list(range(1, reach + 1))
    offsets = len(steps)
    sources = offsets * SRC
    scale = 1.0 / math.sqrt(length * shards)
    run = CORES * length
    coded = run + 3 * LANES

    other = swapped(strain_rate, "tm", 1)
    own = call(
        functools.partial(pack_kernel, group, chips),
        jax.ShapeDtypeStruct((chips * group + SRC, length), jnp.float32),
        [strain_rate],
        flops=8 * channels * length,
    )
    *blocks, own_sources = call(
        functools.partial(code_kernel, group),
        [jax.ShapeDtypeStruct((group, coded), jnp.bfloat16)] * chips
        + [jax.ShapeDtypeStruct((SRC, coded), jnp.bfloat16)],
        [own, other],
        flops=8 * (chips * group + SRC) * run * (256 + 2 * LANES),
    )
    arrived = [passed_along(own_sources, "chan", d) for d in steps]
    blocks = [jnp.concatenate([block] + arrived) for block in blocks]
    blocks = blocks[:1] + [swapped(blocks[m], "tm", CORES * m) for m in range(1, chips)]
    columns = -(-group * FINE // LANES) * LANES
    heights = -(-COARSE * sources // LANES) * LANES
    results = call(
        functools.partial(correlate_kernel, offsets, scale),
        [jax.ShapeDtypeStruct((SRC, group * LAGS), jnp.bfloat16)] * offsets,
        blocks,
        scratch=[
            pltpu.VMEM((chips, group + sources, coded), jnp.float32),
            pltpu.VMEM((heights // LANES, columns, LANES), jnp.float32),
            pltpu.VMEM((heights, columns), jnp.float32),
        ],
        flops=2 * shards * (length + PAD) * group * FINE * COARSE * sources,
    )
    arrived = [passed_along(r, "chan", -d) for r, d in zip(results, steps)]
    return jnp.stack(arrived, axis=1).astype(jnp.float32)


def solution(mesh):
    placed = (P("chan", "tm"),)
    return jax.shard_map(
        body, mesh=mesh, in_specs=placed, out_specs=P("chan", None, "tm"), check_vma=False
    )
```

```python
import functools
import math

import jax
import jax.numpy as jnp
from jax import lax
from jax.experimental import pallas as pl
from jax.experimental.pallas import tpu as pltpu
from jax.sharding import PartitionSpec as P

SRC = 8
MAXLAG = 25
W2 = 64
LAGS = 51
FINE = 8
COARSE = -(-LAGS // FINE)
LANES = 128
PAD = 128
CORES = 2


def passed_along(block, axis, distance):
    devices = range(lax.axis_size(axis))
    route = [((i - distance) % len(devices), i) for i in devices]
    return lax.ppermute(block, axis, route)


def band_matrix(rows, columns, related):
    p = lax.broadcasted_iota(jnp.int32, (rows, columns), 0)
    t = lax.broadcasted_iota(jnp.int32, (rows, columns), 1)
    return jnp.where(related(p, t), 1.0, 0.0).astype(jnp.bfloat16)


def halves(values):
    high = values.astype(jnp.bfloat16).astype(jnp.float32)
    return high, values - high


def banded_sums(pieces, band):
    height = pieces[0].shape[0]
    parts = [halves(piece) for piece in pieces]
    stacked = jnp.concatenate([p[0] for p in parts] + [p[1] for p in parts], axis=0)
    sums = jnp.dot(
        stacked.astype(jnp.bfloat16), band, preferred_element_type=jnp.float32
    )
    count = len(pieces)
    return [
        sums[c * height : (c + 1) * height]
        + sums[(count + c) * height : (count + c + 1) * height]
        for c in range(count)
    ]


def level(window_sums):
    return window_sums / (2 * W2 + 1) + 1e-05


def rows_for_here(ref, group, chips):
    me = lax.axis_index("tm")
    every = ref.shape[0] // SRC
    pieces = []
    for m in range(chips):
        start = pl.multiple_of((me ^ (CORES * m)) * group, group)
        pieces.append(ref[pl.ds(start, group)])
    pieces += [ref[q * every : q * every + 1] for q in range(SRC)]
    return jnp.concatenate(pieces, axis=0)


def pack_kernel(group, chips, x_ref, out_ref):
    out_ref[...] = rows_for_here(x_ref, group, chips)


def code_kernel(group, own_ref, other_ref, *outs):
    blocks, sources_ref = outs[:-1], outs[-1]
    first_core = lax.rem(lax.axis_index("tm"), CORES) == 0
    own = own_ref[...]
    other = rows_for_here(other_ref, group, len(blocks))
    x = jnp.concatenate(
        [jnp.where(first_core, own, other), jnp.where(first_core, other, own)], axis=1
    )
    height, length = x.shape
    border = jnp.zeros((height, LANES), jnp.float32)
    magnitude = jnp.concatenate([border, jnp.abs(x), border], axis=1)
    inner = min(256, length)
    band = band_matrix(
        inner + 2 * LANES, inner, lambda p, t: jnp.abs(p - LANES - t) <= W2
    )
    sums = jnp.concatenate(
        banded_sums(
            [
                magnitude[:, start : start + inner + 2 * LANES]
                for start in range(0, length, inner)
            ],
            band,
        ),
        axis=1,
    )
    normed = x / level(sums)
    left = lax.broadcasted_iota(jnp.int32, (height, LANES), 1) < W2
    tail = length - LANES
    x_high, x_low = halves(jnp.where(left, x[:, :LANES], x[:, tail:]))
    s_high, s_low = halves(jnp.where(left, sums[:, :LANES], sums[:, tail:]))
    coded = jnp.concatenate(
        [
            jnp.where(left, x_high, normed[:, :LANES]),
            normed[:, LANES:tail],
            jnp.where(left, normed[:, tail:], x_high),
            x_low,
            s_high,
            s_low,
        ],
        axis=1,
    ).astype(jnp.bfloat16)
    for m, block in enumerate(blocks):
        block[...] = coded[m * group : (m + 1) * group]
    sources_ref[...] = coded[len(blocks) * group :]


def finished_shards(blocks, held):
    chips, height, width = held.shape
    length = width - 3 * LANES
    chip = lax.div(lax.axis_index("tm"), CORES)
    for m in range(chips):
        held[chip ^ m] = blocks[m][...].astype(jnp.float32)
    left = lax.broadcasted_iota(jnp.int32, (height, LANES), 1) < W2
    tail = length - LANES
    nothing = jnp.zeros((height, LANES), jnp.float32)
    x_ends, s_ends = [], []
    for c in range(chips):
        x_ends.append(
            jnp.where(left, held[c, :, :LANES], held[c, :, tail:length])
            + held[c, :, length : length + LANES]
        )
        s_ends.append(
            held[c, :, length + LANES : length + 2 * LANES]
            + held[c, :, length + 2 * LANES :]
        )

    def meeting(ends):
        return [
            jnp.where(left, after, before)
            for before, after in zip([nothing] + ends, ends + [nothing])
        ]

    def across(p, t):
        at_p, at_t = jnp.where(p < W2, p, p - LANES), jnp.where(t < W2, t, t - LANES)
        return ((p < W2) != (t < W2)) & (jnp.abs(at_p - at_t) <= W2)

    x_meet = meeting(x_ends)
    added = banded_sums(
        [jnp.abs(x) for x in x_meet], band_matrix(LANES, LANES, across)
    )
    ends = [x / level(s + a) for x, s, a in zip(x_meet, meeting(s_ends), added)]
    shard = length // CORES
    padding = jnp.zeros((height, PAD), jnp.float32)
    for k in range(chips * CORES):
        c, part = k // CORES, k % CORES
        pieces = [held[c, :, part * shard : (part + 1) * shard], padding]
        if part == 0:
            head = jnp.where(left, ends[c], held[c, :, :LANES])
            pieces = [head, held[c, :, LANES:shard], padding]
        if part == CORES - 1:
            last = jnp.where(left, held[c, :, tail:length], ends[c + 1])
            pieces = [held[c, :, part * shard : tail], last, padding]
        yield jnp.concatenate(pieces, axis=1)


def join_kernel(offsets, *refs):
    refs[-1][...] = jnp.concatenate(
        [ref[...].astype(jnp.float32) for ref in refs[:offsets]], axis=0
    ).astype(jnp.bfloat16)


def receiver_kernel(*refs):
    *blocks, out_ref, held = refs
    for k, wide in enumerate(finished_shards(blocks, held)):
        fine = [pltpu.roll(wide, MAXLAG - j, 1) for j in range(FINE)]
        out_ref[k] = jnp.concatenate(fine, axis=0).astype(jnp.bfloat16)


def correlate_kernel(offsets, scale, receivers_ref, *refs):
    chips = len(refs) - offsets - 3
    blocks, refs = refs[:chips], refs[chips:]
    outs, (held, mixed, table) = refs[:offsets], refs[offsets:]
    sources = offsets * SRC
    group = receivers_ref.shape[1] // FINE
    product = None
    for k, wide in enumerate(finished_shards(blocks, held)):
        coarse = [pltpu.roll(wide, FINE * i, 1) if i else wide for i in range(COARSE)]
        term = lax.dot_general(
            receivers_ref[k],
            jnp.concatenate(coarse, axis=0).astype(jnp.bfloat16),
            (((1,), (1,)), ((), ())),
            preferred_element_type=jnp.float32,
        )
        product = term if product is None else product + term
    product = product * scale
    for h in range(mixed.shape[0]):
        first, last = h * LANES, min((h + 1) * LANES, COARSE * sources)
        for j in range(FINE):
            mixed[h, pl.ds(j, group, stride=FINE), : last - first] = product[
                j * group : (j + 1) * group, first:last
            ]
        table[h * LANES : (h + 1) * LANES] = mixed[h].T
    lane = lax.broadcasted_iota(jnp.int32, (sources, LANES), 1)
    width = group * LAGS
    tiles = [None] * -(-width // LANES)

    def place(tile, piece, low, high):
        if tiles[tile] is None:
            tiles[tile] = piece
        elif low == 0:
            tiles[tile] = jnp.where(lane < high, piece, tiles[tile])
        else:
            tiles[tile] = jnp.where(lane >= low, piece, tiles[tile])

    for b in range(group):
        column = b * FINE
        for i in range(COARSE):
            piece = table[
                i * sources : (i + 1) * sources,
                column // LANES * LANES : (column // LANES + 1) * LANES,
            ]
            start = b * LAGS + i * FINE
            shift = (start - column) % LANES
            if shift:
                piece = pltpu.roll(piece, shift, 1)
            count = min(FINE, LAGS - i * FINE)
            tile, low = start // LANES, start % LANES
            place(tile, piece, low, LANES)
            if low + count > LANES:
                tiles[tile + 1] = piece
    for tile, value in enumerate(tiles):
        first = tile * LANES
        last = min(first + LANES, width)
        for o in range(offsets):
            rows = value[o * SRC : (o + 1) * SRC, : last - first]
            outs[o][:, first:last] = rows.astype(jnp.bfloat16)


def call(kernel, out_shape, inputs, scratch=(), flops=0):
    single = not isinstance(out_shape, list)
    spec = pl.BlockSpec(memory_space=pltpu.VMEM)
    moved = sum(v.size * v.dtype.itemsize for v in inputs)
    return pl.pallas_call(
        kernel,
        out_shape=out_shape,
        in_specs=[spec] * len(inputs),
        out_specs=spec if single else [spec] * len(out_shape),
        scratch_shapes=list(scratch),
        compiler_params=pltpu.CompilerParams(vmem_limit_bytes=32 * 1024 * 1024),
        cost_estimate=pl.CostEstimate(
            flops=flops, bytes_accessed=moved, transcendentals=0
        ),
    )(*inputs)


def swapped(block, axis, m):
    devices = range(lax.axis_size(axis))
    return lax.ppermute(block, axis, [(k, k ^ m) for k in devices])


def body(strain_rate):
    channels, length = strain_rate.shape
    shards = lax.axis_size("tm")
    chips = shards // CORES
    reach = lax.axis_size("chan") // 4
    group = channels // shards
    steps = list(range(-reach, 0)) + list(range(1, reach + 1))
    offsets = len(steps)
    sources = offsets * SRC
    scale = 1.0 / math.sqrt(length * shards)
    run = CORES * length
    coded = run + 3 * LANES

    other = swapped(strain_rate, "tm", 1)
    own = call(
        functools.partial(pack_kernel, group, chips),
        jax.ShapeDtypeStruct((chips * group + SRC, length), jnp.float32),
        [strain_rate],
        flops=8 * channels * length,
    )
    *blocks, own_sources = call(
        functools.partial(code_kernel, group),
        [jax.ShapeDtypeStruct((group, coded), jnp.bfloat16)] * chips
        + [jax.ShapeDtypeStruct((SRC, coded), jnp.bfloat16)],
        [own, other],
        flops=8 * (chips * group + SRC) * run * (256 + 2 * LANES),
    )
    arrived = [passed_along(own_sources, "chan", d) for d in steps]

    def between_chips(pieces):
        return pieces[:1] + [
            swapped(pieces[m], "tm", CORES * m) for m in range(1, chips)
        ]

    blocks = between_chips(blocks)
    joined = call(
        functools.partial(join_kernel, offsets),
        jax.ShapeDtypeStruct((sources, coded), jnp.bfloat16),
        arrived + blocks[1:],
    )
    senders = between_chips([joined] * chips)
    receivers = call(
        receiver_kernel,
        jax.ShapeDtypeStruct((shards, FINE * group, length + PAD), jnp.bfloat16),
        blocks,
        scratch=[pltpu.VMEM((chips, group, coded), jnp.float32)],
        flops=shards * group * 2 * length * length,
    )
    columns = -(-group * FINE // LANES) * LANES
    heights = -(-COARSE * sources // LANES) * LANES
    results = call(
        functools.partial(correlate_kernel, offsets, scale),
        [jax.ShapeDtypeStruct((SRC, group * LAGS), jnp.bfloat16)] * offsets,
        [receivers] + senders,
        scratch=[
            pltpu.VMEM((chips, sources, coded), jnp.float32),
            pltpu.VMEM((heights // LANES, columns, LANES), jnp.float32),
            pltpu.VMEM((heights, columns), jnp.float32),
        ],
        flops=2 * shards * (length + PAD) * group * FINE * COARSE * sources,
    )
    arrived = [passed_along(r, "chan", -d) for r, d in zip(results, steps)]
    return jnp.stack(arrived, axis=1).astype(jnp.float32)


def solution(mesh):
    placed = (P("chan", "tm"),)
    return jax.shard_map(
        body, mesh=mesh, in_specs=placed, out_specs=P("chan", None, "tm"), check_vma=False
    )
```

```python
import functools
import math

import jax
import jax.numpy as jnp
from jax import lax
from jax.experimental import pallas as pl
from jax.experimental.pallas import tpu as pltpu
from jax.sharding import PartitionSpec as P

SRC = 8
MAXLAG = 25
W2 = 64
LAGS = 51
FINE = 8
COARSE = -(-LAGS // FINE)
LANES = 128
PAD = 128
CORES = 2


def passed_along(block, axis, distance):
    devices = range(lax.axis_size(axis))
    route = [((i - distance) % len(devices), i) for i in devices]
    return lax.ppermute(block, axis, route)


def band_matrix(rows, columns, related):
    p = lax.broadcasted_iota(jnp.int32, (rows, columns), 0)
    t = lax.broadcasted_iota(jnp.int32, (rows, columns), 1)
    return jnp.where(related(p, t), 1.0, 0.0).astype(jnp.bfloat16)


def halves(values):
    high = values.astype(jnp.bfloat16).astype(jnp.float32)
    return high, values - high


def banded_sums(pieces, band):
    height = pieces[0].shape[0]
    parts = [halves(piece) for piece in pieces]
    stacked = jnp.concatenate([p[0] for p in parts] + [p[1] for p in parts], axis=0)
    sums = jnp.dot(
        stacked.astype(jnp.bfloat16), band, preferred_element_type=jnp.float32
    )
    count = len(pieces)
    return [
        sums[c * height : (c + 1) * height]
        + sums[(count + c) * height : (count + c + 1) * height]
        for c in range(count)
    ]


def level(window_sums):
    return window_sums / (2 * W2 + 1) + 1e-05


def rows_for_here(ref, group, chips):
    me = lax.axis_index("tm")
    every = ref.shape[0] // SRC
    pieces = []
    for m in range(chips):
        start = pl.multiple_of((me ^ (CORES * m)) * group, group)
        pieces.append(ref[pl.ds(start, group)])
    pieces += [ref[q * every : q * every + 1] for q in range(SRC)]
    return jnp.concatenate(pieces, axis=0)


def pack_kernel(group, chips, x_ref, out_ref):
    out_ref[...] = rows_for_here(x_ref, group, chips)


def code_kernel(group, own_ref, other_ref, *outs):
    blocks, sources_ref = outs[:-1], outs[-1]
    first_core = lax.rem(lax.axis_index("tm"), CORES) == 0
    own = own_ref[...]
    other = rows_for_here(other_ref, group, len(blocks))
    x = jnp.concatenate(
        [jnp.where(first_core, own, other), jnp.where(first_core, other, own)], axis=1
    )
    height, length = x.shape
    border = jnp.zeros((height, LANES), jnp.float32)
    magnitude = jnp.concatenate([border, jnp.abs(x), border], axis=1)
    inner = min(256, length)
    band = band_matrix(
        inner + 2 * LANES, inner, lambda p, t: jnp.abs(p - LANES - t) <= W2
    )
    sums = jnp.concatenate(
        banded_sums(
            [
                magnitude[:, start : start + inner + 2 * LANES]
                for start in range(0, length, inner)
            ],
            band,
        ),
        axis=1,
    )
    normed = x / level(sums)
    left = lax.broadcasted_iota(jnp.int32, (height, LANES), 1) < W2
    tail = length - LANES
    x_high, x_low = halves(jnp.where(left, x[:, :LANES], x[:, tail:]))
    s_high, s_low = halves(jnp.where(left, sums[:, :LANES], sums[:, tail:]))
    coded = jnp.concatenate(
        [
            jnp.where(left, x_high, normed[:, :LANES]),
            normed[:, LANES:tail],
            jnp.where(left, normed[:, tail:], x_high),
            x_low,
            s_high,
            s_low,
        ],
        axis=1,
    ).astype(jnp.bfloat16)
    for m, block in enumerate(blocks):
        block[...] = coded[m * group : (m + 1) * group]
    sources_ref[...] = coded[len(blocks) * group :]


def finished_shards(runs, held):
    chips, height, width = held.shape
    length = width - 3 * LANES
    chip = lax.div(lax.axis_index("tm"), CORES)
    for m in range(chips):
        held[chip ^ m] = runs[m]
    left = lax.broadcasted_iota(jnp.int32, (height, LANES), 1) < W2
    tail = length - LANES
    nothing = jnp.zeros((height, LANES), jnp.float32)
    x_ends, s_ends = [], []
    for c in range(chips):
        x_ends.append(
            jnp.where(left, held[c, :, :LANES], held[c, :, tail:length])
            + held[c, :, length : length + LANES]
        )
        s_ends.append(
            held[c, :, length + LANES : length + 2 * LANES]
            + held[c, :, length + 2 * LANES :]
        )

    def meeting(ends):
        return [
            jnp.where(left, after, before)
            for before, after in zip([nothing] + ends, ends + [nothing])
        ]

    def across(p, t):
        at_p, at_t = jnp.where(p < W2, p, p - LANES), jnp.where(t < W2, t, t - LANES)
        return ((p < W2) != (t < W2)) & (jnp.abs(at_p - at_t) <= W2)

    x_meet = meeting(x_ends)
    added = banded_sums(
        [jnp.abs(x) for x in x_meet], band_matrix(LANES, LANES, across)
    )
    ends = [x / level(s + a) for x, s, a in zip(x_meet, meeting(s_ends), added)]
    shard = length // CORES
    padding = jnp.zeros((height, PAD), jnp.float32)
    for k in range(chips * CORES):
        c, part = k // CORES, k % CORES
        pieces = [held[c, :, part * shard : (part + 1) * shard], padding]
        if part == 0:
            head = jnp.where(left, ends[c], held[c, :, :LANES])
            pieces = [head, held[c, :, LANES:shard], padding]
        if part == CORES - 1:
            last = jnp.where(left, held[c, :, tail:length], ends[c + 1])
            pieces = [held[c, :, part * shard : tail], last, padding]
        yield jnp.concatenate(pieces, axis=1)


def receiver_kernel(group, *refs):
    *blocks, out_ref, held = refs
    runs = [ref[...].astype(jnp.float32)[:group] for ref in blocks]
    for k, wide in enumerate(finished_shards(runs, held)):
        fine = [pltpu.roll(wide, MAXLAG - j, 1) for j in range(FINE)]
        out_ref[k] = jnp.concatenate(fine, axis=0).astype(jnp.bfloat16)


def correlate_kernel(offsets, scale, receivers_ref, own_ref, other_ref, *refs):
    outs, (held, mixed, table) = refs[:offsets], refs[offsets:]
    chips, sources = held.shape[:2]
    group = receivers_ref.shape[1] // FINE
    first_core = lax.rem(lax.axis_index("tm"), CORES) == 0
    own, other = [ref[...].astype(jnp.float32) for ref in (own_ref, other_ref)]
    low, high = jnp.where(first_core, own, other), jnp.where(first_core, other, own)
    half = sources // CORES
    runs = [
        jnp.concatenate(
            [low[m * half : (m + 1) * half], high[m * half : (m + 1) * half]], axis=0
        )
        for m in range(chips)
    ]
    product = None
    for k, wide in enumerate(finished_shards(runs, held)):
        coarse = [pltpu.roll(wide, FINE * i, 1) if i else wide for i in range(COARSE)]
        term = lax.dot_general(
            receivers_ref[k],
            jnp.concatenate(coarse, axis=0).astype(jnp.bfloat16),
            (((1,), (1,)), ((), ())),
            preferred_element_type=jnp.float32,
        )
        product = term if product is None else product + term
    product = product * scale
    for h in range(mixed.shape[0]):
        first, last = h * LANES, min((h + 1) * LANES, COARSE * sources)
        for j in range(FINE):
            mixed[h, pl.ds(j, group, stride=FINE), : last - first] = product[
                j * group : (j + 1) * group, first:last
            ]
        table[h * LANES : (h + 1) * LANES] = mixed[h].T
    lane = lax.broadcasted_iota(jnp.int32, (sources, LANES), 1)
    width = group * LAGS
    tiles = [None] * -(-width // LANES)

    def place(tile, piece, low, high):
        if tiles[tile] is None:
            tiles[tile] = piece
        elif low == 0:
            tiles[tile] = jnp.where(lane < high, piece, tiles[tile])
        else:
            tiles[tile] = jnp.where(lane >= low, piece, tiles[tile])

    for b in range(group):
        column = b * FINE
        for i in range(COARSE):
            piece = table[
                i * sources : (i + 1) * sources,
                column // LANES * LANES : (column // LANES + 1) * LANES,
            ]
            start = b * LAGS + i * FINE
            shift = (start - column) % LANES
            if shift:
                piece = pltpu.roll(piece, shift, 1)
            count = min(FINE, LAGS - i * FINE)
            tile, low = start // LANES, start % LANES
            place(tile, piece, low, LANES)
            if low + count > LANES:
                tiles[tile + 1] = piece
    for tile, value in enumerate(tiles):
        first = tile * LANES
        last = min(first + LANES, width)
        for o in range(offsets):
            rows = value[o * SRC : (o + 1) * SRC, : last - first]
            outs[o][:, first:last] = rows.astype(jnp.bfloat16)


def call(kernel, out_shape, inputs, scratch=(), flops=0):
    single = not isinstance(out_shape, list)
    spec = pl.BlockSpec(memory_space=pltpu.VMEM)
    moved = sum(v.size * v.dtype.itemsize for v in inputs)
    return pl.pallas_call(
        kernel,
        out_shape=out_shape,
        in_specs=[spec] * len(inputs),
        out_specs=spec if single else [spec] * len(out_shape),
        scratch_shapes=list(scratch),
        compiler_params=pltpu.CompilerParams(vmem_limit_bytes=32 * 1024 * 1024),
        cost_estimate=pl.CostEstimate(
            flops=flops, bytes_accessed=moved, transcendentals=0
        ),
    )(*inputs)


def swapped(block, axis, m):
    devices = range(lax.axis_size(axis))
    return lax.ppermute(block, axis, [(k, k ^ m) for k in devices])


def from_blocks(block, low, high):
    count, places = lax.axis_size("chan"), lax.axis_size("tm")
    route = []
    for i in range(count):
        for k in range(places):
            d = low if k % CORES == 0 else high
            route.append((((i - d) % count) * places + k, i * places + k))
    return lax.ppermute(block, ("chan", "tm"), route)


def body(strain_rate):
    channels, length = strain_rate.shape
    shards = lax.axis_size("tm")
    chips = shards // CORES
    reach = lax.axis_size("chan") // 4
    group = channels // shards
    steps = list(range(-reach, 0)) + list(range(1, reach + 1))
    offsets = len(steps)
    sources = offsets * SRC
    scale = 1.0 / math.sqrt(length * shards)
    run = CORES * length
    coded = run + 3 * LANES

    other = swapped(strain_rate, "tm", 1)
    own = call(
        functools.partial(pack_kernel, group, chips),
        jax.ShapeDtypeStruct((chips * group + SRC, length), jnp.float32),
        [strain_rate],
        flops=8 * channels * length,
    )
    *blocks, own_sources = call(
        functools.partial(code_kernel, group),
        [jax.ShapeDtypeStruct((group, coded), jnp.bfloat16)] * chips
        + [jax.ShapeDtypeStruct((SRC, coded), jnp.bfloat16)],
        [own, other],
        flops=8 * (chips * group + SRC) * run * (256 + 2 * LANES),
    )
    arrived = [from_blocks(own_sources, steps[h], steps[reach + h]) for h in range(reach)]
    blocks = [jnp.concatenate([block] + arrived) for block in blocks]
    blocks = blocks[:1] + [swapped(blocks[m], "tm", CORES * m) for m in range(1, chips)]
    own = jnp.concatenate([block[group:] for block in blocks])
    other = swapped(own, "tm", 1)
    receivers = call(
        functools.partial(receiver_kernel, group),
        jax.ShapeDtypeStruct((shards, FINE * group, length + PAD), jnp.bfloat16),
        blocks,
        scratch=[pltpu.VMEM((chips, group, coded), jnp.float32)],
        flops=shards * group * 2 * length * length,
    )
    columns = -(-group * FINE // LANES) * LANES
    heights = -(-COARSE * sources // LANES) * LANES
    results = call(
        functools.partial(correlate_kernel, offsets, scale),
        [jax.ShapeDtypeStruct((SRC, group * LAGS), jnp.bfloat16)] * offsets,
        [receivers, own, other],
        scratch=[
            pltpu.VMEM((chips, sources, coded), jnp.float32),
            pltpu.VMEM((heights // LANES, columns, LANES), jnp.float32),
            pltpu.VMEM((heights, columns), jnp.float32),
        ],
        flops=2 * shards * (length + PAD) * group * FINE * COARSE * sources,
    )
    arrived = [passed_along(r, "chan", -d) for r, d in zip(results, steps)]
    return jnp.stack(arrived, axis=1).astype(jnp.float32)


def solution(mesh):
    placed = (P("chan", "tm"),)
    return jax.shard_map(
        body, mesh=mesh, in_specs=placed, out_specs=P("chan", None, "tm"), check_vma=False
    )
```

```python
import functools
import math

import jax
import jax.numpy as jnp
from jax import lax
from jax.experimental import pallas as pl
from jax.experimental.pallas import tpu as pltpu
from jax.sharding import PartitionSpec as P

SRC = 8
MAXLAG = 25
W2 = 64
LAGS = 51
FINE = 8
COARSE = -(-LAGS // FINE)
LANES = 128
PAD = 128
CORES = 2


def paired(distance):
    return lax.axis_size("chan") % (2 * distance) == 0


def is_lower(i, distance):
    return i // distance % 2 == 0


def both_routes(distance):
    count = lax.axis_size("chan")
    blocks = range(count)
    if not paired(distance):
        up = [(i, (i + distance) % count) for i in blocks]
        return [up, [(j, i) for i, j in up]]
    turns = [distance if is_lower(i, distance) else -distance for i in blocks]
    return [
        [(i, (i + turns[i]) % count) for i in blocks],
        [(i, (i - turns[i]) % count) for i in blocks],
    ]


def back(route):
    return [(j, i) for i, j in route]


def band_matrix(rows, columns, related):
    p = lax.broadcasted_iota(jnp.int32, (rows, columns), 0)
    t = lax.broadcasted_iota(jnp.int32, (rows, columns), 1)
    return jnp.where(related(p, t), 1.0, 0.0).astype(jnp.bfloat16)


def halves(values):
    high = values.astype(jnp.bfloat16).astype(jnp.float32)
    return high, values - high


def banded_sums(pieces, band):
    height = pieces[0].shape[0]
    parts = [halves(piece) for piece in pieces]
    stacked = jnp.concatenate([p[0] for p in parts] + [p[1] for p in parts], axis=0)
    sums = jnp.dot(
        stacked.astype(jnp.bfloat16), band, preferred_element_type=jnp.float32
    )
    count = len(pieces)
    return [
        sums[c * height : (c + 1) * height]
        + sums[(count + c) * height : (count + c + 1) * height]
        for c in range(count)
    ]


def level(window_sums):
    return window_sums / (2 * W2 + 1) + 1e-05


def rows_for_here(ref, group, chips):
    me = lax.axis_index("tm")
    every = ref.shape[0] // SRC
    pieces = []
    for m in range(chips):
        start = pl.multiple_of((me ^ (CORES * m)) * group, group)
        pieces.append(ref[pl.ds(start, group)])
    pieces += [ref[q * every : q * every + 1] for q in range(SRC)]
    return jnp.concatenate(pieces, axis=0)


def pack_kernel(group, chips, x_ref, out_ref):
    out_ref[...] = rows_for_here(x_ref, group, chips)


def code_kernel(group, own_ref, other_ref, *outs):
    blocks, sources_ref = outs[:-1], outs[-1]
    first_core = lax.rem(lax.axis_index("tm"), CORES) == 0
    own = own_ref[...]
    other = rows_for_here(other_ref, group, len(blocks))
    x = jnp.concatenate(
        [jnp.where(first_core, own, other), jnp.where(first_core, other, own)], axis=1
    )
    height, length = x.shape
    border = jnp.zeros((height, LANES), jnp.float32)
    magnitude = jnp.concatenate([border, jnp.abs(x), border], axis=1)
    inner = min(256, length)
    band = band_matrix(
        inner + 2 * LANES, inner, lambda p, t: jnp.abs(p - LANES - t) <= W2
    )
    sums = jnp.concatenate(
        banded_sums(
            [
                magnitude[:, start : start + inner + 2 * LANES]
                for start in range(0, length, inner)
            ],
            band,
        ),
        axis=1,
    )
    normed = x / level(sums)
    left = lax.broadcasted_iota(jnp.int32, (height, LANES), 1) < W2
    tail = length - LANES
    x_high, x_low = halves(jnp.where(left, x[:, :LANES], x[:, tail:]))
    s_high, s_low = halves(jnp.where(left, sums[:, :LANES], sums[:, tail:]))
    coded = jnp.concatenate(
        [
            jnp.where(left, x_high, normed[:, :LANES]),
            normed[:, LANES:tail],
            jnp.where(left, normed[:, tail:], x_high),
            x_low,
            s_high,
            s_low,
        ],
        axis=1,
    ).astype(jnp.bfloat16)
    for m, block in enumerate(blocks):
        block[...] = coded[m * group : (m + 1) * group]
    sources_ref[...] = coded[len(blocks) * group :]


def correlate_kernel(offsets, scale, *refs):
    chips = len(refs) - offsets - 3
    blocks, refs = refs[:chips], refs[chips:]
    outs, (held, mixed, table) = refs[:offsets], refs[offsets:]
    sources = offsets * SRC
    height, width = held.shape[1:]
    group = height - sources
    length = width - 3 * LANES
    chip = lax.div(lax.axis_index("tm"), CORES)
    for m in range(chips):
        held[chip ^ m] = blocks[m][...].astype(jnp.float32)
    left = lax.broadcasted_iota(jnp.int32, (height, LANES), 1) < W2
    tail = length - LANES
    nothing = jnp.zeros((height, LANES), jnp.float32)
    x_ends, s_ends = [], []
    for c in range(chips):
        x_ends.append(
            jnp.where(left, held[c, :, :LANES], held[c, :, tail:length])
            + held[c, :, length : length + LANES]
        )
        s_ends.append(
            held[c, :, length + LANES : length + 2 * LANES]
            + held[c, :, length + 2 * LANES :]
        )

    def meeting(ends):
        return [
            jnp.where(left, after, before)
            for before, after in zip([nothing] + ends, ends + [nothing])
        ]

    def across(p, t):
        at_p, at_t = jnp.where(p < W2, p, p - LANES), jnp.where(t < W2, t, t - LANES)
        return ((p < W2) != (t < W2)) & (jnp.abs(at_p - at_t) <= W2)

    x_meet = meeting(x_ends)
    added = banded_sums(
        [jnp.abs(x) for x in x_meet], band_matrix(LANES, LANES, across)
    )
    ends = [x / level(s + a) for x, s, a in zip(x_meet, meeting(s_ends), added)]
    shard = length // CORES
    padding = jnp.zeros((height, PAD), jnp.float32)
    product = None
    for k in range(chips * CORES):
        c, part = k // CORES, k % CORES
        pieces = [held[c, :, part * shard : (part + 1) * shard], padding]
        if part == 0:
            head = jnp.where(left, ends[c], held[c, :, :LANES])
            pieces = [head, held[c, :, LANES:shard], padding]
        if part == CORES - 1:
            last = jnp.where(left, held[c, :, tail:length], ends[c + 1])
            pieces = [held[c, :, part * shard : tail], last, padding]
        wide = jnp.concatenate(pieces, axis=1)
        receivers, senders = wide[:group], wide[group:]
        fine = [pltpu.roll(receivers, MAXLAG - j, 1) for j in range(FINE)]
        coarse = [
            pltpu.roll(senders, FINE * i, 1) if i else senders for i in range(COARSE)
        ]
        term = lax.dot_general(
            jnp.concatenate(fine, axis=0).astype(jnp.bfloat16),
            jnp.concatenate(coarse, axis=0).astype(jnp.bfloat16),
            (((1,), (1,)), ((), ())),
            preferred_element_type=jnp.float32,
        )
        product = term if product is None else product + term
    product = product * scale
    for h in range(mixed.shape[0]):
        first, last = h * LANES, min((h + 1) * LANES, COARSE * sources)
        for j in range(FINE):
            mixed[h, pl.ds(j, group, stride=FINE), : last - first] = product[
                j * group : (j + 1) * group, first:last
            ]
        table[h * LANES : (h + 1) * LANES] = mixed[h].T
    lane = lax.broadcasted_iota(jnp.int32, (sources, LANES), 1)
    width = group * LAGS
    tiles = [None] * -(-width // LANES)

    def place(tile, piece, low, high):
        if tiles[tile] is None:
            tiles[tile] = piece
        elif low == 0:
            tiles[tile] = jnp.where(lane < high, piece, tiles[tile])
        else:
            tiles[tile] = jnp.where(lane >= low, piece, tiles[tile])

    for b in range(group):
        column = b * FINE
        for i in range(COARSE):
            piece = table[
                i * sources : (i + 1) * sources,
                column // LANES * LANES : (column // LANES + 1) * LANES,
            ]
            start = b * LAGS + i * FINE
            shift = (start - column) % LANES
            if shift:
                piece = pltpu.roll(piece, shift, 1)
            count = min(FINE, LAGS - i * FINE)
            tile, low = start // LANES, start % LANES
            place(tile, piece, low, LANES)
            if low + count > LANES:
                tiles[tile + 1] = piece
    for tile, value in enumerate(tiles):
        first = tile * LANES
        last = min(first + LANES, width)
        for o in range(offsets):
            rows = value[o * SRC : (o + 1) * SRC, : last - first]
            outs[o][:, first:last] = rows.astype(jnp.bfloat16)


def call(kernel, out_shape, inputs, scratch=(), flops=0):
    single = not isinstance(out_shape, list)
    spec = pl.BlockSpec(memory_space=pltpu.VMEM)
    moved = sum(v.size * v.dtype.itemsize for v in inputs)
    return pl.pallas_call(
        kernel,
        out_shape=out_shape,
        in_specs=[spec] * len(inputs),
        out_specs=spec if single else [spec] * len(out_shape),
        scratch_shapes=list(scratch),
        compiler_params=pltpu.CompilerParams(vmem_limit_bytes=32 * 1024 * 1024),
        cost_estimate=pl.CostEstimate(
            flops=flops, bytes_accessed=moved, transcendentals=0
        ),
    )(*inputs)


def swapped(block, axis, m):
    devices = range(lax.axis_size(axis))
    return lax.ppermute(block, axis, [(k, k ^ m) for k in devices])


def body(strain_rate):
    channels, length = strain_rate.shape
    shards = lax.axis_size("tm")
    chips = shards // CORES
    reach = lax.axis_size("chan") // 4
    group = channels // shards
    offsets = 2 * reach
    sources = offsets * SRC
    scale = 1.0 / math.sqrt(length * shards)
    run = CORES * length
    coded = run + 3 * LANES

    other = swapped(strain_rate, "tm", 1)
    own = call(
        functools.partial(pack_kernel, group, chips),
        jax.ShapeDtypeStruct((chips * group + SRC, length), jnp.float32),
        [strain_rate],
        flops=8 * channels * length,
    )
    *blocks, own_sources = call(
        functools.partial(code_kernel, group),
        [jax.ShapeDtypeStruct((group, coded), jnp.bfloat16)] * chips
        + [jax.ShapeDtypeStruct((SRC, coded), jnp.bfloat16)],
        [own, other],
        flops=8 * (chips * group + SRC) * run * (256 + 2 * LANES),
    )
    routes = [route for d in range(1, reach + 1) for route in both_routes(d)]
    arrived = [lax.ppermute(own_sources, "chan", route) for route in routes]
    blocks = [jnp.concatenate([block] + arrived) for block in blocks]
    blocks = blocks[:1] + [swapped(blocks[m], "tm", CORES * m) for m in range(1, chips)]
    columns = -(-group * FINE // LANES) * LANES
    heights = -(-COARSE * sources // LANES) * LANES
    results = call(
        functools.partial(correlate_kernel, offsets, scale),
        [jax.ShapeDtypeStruct((SRC, group * LAGS), jnp.bfloat16)] * offsets,
        blocks,
        scratch=[
            pltpu.VMEM((chips, group + sources, coded), jnp.float32),
            pltpu.VMEM((heights // LANES, columns, LANES), jnp.float32),
            pltpu.VMEM((heights, columns), jnp.float32),
        ],
        flops=2 * shards * (length + PAD) * group * FINE * COARSE * sources,
    )
    arrived = [
        lax.ppermute(result, "chan", back(route))
        for result, route in zip(results, routes)
    ]
    above, below = [], []
    for d in range(1, reach + 1):
        first, second = arrived[2 * d - 2 : 2 * d]
        if paired(d):
            lower = is_lower(lax.axis_index("chan"), d)
            first, second = (
                jnp.where(lower, first, second),
                jnp.where(lower, second, first),
            )
        above.append(first)
        below.append(second)
    return jnp.stack(below[::-1] + above, axis=1).astype(jnp.float32)


def solution(mesh):
    placed = (P("chan", "tm"),)
    return jax.shard_map(
        body, mesh=mesh, in_specs=placed, out_specs=P("chan", None, "tm"), check_vma=False
    )
```

```python
import functools
import math

import jax
import jax.numpy as jnp
from jax import lax
from jax.experimental import pallas as pl
from jax.experimental.pallas import tpu as pltpu
from jax.sharding import PartitionSpec as P

SRC = 8
MAXLAG = 25
W2 = 64
LAGS = 51
FINE = 8
COARSE = -(-LAGS // FINE)
LANES = 128
PAD = 128
CORES = 2


def passed_along(block, axis, distance):
    devices = range(lax.axis_size(axis))
    route = [((i - distance) % len(devices), i) for i in devices]
    return lax.ppermute(block, axis, route)


def band_matrix(rows, columns, related):
    p = lax.broadcasted_iota(jnp.int32, (rows, columns), 0)
    t = lax.broadcasted_iota(jnp.int32, (rows, columns), 1)
    return jnp.where(related(p, t), 1.0, 0.0).astype(jnp.bfloat16)


def halves(values):
    high = values.astype(jnp.bfloat16).astype(jnp.float32)
    return high, values - high


def banded_sums(pieces, band):
    height = pieces[0].shape[0]
    parts = [halves(piece) for piece in pieces]
    stacked = jnp.concatenate([p[0] for p in parts] + [p[1] for p in parts], axis=0)
    sums = jnp.dot(
        stacked.astype(jnp.bfloat16), band, preferred_element_type=jnp.float32
    )
    count = len(pieces)
    return [
        sums[c * height : (c + 1) * height]
        + sums[(count + c) * height : (count + c + 1) * height]
        for c in range(count)
    ]


def level(window_sums):
    return window_sums / (2 * W2 + 1) + 1e-05


def rows_for_here(ref, group, chips):
    me = lax.axis_index("tm")
    every = ref.shape[0] // SRC
    pieces = []
    for m in range(chips):
        start = pl.multiple_of((me ^ (CORES * m)) * group, group)
        pieces.append(ref[pl.ds(start, group)])
    pieces += [ref[q * every : q * every + 1] for q in range(SRC)]
    return jnp.concatenate(pieces, axis=0)


def pack_kernel(group, chips, x_ref, out_ref):
    out_ref[...] = rows_for_here(x_ref, group, chips)


def code_kernel(group, own_ref, other_ref, *outs):
    blocks, sources_ref = outs[:-1], outs[-1]
    first_core = lax.rem(lax.axis_index("tm"), CORES) == 0
    own = own_ref[...]
    other = rows_for_here(other_ref, group, len(blocks))
    x = jnp.concatenate(
        [jnp.where(first_core, own, other), jnp.where(first_core, other, own)], axis=1
    )
    height, length = x.shape
    border = jnp.zeros((height, LANES), jnp.float32)
    magnitude = jnp.concatenate([border, jnp.abs(x), border], axis=1)
    inner = min(256, length)
    band = band_matrix(
        inner + 2 * LANES, inner, lambda p, t: jnp.abs(p - LANES - t) <= W2
    )
    sums = jnp.concatenate(
        banded_sums(
            [
                magnitude[:, start : start + inner + 2 * LANES]
                for start in range(0, length, inner)
            ],
            band,
        ),
        axis=1,
    )
    levels = level(sums)
    normed = x / levels
    left = lax.broadcasted_iota(jnp.int32, (height, LANES), 1) < W2
    tail = length - LANES
    ends = jnp.where(left, normed[:, :LANES], normed[:, tail:])
    end_levels = jnp.where(left, levels[:, :LANES], levels[:, tail:])
    coded = jnp.concatenate([normed, halves(ends)[1], end_levels], axis=1)
    coded = coded.astype(jnp.bfloat16)
    for m, block in enumerate(blocks):
        block[...] = coded[m * group : (m + 1) * group]
    sources_ref[...] = coded[len(blocks) * group :]


def finished_shards(runs, held):
    chips, height, width = held.shape
    length = width - 2 * LANES
    chip = lax.div(lax.axis_index("tm"), CORES)
    for m in range(chips):
        held[chip ^ m] = runs[m]
    left = lax.broadcasted_iota(jnp.int32, (height, LANES), 1) < W2
    tail = length - LANES
    end_values, end_levels = [], []
    for c in range(chips):
        end_values.append(
            jnp.where(left, held[c, :, :LANES], held[c, :, tail:length])
            + held[c, :, length : length + LANES]
        )
        end_levels.append(held[c, :, length + LANES :])

    def meeting(ends, outside):
        outside = [jnp.full((height, LANES), outside, jnp.float32)]
        return [
            jnp.where(left, after, before)
            for before, after in zip(outside + ends, ends + outside)
        ]

    def across(p, t):
        at_p, at_t = jnp.where(p < W2, p, p - LANES), jnp.where(t < W2, t, t - LANES)
        return ((p < W2) != (t < W2)) & (jnp.abs(at_p - at_t) <= W2)

    values, levels = meeting(end_values, 0.0), meeting(end_levels, 1.0)
    added = banded_sums(
        [jnp.abs(v) * l for v, l in zip(values, levels)],
        band_matrix(LANES, LANES, across),
    )
    ends = [
        v * l / (l + a / (2 * W2 + 1)) for v, l, a in zip(values, levels, added)
    ]
    shard = length // CORES
    padding = jnp.zeros((height, PAD), jnp.float32)
    for k in range(chips * CORES):
        c, part = k // CORES, k % CORES
        pieces = [held[c, :, part * shard : (part + 1) * shard], padding]
        if part == 0:
            head = jnp.where(left, ends[c], held[c, :, :LANES])
            pieces = [head, held[c, :, LANES:shard], padding]
        if part == CORES - 1:
            last = jnp.where(left, held[c, :, tail:length], ends[c + 1])
            pieces = [held[c, :, part * shard : tail], last, padding]
        yield jnp.concatenate(pieces, axis=1)


def receiver_kernel(group, *refs):
    *blocks, out_ref, held = refs
    runs = [ref[...].astype(jnp.float32)[:group] for ref in blocks]
    for k, wide in enumerate(finished_shards(runs, held)):
        fine = [pltpu.roll(wide, MAXLAG - j, 1) for j in range(FINE)]
        out_ref[k] = jnp.concatenate(fine, axis=0).astype(jnp.bfloat16)


def correlate_kernel(offsets, scale, receivers_ref, own_ref, other_ref, *refs):
    outs, (held, mixed, table) = refs[:offsets], refs[offsets:]
    chips, sources = held.shape[:2]
    group = receivers_ref.shape[1] // FINE
    first_core = lax.rem(lax.axis_index("tm"), CORES) == 0
    own, other = [ref[...].astype(jnp.float32) for ref in (own_ref, other_ref)]
    high, low = jnp.where(first_core, own, other), jnp.where(first_core, other, own)
    half = sources // CORES
    runs = [
        jnp.concatenate(
            [low[m * half : (m + 1) * half], high[m * half : (m + 1) * half]], axis=0
        )
        for m in range(chips)
    ]
    product = None
    for k, wide in enumerate(finished_shards(runs, held)):
        coarse = [pltpu.roll(wide, FINE * i, 1) if i else wide for i in range(COARSE)]
        term = lax.dot_general(
            receivers_ref[k],
            jnp.concatenate(coarse, axis=0).astype(jnp.bfloat16),
            (((1,), (1,)), ((), ())),
            preferred_element_type=jnp.float32,
        )
        product = term if product is None else product + term
    product = product * scale
    for h in range(mixed.shape[0]):
        first, last = h * LANES, min((h + 1) * LANES, COARSE * sources)
        for j in range(FINE):
            mixed[h, pl.ds(j, group, stride=FINE), : last - first] = product[
                j * group : (j + 1) * group, first:last
            ]
        table[h * LANES : (h + 1) * LANES] = mixed[h].T
    lane = lax.broadcasted_iota(jnp.int32, (sources, LANES), 1)
    width = group * LAGS
    tiles = [None] * -(-width // LANES)

    def place(tile, piece, low, high):
        if tiles[tile] is None:
            tiles[tile] = piece
        elif low == 0:
            tiles[tile] = jnp.where(lane < high, piece, tiles[tile])
        else:
            tiles[tile] = jnp.where(lane >= low, piece, tiles[tile])

    for b in range(group):
        column = b * FINE
        for i in range(COARSE):
            piece = table[
                i * sources : (i + 1) * sources,
                column // LANES * LANES : (column // LANES + 1) * LANES,
            ]
            start = b * LAGS + i * FINE
            shift = (start - column) % LANES
            if shift:
                piece = pltpu.roll(piece, shift, 1)
            count = min(FINE, LAGS - i * FINE)
            tile, low = start // LANES, start % LANES
            place(tile, piece, low, LANES)
            if low + count > LANES:
                tiles[tile + 1] = piece
    for tile, value in enumerate(tiles):
        first = tile * LANES
        last = min(first + LANES, width)
        for o in range(offsets):
            rows = value[o * SRC : (o + 1) * SRC, : last - first]
            outs[o][:, first:last] = rows.astype(jnp.bfloat16)


def stack_kernel(*refs):
    out_ref = refs[-1]
    for o, ref in enumerate(refs[:-1]):
        out_ref[:, o, :] = ref[...].astype(jnp.float32)


def call(kernel, out_shape, inputs, scratch=(), flops=0):
    single = not isinstance(out_shape, list)
    spec = pl.BlockSpec(memory_space=pltpu.VMEM)
    moved = sum(v.size * v.dtype.itemsize for v in inputs)
    return pl.pallas_call(
        kernel,
        out_shape=out_shape,
        in_specs=[spec] * len(inputs),
        out_specs=spec if single else [spec] * len(out_shape),
        scratch_shapes=list(scratch),
        compiler_params=pltpu.CompilerParams(vmem_limit_bytes=32 * 1024 * 1024),
        cost_estimate=pl.CostEstimate(
            flops=flops, bytes_accessed=moved, transcendentals=0
        ),
    )(*inputs)


def swapped(block, axis, m):
    devices = range(lax.axis_size(axis))
    return lax.ppermute(block, axis, [(k, k ^ m) for k in devices])


def from_blocks(block, first, second):
    count, places = lax.axis_size("chan"), lax.axis_size("tm")
    route = []
    for i in range(count):
        for k in range(places):
            d = first if k % CORES == 0 else second
            route.append((((i - d) % count) * places + k, i * places + k))
    return lax.ppermute(block, ("chan", "tm"), route)


def body(strain_rate):
    channels, length = strain_rate.shape
    shards = lax.axis_size("tm")
    chips = shards // CORES
    reach = lax.axis_size("chan") // 4
    group = channels // shards
    steps = list(range(-reach, 0)) + list(range(1, reach + 1))
    offsets = len(steps)
    sources = offsets * SRC
    scale = 1.0 / math.sqrt(length * shards)
    run = CORES * length
    coded = run + 2 * LANES

    other = swapped(strain_rate, "tm", 1)
    own = call(
        functools.partial(pack_kernel, group, chips),
        jax.ShapeDtypeStruct((chips * group + SRC, length), jnp.float32),
        [strain_rate],
        flops=8 * channels * length,
    )
    *blocks, own_sources = call(
        functools.partial(code_kernel, group),
        [jax.ShapeDtypeStruct((group, coded), jnp.bfloat16)] * chips
        + [jax.ShapeDtypeStruct((SRC, coded), jnp.bfloat16)],
        [own, other],
        flops=8 * (chips * group + SRC) * run * (256 + 2 * LANES),
    )
    arrived = [from_blocks(own_sources, steps[reach + h], steps[h]) for h in range(reach)]
    blocks = [jnp.concatenate([block] + arrived) for block in blocks]
    blocks = blocks[:1] + [swapped(blocks[m], "tm", CORES * m) for m in range(1, chips)]
    own = jnp.concatenate([block[group:] for block in blocks])
    other = swapped(own, "tm", 1)
    receivers = call(
        functools.partial(receiver_kernel, group),
        jax.ShapeDtypeStruct((shards, FINE * group, length + PAD), jnp.bfloat16),
        blocks,
        scratch=[pltpu.VMEM((chips, group, coded), jnp.float32)],
        flops=shards * group * 2 * length * length,
    )
    columns = -(-group * FINE // LANES) * LANES
    heights = -(-COARSE * sources // LANES) * LANES
    results = call(
        functools.partial(correlate_kernel, offsets, scale),
        [jax.ShapeDtypeStruct((SRC, group * LAGS), jnp.bfloat16)] * offsets,
        [receivers, own, other],
        scratch=[
            pltpu.VMEM((chips, sources, coded), jnp.float32),
            pltpu.VMEM((heights // LANES, columns, LANES), jnp.float32),
            pltpu.VMEM((heights, columns), jnp.float32),
        ],
        flops=2 * shards * (length + PAD) * group * FINE * COARSE * sources,
    )
    arrived = [passed_along(r, "chan", -d) for r, d in zip(results, steps)]
    return call(
        stack_kernel,
        jax.ShapeDtypeStruct((SRC, offsets, group * LAGS), jnp.float32),
        arrived,
    )


def solution(mesh):
    placed = (P("chan", "tm"),)
    return jax.shard_map(
        body, mesh=mesh, in_specs=placed, out_specs=P("chan", None, "tm"), check_vma=False
    )
```

```python
import functools
import math

import jax
import jax.numpy as jnp
from jax import lax
from jax.experimental import pallas as pl
from jax.experimental.pallas import tpu as pltpu
from jax.sharding import PartitionSpec as P

SRC = 8
MAXLAG = 25
W2 = 64
LAGS = 51
FINE = 8
COARSE = -(-LAGS // FINE)
LANES = 128
PAD = 128
CORES = 2


def passed_along(block, axis, distance):
    devices = range(lax.axis_size(axis))
    route = [((i - distance) % len(devices), i) for i in devices]
    return lax.ppermute(block, axis, route)


def band_matrix(rows, columns, related):
    p = lax.broadcasted_iota(jnp.int32, (rows, columns), 0)
    t = lax.broadcasted_iota(jnp.int32, (rows, columns), 1)
    return jnp.where(related(p, t), 1.0, 0.0).astype(jnp.bfloat16)


def halves(values):
    high = values.astype(jnp.bfloat16).astype(jnp.float32)
    return high, values - high


def banded_sums(pieces, band):
    height = pieces[0].shape[0]
    parts = [halves(piece) for piece in pieces]
    stacked = jnp.concatenate([p[0] for p in parts] + [p[1] for p in parts], axis=0)
    sums = jnp.dot(
        stacked.astype(jnp.bfloat16), band, preferred_element_type=jnp.float32
    )
    count = len(pieces)
    return [
        sums[c * height : (c + 1) * height]
        + sums[(count + c) * height : (count + c + 1) * height]
        for c in range(count)
    ]


def level(window_sums):
    return window_sums / (2 * W2 + 1) + 1e-05


def rows_for_here(ref, group, chips):
    me = lax.axis_index("tm")
    every = ref.shape[0] // SRC
    pieces = []
    for m in range(chips):
        start = pl.multiple_of((me ^ (CORES * m)) * group, group)
        pieces.append(ref[pl.ds(start, group)])
    pieces += [ref[q * every : q * every + 1] for q in range(SRC)]
    return jnp.concatenate(pieces, axis=0)


def pack_kernel(group, chips, x_ref, out_ref):
    out_ref[...] = rows_for_here(x_ref, group, chips)


def coded_rows(own, other):
    first_core = lax.rem(lax.axis_index("tm"), CORES) == 0
    x = jnp.concatenate(
        [jnp.where(first_core, own, other), jnp.where(first_core, other, own)], axis=1
    )
    height, length = x.shape
    border = jnp.zeros((height, LANES), jnp.float32)
    magnitude = jnp.concatenate([border, jnp.abs(x), border], axis=1)
    inner = min(256, length)
    band = band_matrix(
        inner + 2 * LANES, inner, lambda p, t: jnp.abs(p - LANES - t) <= W2
    )
    sums = jnp.concatenate(
        banded_sums(
            [
                magnitude[:, start : start + inner + 2 * LANES]
                for start in range(0, length, inner)
            ],
            band,
        ),
        axis=1,
    )
    levels = level(sums)
    normed = x / levels
    left = lax.broadcasted_iota(jnp.int32, (height, LANES), 1) < W2
    tail = length - LANES
    ends = jnp.where(left, normed[:, :LANES], normed[:, tail:])
    end_levels = jnp.where(left, levels[:, :LANES], levels[:, tail:])
    coded = jnp.concatenate([normed, halves(ends)[1], end_levels], axis=1)
    return coded.astype(jnp.bfloat16)


def code_sources_kernel(group, chips, own_ref, other_ref, out_ref):
    first = chips * group
    other = rows_for_here(other_ref, group, chips)
    out_ref[...] = coded_rows(own_ref[first:], other[first:])


def code_receivers_kernel(group, chips, own_ref, other_ref, out_ref):
    last = chips * group
    other = rows_for_here(other_ref, group, chips)
    out_ref[...] = coded_rows(own_ref[:last], other[:last])


def join_kernel(offsets, receivers_ref, *refs):
    given, blocks = refs[:offsets], refs[offsets:]
    group = receivers_ref.shape[0] // len(blocks)
    sources = [ref[...].astype(jnp.float32) for ref in given]
    receivers = receivers_ref[...].astype(jnp.float32)
    for m, block in enumerate(blocks):
        rows = [receivers[m * group : (m + 1) * group]] + sources
        block[...] = jnp.concatenate(rows, axis=0).astype(jnp.bfloat16)


def finished_shards(runs, held):
    chips, height, width = held.shape
    length = width - 2 * LANES
    chip = lax.div(lax.axis_index("tm"), CORES)
    for m in range(chips):
        held[chip ^ m] = runs[m]
    left = lax.broadcasted_iota(jnp.int32, (height, LANES), 1) < W2
    tail = length - LANES
    end_values, end_levels = [], []
    for c in range(chips):
        end_values.append(
            jnp.where(left, held[c, :, :LANES], held[c, :, tail:length])
            + held[c, :, length : length + LANES]
        )
        end_levels.append(held[c, :, length + LANES :])

    def meeting(ends, outside):
        outside = [jnp.full((height, LANES), outside, jnp.float32)]
        return [
            jnp.where(left, after, before)
            for before, after in zip(outside + ends, ends + outside)
        ]

    def across(p, t):
        at_p, at_t = jnp.where(p < W2, p, p - LANES), jnp.where(t < W2, t, t - LANES)
        return ((p < W2) != (t < W2)) & (jnp.abs(at_p - at_t) <= W2)

    values, levels = meeting(end_values, 0.0), meeting(end_levels, 1.0)
    added = banded_sums(
        [jnp.abs(v) * l for v, l in zip(values, levels)],
        band_matrix(LANES, LANES, across),
    )
    ends = [
        v * l / (l + a / (2 * W2 + 1)) for v, l, a in zip(values, levels, added)
    ]
    shard = length // CORES
    padding = jnp.zeros((height, PAD), jnp.float32)
    for k in range(chips * CORES):
        c, part = k // CORES, k % CORES
        pieces = [held[c, :, part * shard : (part + 1) * shard], padding]
        if part == 0:
            head = jnp.where(left, ends[c], held[c, :, :LANES])
            pieces = [head, held[c, :, LANES:shard], padding]
        if part == CORES - 1:
            last = jnp.where(left, held[c, :, tail:length], ends[c + 1])
            pieces = [held[c, :, part * shard : tail], last, padding]
        yield jnp.concatenate(pieces, axis=1)


def correlate_kernel(offsets, scale, *refs):
    chips = len(refs) - offsets - 3
    blocks, refs = refs[:chips], refs[chips:]
    outs, (held, mixed, table) = refs[:offsets], refs[offsets:]
    sources = offsets * SRC
    group = held.shape[1] - sources
    runs = [ref[...].astype(jnp.float32) for ref in blocks[:1] + blocks[:0:-1]]
    product = None
    for wide in finished_shards(runs, held):
        receivers, senders = wide[:group], wide[group:]
        fine = [pltpu.roll(receivers, MAXLAG - j, 1) for j in range(FINE)]
        coarse = [
            pltpu.roll(senders, FINE * i, 1) if i else senders for i in range(COARSE)
        ]
        term = lax.dot_general(
            jnp.concatenate(fine, axis=0).astype(jnp.bfloat16),
            jnp.concatenate(coarse, axis=0).astype(jnp.bfloat16),
            (((1,), (1,)), ((), ())),
            preferred_element_type=jnp.float32,
        )
        product = term if product is None else product + term
    product = product * scale
    for h in range(mixed.shape[0]):
        first, last = h * LANES, min((h + 1) * LANES, COARSE * sources)
        for j in range(FINE):
            mixed[h, pl.ds(j, group, stride=FINE), : last - first] = product[
                j * group : (j + 1) * group, first:last
            ]
        table[h * LANES : (h + 1) * LANES] = mixed[h].T
    lane = lax.broadcasted_iota(jnp.int32, (sources, LANES), 1)
    width = group * LAGS
    tiles = [None] * -(-width // LANES)

    def place(tile, piece, low, high):
        if tiles[tile] is None:
            tiles[tile] = piece
        elif low == 0:
            tiles[tile] = jnp.where(lane < high, piece, tiles[tile])
        else:
            tiles[tile] = jnp.where(lane >= low, piece, tiles[tile])

    for b in range(group):
        column = b * FINE
        for i in range(COARSE):
            piece = table[
                i * sources : (i + 1) * sources,
                column // LANES * LANES : (column // LANES + 1) * LANES,
            ]
            start = b * LAGS + i * FINE
            shift = (start - column) % LANES
            if shift:
                piece = pltpu.roll(piece, shift, 1)
            count = min(FINE, LAGS - i * FINE)
            tile, low = start // LANES, start % LANES
            place(tile, piece, low, LANES)
            if low + count > LANES:
                tiles[tile + 1] = piece
    for tile, value in enumerate(tiles):
        first = tile * LANES
        last = min(first + LANES, width)
        for o in range(offsets):
            rows = value[o * SRC : (o + 1) * SRC, : last - first]
            outs[o][:, first:last] = rows.astype(jnp.bfloat16)


def stack_kernel(*refs):
    out_ref = refs[-1]
    for o, ref in enumerate(refs[:-1]):
        out_ref[:, o, :] = ref[...].astype(jnp.float32)


def call(kernel, out_shape, inputs, scratch=(), flops=0):
    single = not isinstance(out_shape, list)
    spec = pl.BlockSpec(memory_space=pltpu.VMEM)
    moved = sum(v.size * v.dtype.itemsize for v in inputs)
    return pl.pallas_call(
        kernel,
        out_shape=out_shape,
        in_specs=[spec] * len(inputs),
        out_specs=spec if single else [spec] * len(out_shape),
        scratch_shapes=list(scratch),
        compiler_params=pltpu.CompilerParams(vmem_limit_bytes=32 * 1024 * 1024),
        cost_estimate=pl.CostEstimate(
            flops=flops, bytes_accessed=moved, transcendentals=0
        ),
    )(*inputs)


def swapped(block, axis, m):
    devices = range(lax.axis_size(axis))
    return lax.ppermute(block, axis, [(k, k ^ m) for k in devices])


def body(strain_rate):
    channels, length = strain_rate.shape
    shards = lax.axis_size("tm")
    chips = shards // CORES
    reach = lax.axis_size("chan") // 4
    group = channels // shards
    steps = list(range(-reach, 0)) + list(range(1, reach + 1))
    offsets = len(steps)
    sources = offsets * SRC
    scale = 1.0 / math.sqrt(length * shards)
    run = CORES * length
    coded = run + 2 * LANES

    other = swapped(strain_rate, "tm", 1)
    own = call(
        functools.partial(pack_kernel, group, chips),
        jax.ShapeDtypeStruct((chips * group + SRC, length), jnp.float32),
        [strain_rate],
        flops=8 * channels * length,
    )
    own_sources = call(
        functools.partial(code_sources_kernel, group, chips),
        jax.ShapeDtypeStruct((SRC, coded), jnp.bfloat16),
        [own, other],
    )
    arrived = [passed_along(own_sources, "chan", d) for d in steps]
    own_receivers = call(
        functools.partial(code_receivers_kernel, group, chips),
        jax.ShapeDtypeStruct((chips * group, coded), jnp.bfloat16),
        [own, other],
        flops=8 * chips * group * run * (256 + 2 * LANES),
    )
    blocks = call(
        functools.partial(join_kernel, offsets),
        [jax.ShapeDtypeStruct((group + sources, coded), jnp.bfloat16)] * chips,
        [own_receivers] + arrived,
    )
    blocks = list(blocks[:1]) + [
        swapped(blocks[m], "tm", CORES * m) for m in range(chips - 1, 0, -1)
    ]
    columns = -(-group * FINE // LANES) * LANES
    heights = -(-COARSE * sources // LANES) * LANES
    results = call(
        functools.partial(correlate_kernel, offsets, scale),
        [jax.ShapeDtypeStruct((SRC, group * LAGS), jnp.bfloat16)] * offsets,
        blocks,
        scratch=[
            pltpu.VMEM((chips, group + sources, coded), jnp.float32),
            pltpu.VMEM((heights // LANES, columns, LANES), jnp.float32),
            pltpu.VMEM((heights, columns), jnp.float32),
        ],
        flops=2 * shards * (length + PAD) * group * FINE * COARSE * sources,
    )
    arrived = [passed_along(r, "chan", -d) for r, d in zip(results, steps)]
    return call(
        stack_kernel,
        jax.ShapeDtypeStruct((SRC, offsets, group * LAGS), jnp.float32),
        arrived,
    )


def solution(mesh):
    placed = (P("chan", "tm"),)
    return jax.shard_map(
        body, mesh=mesh, in_specs=placed, out_specs=P("chan", None, "tm"), check_vma=False
    )
```

```python
import functools
import math

import jax
import jax.numpy as jnp
from jax import lax
from jax.experimental import pallas as pl
from jax.experimental.pallas import tpu as pltpu
from jax.sharding import PartitionSpec as P

SRC = 8
MAXLAG = 25
W2 = 64
LAGS = 51
FINE = 8
COARSE = -(-LAGS // FINE)
LANES = 128
PAD = 128
CORES = 2


def passed_along(block, axis, distance):
    devices = range(lax.axis_size(axis))
    route = [((i - distance) % len(devices), i) for i in devices]
    return lax.ppermute(block, axis, route)


def band_matrix(rows, columns, related):
    p = lax.broadcasted_iota(jnp.int32, (rows, columns), 0)
    t = lax.broadcasted_iota(jnp.int32, (rows, columns), 1)
    return jnp.where(related(p, t), 1.0, 0.0).astype(jnp.bfloat16)


def halves(values):
    high = values.astype(jnp.bfloat16).astype(jnp.float32)
    return high, values - high


def banded_sums(pieces, band):
    height = pieces[0].shape[0]
    parts = [halves(piece) for piece in pieces]
    stacked = jnp.concatenate([p[0] for p in parts] + [p[1] for p in parts], axis=0)
    sums = jnp.dot(
        stacked.astype(jnp.bfloat16), band, preferred_element_type=jnp.float32
    )
    count = len(pieces)
    return [
        sums[c * height : (c + 1) * height]
        + sums[(count + c) * height : (count + c + 1) * height]
        for c in range(count)
    ]


def level(window_sums):
    return window_sums / (2 * W2 + 1) + 1e-05


def rows_for_here(ref, group, chips):
    me = lax.axis_index("tm")
    every = ref.shape[0] // SRC
    pieces = []
    for m in range(chips):
        start = pl.multiple_of((me ^ (CORES * m)) * group, group)
        pieces.append(ref[pl.ds(start, group)])
    pieces += [ref[q * every : q * every + 1] for q in range(SRC)]
    return jnp.concatenate(pieces, axis=0)


def pack_kernel(group, chips, x_ref, out_ref):
    out_ref[...] = rows_for_here(x_ref, group, chips)


def coded_rows(own, other):
    first_core = lax.rem(lax.axis_index("tm"), CORES) == 0
    x = jnp.concatenate(
        [jnp.where(first_core, own, other), jnp.where(first_core, other, own)], axis=1
    )
    height, length = x.shape
    border = jnp.zeros((height, LANES), jnp.float32)
    magnitude = jnp.concatenate([border, jnp.abs(x), border], axis=1)
    inner = min(256, length)
    band = band_matrix(
        inner + 2 * LANES, inner, lambda p, t: jnp.abs(p - LANES - t) <= W2
    )
    sums = jnp.concatenate(
        banded_sums(
            [
                magnitude[:, start : start + inner + 2 * LANES]
                for start in range(0, length, inner)
            ],
            band,
        ),
        axis=1,
    )
    levels = level(sums)
    normed = x / levels
    left = lax.broadcasted_iota(jnp.int32, (height, LANES), 1) < W2
    tail = length - LANES
    ends = jnp.where(left, normed[:, :LANES], normed[:, tail:])
    end_levels = jnp.where(left, levels[:, :LANES], levels[:, tail:])
    coded = jnp.concatenate([normed, halves(ends)[1], end_levels], axis=1)
    return coded.astype(jnp.bfloat16)


def code_sources_kernel(group, chips, own_ref, other_ref, out_ref):
    first = chips * group
    other = rows_for_here(other_ref, group, chips)
    out_ref[...] = coded_rows(own_ref[first:], other[first:])


def code_receivers_kernel(group, chips, own_ref, other_ref, out_ref):
    last = chips * group
    other = rows_for_here(other_ref, group, chips)
    out_ref[...] = coded_rows(own_ref[:last], other[:last])


def join_kernel(offsets, receivers_ref, *refs):
    given, blocks = refs[:offsets], refs[offsets:]
    group = receivers_ref.shape[0] // len(blocks)
    sources = [ref[...].astype(jnp.float32) for ref in given]
    receivers = receivers_ref[...].astype(jnp.float32)
    for m, block in enumerate(blocks):
        rows = [receivers[m * group : (m + 1) * group]] + sources[::-1]
        block[...] = jnp.concatenate(rows, axis=0).astype(jnp.bfloat16)


def finished_shards(runs, held):
    chips, height, width = held.shape
    length = width - 2 * LANES
    chip = lax.div(lax.axis_index("tm"), CORES)
    for m in range(chips):
        held[chip ^ m] = runs[m]
    left = lax.broadcasted_iota(jnp.int32, (height, LANES), 1) < W2
    tail = length - LANES
    end_values, end_levels = [], []
    for c in range(chips):
        end_values.append(
            jnp.where(left, held[c, :, :LANES], held[c, :, tail:length])
            + held[c, :, length : length + LANES]
        )
        end_levels.append(held[c, :, length + LANES :])

    def meeting(ends, outside):
        outside = [jnp.full((height, LANES), outside, jnp.float32)]
        return [
            jnp.where(left, after, before)
            for before, after in zip(outside + ends, ends + outside)
        ]

    def across(p, t):
        at_p, at_t = jnp.where(p < W2, p, p - LANES), jnp.where(t < W2, t, t - LANES)
        return ((p < W2) != (t < W2)) & (jnp.abs(at_p - at_t) <= W2)

    values, levels = meeting(end_values, 0.0), meeting(end_levels, 1.0)
    added = banded_sums(
        [jnp.abs(v) * l for v, l in zip(values, levels)],
        band_matrix(LANES, LANES, across),
    )
    ends = [
        v * l / (l + a / (2 * W2 + 1)) for v, l, a in zip(values, levels, added)
    ]
    shard = length // CORES
    padding = jnp.zeros((height, PAD), jnp.float32)
    for k in range(chips * CORES):
        c, part = k // CORES, k % CORES
        pieces = [held[c, :, part * shard : (part + 1) * shard], padding]
        if part == 0:
            head = jnp.where(left, ends[c], held[c, :, :LANES])
            pieces = [head, held[c, :, LANES:shard], padding]
        if part == CORES - 1:
            last = jnp.where(left, held[c, :, tail:length], ends[c + 1])
            pieces = [held[c, :, part * shard : tail], last, padding]
        yield jnp.concatenate(pieces, axis=1)


def receiver_kernel(group, *refs):
    *blocks, out_ref, held = refs
    runs = [ref[...].astype(jnp.float32)[:group] for ref in blocks[:1] + blocks[:0:-1]]
    for k, wide in enumerate(finished_shards(runs, held)):
        fine = [pltpu.roll(wide, MAXLAG - j, 1) for j in range(FINE)]
        out_ref[k] = jnp.concatenate(fine, axis=0).astype(jnp.bfloat16)


def correlate_kernel(offsets, scale, receivers_ref, own_ref, other_ref, *refs):
    outs, (held, mixed, table) = refs[:offsets], refs[offsets:]
    chips, sources = held.shape[:2]
    group = receivers_ref.shape[1] // FINE
    first_core = lax.rem(lax.axis_index("tm"), CORES) == 0
    own, other = [ref[...].astype(jnp.float32) for ref in (own_ref, other_ref)]
    gathered = jnp.where(first_core, other, own)
    runs = [gathered[m * sources : (m + 1) * sources] for m in range(chips)]
    product = None
    for k, wide in enumerate(finished_shards(runs, held)):
        coarse = [pltpu.roll(wide, FINE * i, 1) if i else wide for i in range(COARSE)]
        term = lax.dot_general(
            receivers_ref[k],
            jnp.concatenate(coarse, axis=0).astype(jnp.bfloat16),
            (((1,), (1,)), ((), ())),
            preferred_element_type=jnp.float32,
        )
        product = term if product is None else product + term
    product = product * scale
    for h in range(mixed.shape[0]):
        first, last = h * LANES, min((h + 1) * LANES, COARSE * sources)
        for j in range(FINE):
            mixed[h, pl.ds(j, group, stride=FINE), : last - first] = product[
                j * group : (j + 1) * group, first:last
            ]
        table[h * LANES : (h + 1) * LANES] = mixed[h].T
    lane = lax.broadcasted_iota(jnp.int32, (sources, LANES), 1)
    width = group * LAGS
    tiles = [None] * -(-width // LANES)

    def place(tile, piece, low, high):
        if tiles[tile] is None:
            tiles[tile] = piece
        elif low == 0:
            tiles[tile] = jnp.where(lane < high, piece, tiles[tile])
        else:
            tiles[tile] = jnp.where(lane >= low, piece, tiles[tile])

    for b in range(group):
        column = b * FINE
        for i in range(COARSE):
            piece = table[
                i * sources : (i + 1) * sources,
                column // LANES * LANES : (column // LANES + 1) * LANES,
            ]
            start = b * LAGS + i * FINE
            shift = (start - column) % LANES
            if shift:
                piece = pltpu.roll(piece, shift, 1)
            count = min(FINE, LAGS - i * FINE)
            tile, low = start // LANES, start % LANES
            place(tile, piece, low, LANES)
            if low + count > LANES:
                tiles[tile + 1] = piece
    for tile, value in enumerate(tiles):
        first = tile * LANES
        last = min(first + LANES, width)
        for o in range(offsets):
            rows = value[o * SRC : (o + 1) * SRC, : last - first]
            outs[o][:, first:last] = rows.astype(jnp.bfloat16)


def stack_kernel(*refs):
    out_ref = refs[-1]
    for o, ref in enumerate(refs[:-1]):
        out_ref[:, o, :] = ref[...].astype(jnp.float32)


def call(kernel, out_shape, inputs, scratch=(), flops=0):
    single = not isinstance(out_shape, list)
    spec = pl.BlockSpec(memory_space=pltpu.VMEM)
    moved = sum(v.size * v.dtype.itemsize for v in inputs)
    return pl.pallas_call(
        kernel,
        out_shape=out_shape,
        in_specs=[spec] * len(inputs),
        out_specs=spec if single else [spec] * len(out_shape),
        scratch_shapes=list(scratch),
        compiler_params=pltpu.CompilerParams(vmem_limit_bytes=32 * 1024 * 1024),
        cost_estimate=pl.CostEstimate(
            flops=flops, bytes_accessed=moved, transcendentals=0
        ),
    )(*inputs)


def swapped(block, axis, m):
    devices = range(lax.axis_size(axis))
    return lax.ppermute(block, axis, [(k, k ^ m) for k in devices])


def passed_to_last_core(block, distance):
    count, places = lax.axis_size("chan"), lax.axis_size("tm")
    route = [
        ((i - distance) % count * places + k, i * places + k)
        for i in range(count)
        for k in range(CORES - 1, places, CORES)
    ]
    return lax.ppermute(block, ("chan", "tm"), route)


def body(strain_rate):
    channels, length = strain_rate.shape
    shards = lax.axis_size("tm")
    chips = shards // CORES
    reach = lax.axis_size("chan") // 4
    group = channels // shards
    steps = list(range(-reach, 0)) + list(range(1, reach + 1))
    offsets = len(steps)
    sources = offsets * SRC
    scale = 1.0 / math.sqrt(length * shards)
    run = CORES * length
    coded = run + 2 * LANES

    other = swapped(strain_rate, "tm", 1)
    own = call(
        functools.partial(pack_kernel, group, chips),
        jax.ShapeDtypeStruct((chips * group + SRC, length), jnp.float32),
        [strain_rate],
        flops=8 * channels * length,
    )
    own_sources = call(
        functools.partial(code_sources_kernel, group, chips),
        jax.ShapeDtypeStruct((SRC, coded), jnp.bfloat16),
        [own, other],
    )
    arrived = [passed_to_last_core(own_sources, d) for d in steps]
    own_receivers = call(
        functools.partial(code_receivers_kernel, group, chips),
        jax.ShapeDtypeStruct((chips * group, coded), jnp.bfloat16),
        [own, other],
        flops=8 * chips * group * run * (256 + 2 * LANES),
    )
    blocks = call(
        functools.partial(join_kernel, offsets),
        [jax.ShapeDtypeStruct((group + sources, coded), jnp.bfloat16)] * chips,
        [own_receivers] + arrived[::-1],
    )
    blocks = list(blocks[:1]) + [
        swapped(blocks[m], "tm", CORES * m) for m in range(chips - 1, 0, -1)
    ]
    gathered = jnp.concatenate([b[group:] for b in blocks[:1] + blocks[:0:-1]])
    handed = lax.ppermute(
        gathered, "tm", [(k, k - 1) for k in range(CORES - 1, shards, CORES)]
    )
    receivers = call(
        functools.partial(receiver_kernel, group),
        jax.ShapeDtypeStruct((shards, FINE * group, length + PAD), jnp.bfloat16),
        blocks,
        scratch=[pltpu.VMEM((chips, group, coded), jnp.float32)],
        flops=shards * group * 2 * length * length,
    )
    columns = -(-group * FINE // LANES) * LANES
    heights = -(-COARSE * sources // LANES) * LANES
    results = call(
        functools.partial(correlate_kernel, offsets, scale),
        [jax.ShapeDtypeStruct((SRC, group * LAGS), jnp.bfloat16)] * offsets,
        [receivers, gathered, handed],
        scratch=[
            pltpu.VMEM((chips, sources, coded), jnp.float32),
            pltpu.VMEM((heights // LANES, columns, LANES), jnp.float32),
            pltpu.VMEM((heights, columns), jnp.float32),
        ],
        flops=2 * shards * (length + PAD) * group * FINE * COARSE * sources,
    )
    arrived = [passed_along(r, "chan", -d) for r, d in zip(results, steps)]
    return call(
        stack_kernel,
        jax.ShapeDtypeStruct((SRC, offsets, group * LAGS), jnp.float32),
        arrived,
    )


def solution(mesh):
    placed = (P("chan", "tm"),)
    return jax.shard_map(
        body, mesh=mesh, in_specs=placed, out_specs=P("chan", None, "tm"), check_vma=False
    )
```

```python
import functools
import math

import jax
import jax.numpy as jnp
from jax import lax
from jax.experimental import pallas as pl
from jax.experimental.pallas import tpu as pltpu
from jax.sharding import PartitionSpec as P

SRC = 8
MAXLAG = 25
W2 = 64
LAGS = 51
FINE = 8
COARSE = -(-LAGS // FINE)
LANES = 128
PAD = 128
CORES = 2


def passed_along(block, axis, distance):
    devices = range(lax.axis_size(axis))
    route = [((i - distance) % len(devices), i) for i in devices]
    return lax.ppermute(block, axis, route)


def band_matrix(rows, columns, related):
    p = lax.broadcasted_iota(jnp.int32, (rows, columns), 0)
    t = lax.broadcasted_iota(jnp.int32, (rows, columns), 1)
    return jnp.where(related(p, t), 1.0, 0.0).astype(jnp.bfloat16)


def halves(values):
    high = values.astype(jnp.bfloat16).astype(jnp.float32)
    return high, values - high


def banded_sums(pieces, band):
    height = pieces[0].shape[0]
    parts = [halves(piece) for piece in pieces]
    stacked = jnp.concatenate([p[0] for p in parts] + [p[1] for p in parts], axis=0)
    sums = jnp.dot(
        stacked.astype(jnp.bfloat16), band, preferred_element_type=jnp.float32
    )
    count = len(pieces)
    return [
        sums[c * height : (c + 1) * height]
        + sums[(count + c) * height : (count + c + 1) * height]
        for c in range(count)
    ]


def level(window_sums):
    return window_sums / (2 * W2 + 1) + 1e-05


def rows_for_here(ref, group, chips):
    me = lax.axis_index("tm")
    every = ref.shape[0] // SRC
    pieces = []
    for m in range(chips):
        start = pl.multiple_of((me ^ (CORES * m)) * group, group)
        pieces.append(ref[pl.ds(start, group)])
    pieces += [ref[q * every : q * every + 1] for q in range(SRC)]
    return jnp.concatenate(pieces, axis=0)


def pack_kernel(group, chips, x_ref, out_ref):
    out_ref[...] = rows_for_here(x_ref, group, chips)


def coded_rows(own, other):
    first_core = lax.rem(lax.axis_index("tm"), CORES) == 0
    x = jnp.concatenate(
        [jnp.where(first_core, own, other), jnp.where(first_core, other, own)], axis=1
    )
    height, length = x.shape
    border = jnp.zeros((height, LANES), jnp.float32)
    magnitude = jnp.concatenate([border, jnp.abs(x), border], axis=1)
    inner = min(256, length)
    band = band_matrix(
        inner + 2 * LANES, inner, lambda p, t: jnp.abs(p - LANES - t) <= W2
    )
    sums = jnp.concatenate(
        banded_sums(
            [
                magnitude[:, start : start + inner + 2 * LANES]
                for start in range(0, length, inner)
            ],
            band,
        ),
        axis=1,
    )
    levels = level(sums)
    normed = x / levels
    left = lax.broadcasted_iota(jnp.int32, (height, LANES), 1) < W2
    tail = length - LANES
    ends = jnp.where(left, normed[:, :LANES], normed[:, tail:])
    end_levels = jnp.where(left, levels[:, :LANES], levels[:, tail:])
    coded = jnp.concatenate([normed, halves(ends)[1], end_levels], axis=1)
    return coded.astype(jnp.bfloat16)


def code_sources_kernel(group, chips, own_ref, other_ref, out_ref):
    first = chips * group
    other = rows_for_here(other_ref, group, chips)
    out_ref[...] = coded_rows(own_ref[first:], other[first:])


def code_receivers_kernel(group, chips, own_ref, other_ref, out_ref):
    last = chips * group
    other = rows_for_here(other_ref, group, chips)
    out_ref[...] = coded_rows(own_ref[:last], other[:last])


def join_kernel(offsets, receivers_ref, *refs):
    given, blocks = refs[:offsets], refs[offsets:]
    group = receivers_ref.shape[0] // len(blocks)
    sources = [ref[...].astype(jnp.float32) for ref in given]
    receivers = receivers_ref[...].astype(jnp.float32)
    for m, block in enumerate(blocks):
        rows = [receivers[m * group : (m + 1) * group]] + sources[::-1]
        block[...] = jnp.concatenate(rows, axis=0).astype(jnp.bfloat16)


def finished_shards(runs, held):
    chips, height, width = held.shape
    length = width - 2 * LANES
    chip = lax.div(lax.axis_index("tm"), CORES)
    for m in range(chips):
        held[chip ^ m] = runs[m]
    left = lax.broadcasted_iota(jnp.int32, (height, LANES), 1) < W2
    tail = length - LANES
    end_values, end_levels = [], []
    for c in range(chips):
        end_values.append(
            jnp.where(left, held[c, :, :LANES], held[c, :, tail:length])
            + held[c, :, length : length + LANES]
        )
        end_levels.append(held[c, :, length + LANES :])

    def meeting(ends, outside):
        outside = [jnp.full((height, LANES), outside, jnp.float32)]
        return [
            jnp.where(left, after, before)
            for before, after in zip(outside + ends, ends + outside)
        ]

    def across(p, t):
        at_p, at_t = jnp.where(p < W2, p, p - LANES), jnp.where(t < W2, t, t - LANES)
        return ((p < W2) != (t < W2)) & (jnp.abs(at_p - at_t) <= W2)

    values, levels = meeting(end_values, 0.0), meeting(end_levels, 1.0)
    added = banded_sums(
        [jnp.abs(v) * l for v, l in zip(values, levels)],
        band_matrix(LANES, LANES, across),
    )
    ends = [
        v * l / (l + a / (2 * W2 + 1)) for v, l, a in zip(values, levels, added)
    ]
    shard = length // CORES
    padding = jnp.zeros((height, PAD), jnp.float32)
    for k in range(chips * CORES):
        c, part = k // CORES, k % CORES
        pieces = [held[c, :, part * shard : (part + 1) * shard], padding]
        if part == 0:
            head = jnp.where(left, ends[c], held[c, :, :LANES])
            pieces = [head, held[c, :, LANES:shard], padding]
        if part == CORES - 1:
            last = jnp.where(left, held[c, :, tail:length], ends[c + 1])
            pieces = [held[c, :, part * shard : tail], last, padding]
        yield jnp.concatenate(pieces, axis=1)


def receiver_kernel(group, *refs):
    *blocks, out_ref, held = refs
    runs = [ref[...].astype(jnp.float32)[:group] for ref in blocks[:1] + blocks[:0:-1]]
    for k, wide in enumerate(finished_shards(runs, held)):
        fine = [pltpu.roll(wide, MAXLAG - j, 1) for j in range(FINE)]
        out_ref[k] = jnp.concatenate(fine, axis=0).astype(jnp.bfloat16)


def correlate_kernel(offsets, scale, receivers_ref, own_ref, other_ref, *refs):
    outs, (held, mixed, table) = refs[:offsets], refs[offsets:]
    chips, sources = held.shape[:2]
    group = receivers_ref.shape[1] // FINE
    first_core = lax.rem(lax.axis_index("tm"), CORES) == 0
    own, other = [ref[...].astype(jnp.float32) for ref in (own_ref, other_ref)]
    gathered = jnp.where(first_core, other, own)
    runs = [gathered[m * sources : (m + 1) * sources] for m in range(chips)]
    product = None
    for k, wide in enumerate(finished_shards(runs, held)):
        coarse = [pltpu.roll(wide, FINE * i, 1) if i else wide for i in range(COARSE)]
        term = lax.dot_general(
            receivers_ref[k],
            jnp.concatenate(coarse, axis=0).astype(jnp.bfloat16),
            (((1,), (1,)), ((), ())),
            preferred_element_type=jnp.float32,
        )
        product = term if product is None else product + term
    product = product * scale
    for h in range(mixed.shape[0]):
        first, last = h * LANES, min((h + 1) * LANES, COARSE * sources)
        for j in range(FINE):
            mixed[h, pl.ds(j, group, stride=FINE), : last - first] = product[
                j * group : (j + 1) * group, first:last
            ]
        table[h * LANES : (h + 1) * LANES] = mixed[h].T
    lane = lax.broadcasted_iota(jnp.int32, (sources, LANES), 1)
    width = group * LAGS
    tiles = [None] * -(-width // LANES)

    def place(tile, piece, low, high):
        if tiles[tile] is None:
            tiles[tile] = piece
        elif low == 0:
            tiles[tile] = jnp.where(lane < high, piece, tiles[tile])
        else:
            tiles[tile] = jnp.where(lane >= low, piece, tiles[tile])

    for b in range(group):
        column = b * FINE
        for i in range(COARSE):
            piece = table[
                i * sources : (i + 1) * sources,
                column // LANES * LANES : (column // LANES + 1) * LANES,
            ]
            start = b * LAGS + i * FINE
            shift = (start - column) % LANES
            if shift:
                piece = pltpu.roll(piece, shift, 1)
            count = min(FINE, LAGS - i * FINE)
            tile, low = start // LANES, start % LANES
            place(tile, piece, low, LANES)
            if low + count > LANES:
                tiles[tile + 1] = piece
    for tile, value in enumerate(tiles):
        first = tile * LANES
        last = min(first + LANES, width)
        for o in range(offsets):
            rows = value[o * SRC : (o + 1) * SRC, : last - first]
            outs[o][:, first:last] = rows.astype(jnp.bfloat16)


def stack_kernel(*refs):
    out_ref = refs[-1]
    for o, ref in enumerate(refs[:-1]):
        out_ref[:, o, :] = ref[...].astype(jnp.float32)


def call(kernel, out_shape, inputs, scratch=(), flops=0):
    single = not isinstance(out_shape, list)
    spec = pl.BlockSpec(memory_space=pltpu.VMEM)
    moved = sum(v.size * v.dtype.itemsize for v in inputs)
    return pl.pallas_call(
        kernel,
        out_shape=out_shape,
        in_specs=[spec] * len(inputs),
        out_specs=spec if single else [spec] * len(out_shape),
        scratch_shapes=list(scratch),
        compiler_params=pltpu.CompilerParams(vmem_limit_bytes=32 * 1024 * 1024),
        cost_estimate=pl.CostEstimate(
            flops=flops, bytes_accessed=moved, transcendentals=0
        ),
    )(*inputs)


def swapped(block, axis, m):
    devices = range(lax.axis_size(axis))
    return lax.ppermute(block, axis, [(k, k ^ m) for k in devices])


def passed_to_last_core(block, distance):
    count, places = lax.axis_size("chan"), lax.axis_size("tm")
    route = []
    for i in range(count):
        for k in range(places):
            origin = (i - distance) % count if k % CORES == CORES - 1 else i
            route.append((origin * places + k, i * places + k))
    return lax.ppermute(block, ("chan", "tm"), route)


def body(strain_rate):
    channels, length = strain_rate.shape
    shards = lax.axis_size("tm")
    chips = shards // CORES
    reach = lax.axis_size("chan") // 4
    group = channels // shards
    steps = list(range(-reach, 0)) + list(range(1, reach + 1))
    offsets = len(steps)
    sources = offsets * SRC
    scale = 1.0 / math.sqrt(length * shards)
    run = CORES * length
    coded = run + 2 * LANES

    other = swapped(strain_rate, "tm", 1)
    own = call(
        functools.partial(pack_kernel, group, chips),
        jax.ShapeDtypeStruct((chips * group + SRC, length), jnp.float32),
        [strain_rate],
        flops=8 * channels * length,
    )
    own_sources = call(
        functools.partial(code_sources_kernel, group, chips),
        jax.ShapeDtypeStruct((SRC, coded), jnp.bfloat16),
        [own, other],
    )
    arrived = [passed_to_last_core(own_sources, d) for d in steps]
    own_receivers = call(
        functools.partial(code_receivers_kernel, group, chips),
        jax.ShapeDtypeStruct((chips * group, coded), jnp.bfloat16),
        [own, other],
        flops=8 * chips * group * run * (256 + 2 * LANES),
    )
    blocks = call(
        functools.partial(join_kernel, offsets),
        [jax.ShapeDtypeStruct((group + sources, coded), jnp.bfloat16)] * chips,
        [own_receivers] + arrived[::-1],
    )
    blocks = list(blocks[:1]) + [
        swapped(blocks[m], "tm", CORES * m) for m in range(chips - 1, 0, -1)
    ]
    gathered = jnp.concatenate([b[group:] for b in blocks[:1] + blocks[:0:-1]])
    handed = lax.ppermute(
        gathered, "tm", [(k, k - 1) for k in range(CORES - 1, shards, CORES)]
    )
    receivers = call(
        functools.partial(receiver_kernel, group),
        jax.ShapeDtypeStruct((shards, FINE * group, length + PAD), jnp.bfloat16),
        blocks,
        scratch=[pltpu.VMEM((chips, group, coded), jnp.float32)],
        flops=shards * group * 2 * length * length,
    )
    columns = -(-group * FINE // LANES) * LANES
    heights = -(-COARSE * sources // LANES) * LANES
    results = call(
        functools.partial(correlate_kernel, offsets, scale),
        [jax.ShapeDtypeStruct((SRC, group * LAGS), jnp.bfloat16)] * offsets,
        [receivers, gathered, handed],
        scratch=[
            pltpu.VMEM((chips, sources, coded), jnp.float32),
            pltpu.VMEM((heights // LANES, columns, LANES), jnp.float32),
            pltpu.VMEM((heights, columns), jnp.float32),
        ],
        flops=2 * shards * (length + PAD) * group * FINE * COARSE * sources,
    )
    arrived = [passed_along(r, "chan", -d) for r, d in zip(results, steps)]
    return call(
        stack_kernel,
        jax.ShapeDtypeStruct((SRC, offsets, group * LAGS), jnp.float32),
        arrived,
    )


def solution(mesh):
    placed = (P("chan", "tm"),)
    return jax.shard_map(
        body, mesh=mesh, in_specs=placed, out_specs=P("chan", None, "tm"), check_vma=False
    )
```

```python
import functools
import math

import jax
import jax.numpy as jnp
from jax import lax
from jax.experimental import pallas as pl
from jax.experimental.pallas import tpu as pltpu
from jax.sharding import PartitionSpec as P

SRC = 8
MAXLAG = 25
W2 = 64
LAGS = 51
FINE = 8
COARSE = -(-LAGS // FINE)
LANES = 128
PAD = 128
CORES = 2


def passed_along(block, axis, distance):
    devices = range(lax.axis_size(axis))
    route = [((i - distance) % len(devices), i) for i in devices]
    return lax.ppermute(block, axis, route)


def band_matrix(rows, columns, related):
    p = lax.broadcasted_iota(jnp.int32, (rows, columns), 0)
    t = lax.broadcasted_iota(jnp.int32, (rows, columns), 1)
    return jnp.where(related(p, t), 1.0, 0.0).astype(jnp.bfloat16)


def halves(values):
    high = values.astype(jnp.bfloat16).astype(jnp.float32)
    return high, values - high


def banded_sums(pieces, band):
    height = pieces[0].shape[0]
    parts = [halves(piece) for piece in pieces]
    stacked = jnp.concatenate([p[0] for p in parts] + [p[1] for p in parts], axis=0)
    sums = jnp.dot(
        stacked.astype(jnp.bfloat16), band, preferred_element_type=jnp.float32
    )
    count = len(pieces)
    return [
        sums[c * height : (c + 1) * height]
        + sums[(count + c) * height : (count + c + 1) * height]
        for c in range(count)
    ]


def level(window_sums):
    return window_sums / (2 * W2 + 1) + 1e-05


def rows_for_here(ref, group, chips):
    me = lax.axis_index("tm")
    every = ref.shape[0] // SRC
    pieces = []
    for m in range(chips):
        start = pl.multiple_of((me ^ (CORES * m)) * group, group)
        pieces.append(ref[pl.ds(start, group)])
    pieces += [ref[q * every : q * every + 1] for q in range(SRC)]
    return jnp.concatenate(pieces, axis=0)


def pack_kernel(group, chips, x_ref, out_ref):
    out_ref[...] = rows_for_here(x_ref, group, chips)


def coded_rows(own, other):
    first_core = lax.rem(lax.axis_index("tm"), CORES) == 0
    x = jnp.concatenate(
        [jnp.where(first_core, own, other), jnp.where(first_core, other, own)], axis=1
    )
    height, length = x.shape
    border = jnp.zeros((height, LANES), jnp.float32)
    magnitude = jnp.concatenate([border, jnp.abs(x), border], axis=1)
    inner = min(256, length)
    band = band_matrix(
        inner + 2 * LANES, inner, lambda p, t: jnp.abs(p - LANES - t) <= W2
    )
    sums = jnp.concatenate(
        banded_sums(
            [
                magnitude[:, start : start + inner + 2 * LANES]
                for start in range(0, length, inner)
            ],
            band,
        ),
        axis=1,
    )
    levels = level(sums)
    normed = x / levels
    left = lax.broadcasted_iota(jnp.int32, (height, LANES), 1) < W2
    tail = length - LANES
    ends = jnp.where(left, normed[:, :LANES], normed[:, tail:])
    end_levels = jnp.where(left, levels[:, :LANES], levels[:, tail:])
    coded = jnp.concatenate([normed, halves(ends)[1], end_levels], axis=1)
    return coded.astype(jnp.bfloat16)


def code_sources_kernel(group, chips, own_ref, other_ref, out_ref):
    first = chips * group
    other = rows_for_here(other_ref, group, chips)
    out_ref[...] = coded_rows(own_ref[first:], other[first:])


def code_receivers_kernel(group, chips, own_ref, other_ref, out_ref):
    last = chips * group
    other = rows_for_here(other_ref, group, chips)
    out_ref[...] = coded_rows(own_ref[:last], other[:last])


def join_kernel(offsets, receivers_ref, *refs):
    given, blocks = refs[:offsets], refs[offsets:]
    group = receivers_ref.shape[0] // len(blocks)
    sources = [ref[...].astype(jnp.float32) for ref in given]
    receivers = receivers_ref[...].astype(jnp.float32)
    for m, block in enumerate(blocks):
        rows = [receivers[m * group : (m + 1) * group]] + sources
        block[...] = jnp.concatenate(rows, axis=0).astype(jnp.bfloat16)


def finished_shards(runs, held):
    chips, height, width = held.shape
    length = width - 2 * LANES
    chip = lax.div(lax.axis_index("tm"), CORES)
    for m in range(chips):
        held[chip ^ m] = runs[m]
    left = lax.broadcasted_iota(jnp.int32, (height, LANES), 1) < W2
    tail = length - LANES
    end_values, end_levels = [], []

    def lanes(c, first):
        return held[c, :, first : first + LANES].astype(jnp.float32)

    for c in range(chips):
        high = jnp.where(left, lanes(c, 0), lanes(c, tail))
        end_values.append(high + lanes(c, length))
        end_levels.append(lanes(c, length + LANES))

    def meeting(ends, outside):
        outside = [jnp.full((height, LANES), outside, jnp.float32)]
        return [
            jnp.where(left, after, before)
            for before, after in zip(outside + ends, ends + outside)
        ]

    def across(p, t):
        at_p, at_t = jnp.where(p < W2, p, p - LANES), jnp.where(t < W2, t, t - LANES)
        return ((p < W2) != (t < W2)) & (jnp.abs(at_p - at_t) <= W2)

    values, levels = meeting(end_values, 0.0), meeting(end_levels, 1.0)
    added = banded_sums(
        [jnp.abs(v) * l for v, l in zip(values, levels)],
        band_matrix(LANES, LANES, across),
    )
    ends = [
        v * l / (l + a / (2 * W2 + 1)) for v, l, a in zip(values, levels, added)
    ]
    shard = length // CORES
    padding = jnp.zeros((height, PAD), held.dtype)
    for k in range(chips * CORES):
        c, part = k // CORES, k % CORES
        pieces = [held[c, :, part * shard : (part + 1) * shard], padding]
        if part == 0:
            head = jnp.where(left, ends[c], lanes(c, 0)).astype(held.dtype)
            pieces = [head, held[c, :, LANES:shard], padding]
        if part == CORES - 1:
            last = jnp.where(left, lanes(c, tail), ends[c + 1]).astype(held.dtype)
            pieces = [held[c, :, part * shard : tail], last, padding]
        yield jnp.concatenate(pieces, axis=1)


def correlate_kernel(offsets, scale, *refs):
    chips = len(refs) - offsets - 3
    blocks, refs = refs[:chips], refs[chips:]
    outs, (held, mixed, table) = refs[:offsets], refs[offsets:]
    sources = offsets * SRC
    group = held.shape[1] - sources
    runs = [ref[...].astype(held.dtype) for ref in blocks[:1] + blocks[:0:-1]]
    product = None
    for wide in finished_shards(runs, held):
        receivers, senders = wide[:group], wide[group:]
        fine = [pltpu.roll(receivers, MAXLAG - j, 1) for j in range(FINE)]
        coarse = [
            pltpu.roll(senders, FINE * i, 1) if i else senders for i in range(COARSE)
        ]
        term = lax.dot_general(
            jnp.concatenate(fine, axis=0).astype(jnp.bfloat16),
            jnp.concatenate(coarse, axis=0).astype(jnp.bfloat16),
            (((1,), (1,)), ((), ())),
            preferred_element_type=jnp.float32,
        )
        product = term if product is None else product + term
    product = product * scale
    for h in range(mixed.shape[0]):
        first, last = h * LANES, min((h + 1) * LANES, COARSE * sources)
        for j in range(FINE):
            mixed[h, pl.ds(j, group, stride=FINE), : last - first] = product[
                j * group : (j + 1) * group, first:last
            ]
        table[h * LANES : (h + 1) * LANES] = mixed[h].T.astype(table.dtype)
    lane = lax.broadcasted_iota(jnp.int32, (sources, LANES), 1)
    width = group * LAGS
    tiles = [None] * -(-width // LANES)

    def place(tile, piece, low, high):
        if tiles[tile] is None:
            tiles[tile] = piece
        elif low == 0:
            tiles[tile] = jnp.where(lane < high, piece, tiles[tile])
        else:
            tiles[tile] = jnp.where(lane >= low, piece, tiles[tile])

    for b in range(group):
        column = b * FINE
        for i in range(COARSE):
            piece = table[
                i * sources : (i + 1) * sources,
                column // LANES * LANES : (column // LANES + 1) * LANES,
            ]
            start = b * LAGS + i * FINE
            shift = (start - column) % LANES
            if shift:
                piece = pltpu.roll(piece, shift, 1)
            count = min(FINE, LAGS - i * FINE)
            tile, low = start // LANES, start % LANES
            place(tile, piece, low, LANES)
            if low + count > LANES:
                tiles[tile + 1] = piece
    for tile, value in enumerate(tiles):
        first = tile * LANES
        last = min(first + LANES, width)
        for o in range(offsets):
            rows = value.astype(jnp.float32)[o * SRC : (o + 1) * SRC, : last - first]
            outs[o][:, first:last] = rows.astype(jnp.bfloat16)


def stack_kernel(*refs):
    out_ref = refs[-1]
    for o, ref in enumerate(refs[:-1]):
        out_ref[:, o, :] = ref[...].astype(jnp.float32)


def call(kernel, out_shape, inputs, scratch=(), flops=0):
    single = not isinstance(out_shape, list)
    spec = pl.BlockSpec(memory_space=pltpu.VMEM)
    moved = sum(v.size * v.dtype.itemsize for v in inputs)
    return pl.pallas_call(
        kernel,
        out_shape=out_shape,
        in_specs=[spec] * len(inputs),
        out_specs=spec if single else [spec] * len(out_shape),
        scratch_shapes=list(scratch),
        compiler_params=pltpu.CompilerParams(vmem_limit_bytes=32 * 1024 * 1024),
        cost_estimate=pl.CostEstimate(
            flops=flops, bytes_accessed=moved, transcendentals=0
        ),
    )(*inputs)


def swapped(block, axis, m):
    devices = range(lax.axis_size(axis))
    return lax.ppermute(block, axis, [(k, k ^ m) for k in devices])


def body(strain_rate):
    channels, length = strain_rate.shape
    shards = lax.axis_size("tm")
    chips = shards // CORES
    reach = lax.axis_size("chan") // 4
    group = channels // shards
    steps = list(range(-reach, 0)) + list(range(1, reach + 1))
    offsets = len(steps)
    sources = offsets * SRC
    scale = 1.0 / math.sqrt(length * shards)
    run = CORES * length
    coded = run + 2 * LANES

    other = swapped(strain_rate, "tm", 1)
    own = call(
        functools.partial(pack_kernel, group, chips),
        jax.ShapeDtypeStruct((chips * group + SRC, length), jnp.float32),
        [strain_rate],
        flops=8 * channels * length,
    )
    own_sources = call(
        functools.partial(code_sources_kernel, group, chips),
        jax.ShapeDtypeStruct((SRC, coded), jnp.bfloat16),
        [own, other],
    )
    arrived = [passed_along(own_sources, "chan", d) for d in steps]
    own_receivers = call(
        functools.partial(code_receivers_kernel, group, chips),
        jax.ShapeDtypeStruct((chips * group, coded), jnp.bfloat16),
        [own, other],
        flops=8 * chips * group * run * (256 + 2 * LANES),
    )
    blocks = call(
        functools.partial(join_kernel, offsets),
        [jax.ShapeDtypeStruct((group + sources, coded), jnp.bfloat16)] * chips,
        [own_receivers] + arrived,
    )
    blocks = list(blocks[:1]) + [
        swapped(blocks[m], "tm", CORES * m) for m in range(chips - 1, 0, -1)
    ]
    columns = -(-group * FINE // LANES) * LANES
    heights = -(-COARSE * sources // LANES) * LANES
    kind = jnp.float32 if group % 16 or sources % 16 else jnp.bfloat16
    results = call(
        functools.partial(correlate_kernel, offsets, scale),
        [jax.ShapeDtypeStruct((SRC, group * LAGS), jnp.bfloat16)] * offsets,
        blocks,
        scratch=[
            pltpu.VMEM((chips, group + sources, coded), kind),
            pltpu.VMEM((heights // LANES, columns, LANES), jnp.float32),
            pltpu.VMEM((heights, columns), kind),
        ],
        flops=2 * shards * (length + PAD) * group * FINE * COARSE * sources,
    )
    arrived = [passed_along(r, "chan", -d) for r, d in zip(results, steps)]
    return call(
        stack_kernel,
        jax.ShapeDtypeStruct((SRC, offsets, group * LAGS), jnp.float32),
        arrived,
    )


def solution(mesh):
    placed = (P("chan", "tm"),)
    return jax.shard_map(
        body, mesh=mesh, in_specs=placed, out_specs=P("chan", None, "tm"), check_vma=False
    )
```

```python
import functools
import math

import jax
import jax.numpy as jnp
from jax import lax
from jax.experimental import pallas as pl
from jax.experimental.pallas import tpu as pltpu
from jax.sharding import PartitionSpec as P

SRC = 8
MAXLAG = 25
W2 = 64
LAGS = 51
FINE = 8
COARSE = -(-LAGS // FINE)
LANES = 128
PAD = 128
CORES = 2


def passed_along(block, axis, distance):
    devices = range(lax.axis_size(axis))
    route = [((i - distance) % len(devices), i) for i in devices]
    return lax.ppermute(block, axis, route)


def band_matrix(rows, columns, related):
    p = lax.broadcasted_iota(jnp.int32, (rows, columns), 0)
    t = lax.broadcasted_iota(jnp.int32, (rows, columns), 1)
    return jnp.where(related(p, t), 1.0, 0.0).astype(jnp.bfloat16)


def halves(values):
    high = values.astype(jnp.bfloat16).astype(jnp.float32)
    return high, values - high


def banded_sums(pieces, band):
    height = pieces[0].shape[0]
    parts = [halves(piece) for piece in pieces]
    stacked = jnp.concatenate([p[0] for p in parts] + [p[1] for p in parts], axis=0)
    sums = jnp.dot(
        stacked.astype(jnp.bfloat16), band, preferred_element_type=jnp.float32
    )
    count = len(pieces)
    return [
        sums[c * height : (c + 1) * height]
        + sums[(count + c) * height : (count + c + 1) * height]
        for c in range(count)
    ]


def level(window_sums):
    return window_sums / (2 * W2 + 1) + 1e-05


def rows_for_here(ref, group, chips):
    core = lax.rem(lax.axis_index("tm"), CORES)
    every = ref.shape[0] // SRC
    pieces = []
    for chip in range(chips):
        start = pl.multiple_of((chip * CORES + core) * group, group)
        pieces.append(ref[pl.ds(start, group)])
    pieces += [ref[q * every : q * every + 1] for q in range(SRC)]
    return jnp.concatenate(pieces, axis=0)


def pack_kernel(group, chips, x_ref, out_ref):
    out_ref[...] = rows_for_here(x_ref, group, chips)


def coded_rows(own, other):
    first_core = lax.rem(lax.axis_index("tm"), CORES) == 0
    x = jnp.concatenate(
        [jnp.where(first_core, own, other), jnp.where(first_core, other, own)], axis=1
    )
    height, length = x.shape
    border = jnp.zeros((height, LANES), jnp.float32)
    magnitude = jnp.concatenate([border, jnp.abs(x), border], axis=1)
    inner = min(256, length)
    band = band_matrix(
        inner + 2 * LANES, inner, lambda p, t: jnp.abs(p - LANES - t) <= W2
    )
    sums = jnp.concatenate(
        banded_sums(
            [
                magnitude[:, start : start + inner + 2 * LANES]
                for start in range(0, length, inner)
            ],
            band,
        ),
        axis=1,
    )
    levels = level(sums)
    normed = x / levels
    left = lax.broadcasted_iota(jnp.int32, (height, LANES), 1) < W2
    tail = length - LANES
    ends = jnp.where(left, normed[:, :LANES], normed[:, tail:])
    end_levels = jnp.where(left, levels[:, :LANES], levels[:, tail:])
    coded = jnp.concatenate([normed, halves(ends)[1], end_levels], axis=1)
    return coded.astype(jnp.bfloat16)


def code_sources_kernel(group, chips, own_ref, other_ref, out_ref):
    first = chips * group
    other = rows_for_here(other_ref, group, chips)
    out_ref[...] = coded_rows(own_ref[first:], other[first:])


def code_receivers_kernel(group, chips, own_ref, other_ref, out_ref):
    last = chips * group
    other = rows_for_here(other_ref, group, chips)
    out_ref[...] = coded_rows(own_ref[:last], other[:last])


def join_kernel(receivers_ref, *refs):
    given, out_ref = refs[:-1], refs[-1]
    chips = out_ref.shape[0]
    group = receivers_ref.shape[0] // chips
    sources = [ref[...].astype(jnp.float32) for ref in given]
    receivers = receivers_ref[...].astype(jnp.float32)
    for chip in range(chips):
        rows = [receivers[chip * group : (chip + 1) * group]] + sources
        out_ref[chip] = jnp.concatenate(rows, axis=0).astype(jnp.bfloat16)


def finished_shards(held):
    chips, height, width = held.shape
    length = width - 2 * LANES
    left = lax.broadcasted_iota(jnp.int32, (height, LANES), 1) < W2
    tail = length - LANES
    end_values, end_levels = [], []

    def lanes(c, first):
        return held[c, :, first : first + LANES].astype(jnp.float32)

    for c in range(chips):
        high = jnp.where(left, lanes(c, 0), lanes(c, tail))
        end_values.append(high + lanes(c, length))
        end_levels.append(lanes(c, length + LANES))

    def meeting(ends, outside):
        outside = [jnp.full((height, LANES), outside, jnp.float32)]
        return [
            jnp.where(left, after, before)
            for before, after in zip(outside + ends, ends + outside)
        ]

    def across(p, t):
        at_p, at_t = jnp.where(p < W2, p, p - LANES), jnp.where(t < W2, t, t - LANES)
        return ((p < W2) != (t < W2)) & (jnp.abs(at_p - at_t) <= W2)

    values, levels = meeting(end_values, 0.0), meeting(end_levels, 1.0)
    added = banded_sums(
        [jnp.abs(v) * l for v, l in zip(values, levels)],
        band_matrix(LANES, LANES, across),
    )
    ends = [
        v * l / (l + a / (2 * W2 + 1)) for v, l, a in zip(values, levels, added)
    ]
    shard = length // CORES
    padding = jnp.zeros((height, PAD), held.dtype)
    for k in range(chips * CORES):
        c, part = k // CORES, k % CORES
        pieces = [held[c, :, part * shard : (part + 1) * shard], padding]
        if part == 0:
            head = jnp.where(left, ends[c], lanes(c, 0)).astype(held.dtype)
            pieces = [head, held[c, :, LANES:shard], padding]
        if part == CORES - 1:
            last = jnp.where(left, lanes(c, tail), ends[c + 1]).astype(held.dtype)
            pieces = [held[c, :, part * shard : tail], last, padding]
        yield jnp.concatenate(pieces, axis=1)


def correlate_kernel(offsets, scale, runs_ref, *refs):
    outs, (held, mixed, table) = refs[:offsets], refs[offsets:]
    sources = offsets * SRC
    group = held.shape[1] - sources
    held[...] = runs_ref[...].astype(held.dtype)
    product = None
    for wide in finished_shards(held):
        receivers, senders = wide[:group], wide[group:]
        fine = [pltpu.roll(receivers, MAXLAG - j, 1) for j in range(FINE)]
        coarse = [
            pltpu.roll(senders, FINE * i, 1) if i else senders for i in range(COARSE)
        ]
        term = lax.dot_general(
            jnp.concatenate(fine, axis=0).astype(jnp.bfloat16),
            jnp.concatenate(coarse, axis=0).astype(jnp.bfloat16),
            (((1,), (1,)), ((), ())),
            preferred_element_type=jnp.float32,
        )
        product = term if product is None else product + term
    product = product * scale
    for h in range(mixed.shape[0]):
        first, last = h * LANES, min((h + 1) * LANES, COARSE * sources)
        for j in range(FINE):
            mixed[h, pl.ds(j, group, stride=FINE), : last - first] = product[
                j * group : (j + 1) * group, first:last
            ]
        table[h * LANES : (h + 1) * LANES] = mixed[h].T.astype(table.dtype)
    lane = lax.broadcasted_iota(jnp.int32, (sources, LANES), 1)
    width = group * LAGS
    tiles = [None] * -(-width // LANES)

    def place(tile, piece, low, high):
        if tiles[tile] is None:
            tiles[tile] = piece
        elif low == 0:
            tiles[tile] = jnp.where(lane < high, piece, tiles[tile])
        else:
            tiles[tile] = jnp.where(lane >= low, piece, tiles[tile])

    for b in range(group):
        column = b * FINE
        for i in range(COARSE):
            piece = table[
                i * sources : (i + 1) * sources,
                column // LANES * LANES : (column // LANES + 1) * LANES,
            ]
            start = b * LAGS + i * FINE
            shift = (start - column) % LANES
            if shift:
                piece = pltpu.roll(piece, shift, 1)
            count = min(FINE, LAGS - i * FINE)
            tile, low = start // LANES, start % LANES
            place(tile, piece, low, LANES)
            if low + count > LANES:
                tiles[tile + 1] = piece
    for tile, value in enumerate(tiles):
        first = tile * LANES
        last = min(first + LANES, width)
        for o in range(offsets):
            rows = value.astype(jnp.float32)[o * SRC : (o + 1) * SRC, : last - first]
            outs[o][:, first:last] = rows.astype(jnp.bfloat16)


def stack_kernel(*refs):
    out_ref = refs[-1]
    for o, ref in enumerate(refs[:-1]):
        out_ref[:, o, :] = ref[...].astype(jnp.float32)


def call(kernel, out_shape, inputs, scratch=(), flops=0):
    single = not isinstance(out_shape, list)
    spec = pl.BlockSpec(memory_space=pltpu.VMEM)
    moved = sum(v.size * v.dtype.itemsize for v in inputs)
    return pl.pallas_call(
        kernel,
        out_shape=out_shape,
        in_specs=[spec] * len(inputs),
        out_specs=spec if single else [spec] * len(out_shape),
        scratch_shapes=list(scratch),
        compiler_params=pltpu.CompilerParams(vmem_limit_bytes=32 * 1024 * 1024),
        cost_estimate=pl.CostEstimate(
            flops=flops, bytes_accessed=moved, transcendentals=0
        ),
    )(*inputs)


def swapped(block, axis, m):
    devices = range(lax.axis_size(axis))
    return lax.ppermute(block, axis, [(k, k ^ m) for k in devices])


def body(strain_rate):
    channels, length = strain_rate.shape
    shards = lax.axis_size("tm")
    chips = shards // CORES
    reach = lax.axis_size("chan") // 4
    group = channels // shards
    steps = list(range(-reach, 0)) + list(range(1, reach + 1))
    offsets = len(steps)
    sources = offsets * SRC
    scale = 1.0 / math.sqrt(length * shards)
    run = CORES * length
    coded = run + 2 * LANES

    other = swapped(strain_rate, "tm", 1)
    own = call(
        functools.partial(pack_kernel, group, chips),
        jax.ShapeDtypeStruct((chips * group + SRC, length), jnp.float32),
        [strain_rate],
        flops=8 * channels * length,
    )
    own_sources = call(
        functools.partial(code_sources_kernel, group, chips),
        jax.ShapeDtypeStruct((SRC, coded), jnp.bfloat16),
        [own, other],
    )
    arrived = [passed_along(own_sources, "chan", d) for d in steps]
    own_receivers = call(
        functools.partial(code_receivers_kernel, group, chips),
        jax.ShapeDtypeStruct((chips * group, coded), jnp.bfloat16),
        [own, other],
        flops=8 * chips * group * run * (256 + 2 * LANES),
    )
    blocks = call(
        join_kernel,
        jax.ShapeDtypeStruct((chips, group + sources, coded), jnp.bfloat16),
        [own_receivers] + arrived,
    )
    same_core = [list(range(core, shards, CORES)) for core in range(CORES)]
    runs = lax.all_to_all(
        blocks, "tm", 0, 0, axis_index_groups=same_core, tiled=True
    )
    columns = -(-group * FINE // LANES) * LANES
    heights = -(-COARSE * sources // LANES) * LANES
    kind = jnp.float32 if group % 16 or sources % 16 else jnp.bfloat16
    results = call(
        functools.partial(correlate_kernel, offsets, scale),
        [jax.ShapeDtypeStruct((SRC, group * LAGS), jnp.bfloat16)] * offsets,
        [runs],
        scratch=[
            pltpu.VMEM((chips, group + sources, coded), kind),
            pltpu.VMEM((heights // LANES, columns, LANES), jnp.float32),
            pltpu.VMEM((heights, columns), kind),
        ],
        flops=2 * shards * (length + PAD) * group * FINE * COARSE * sources,
    )
    arrived = [passed_along(r, "chan", -d) for r, d in zip(results, steps)]
    return call(
        stack_kernel,
        jax.ShapeDtypeStruct((SRC, offsets, group * LAGS), jnp.float32),
        arrived,
    )


def solution(mesh):
    placed = (P("chan", "tm"),)
    return jax.shard_map(
        body, mesh=mesh, in_specs=placed, out_specs=P("chan", None, "tm"), check_vma=False
    )
```

```python
import functools
import math

import jax
import jax.numpy as jnp
from jax import lax
from jax.experimental import pallas as pl
from jax.experimental.pallas import tpu as pltpu
from jax.sharding import PartitionSpec as P

SRC = 8
MAXLAG = 25
W2 = 64
LAGS = 51
FINE = 8
COARSE = -(-LAGS // FINE)
LANES = 128
PAD = 128
CORES = 2


def passed_along(block, axis, distance):
    devices = range(lax.axis_size(axis))
    route = [((i - distance) % len(devices), i) for i in devices]
    return lax.ppermute(block, axis, route)


def band_matrix(rows, columns, related):
    p = lax.broadcasted_iota(jnp.int32, (rows, columns), 0)
    t = lax.broadcasted_iota(jnp.int32, (rows, columns), 1)
    return jnp.where(related(p, t), 1.0, 0.0).astype(jnp.bfloat16)


def halves(values):
    high = values.astype(jnp.bfloat16).astype(jnp.float32)
    return high, values - high


def banded_sums(pieces, band):
    height = pieces[0].shape[0]
    parts = [halves(piece) for piece in pieces]
    stacked = jnp.concatenate([p[0] for p in parts] + [p[1] for p in parts], axis=0)
    sums = jnp.dot(
        stacked.astype(jnp.bfloat16), band, preferred_element_type=jnp.float32
    )
    count = len(pieces)
    return [
        sums[c * height : (c + 1) * height]
        + sums[(count + c) * height : (count + c + 1) * height]
        for c in range(count)
    ]


def level(window_sums):
    return window_sums / (2 * W2 + 1) + 1e-05


def rows_for_here(ref, group, chips):
    me = lax.axis_index("tm")
    every = ref.shape[0] // SRC
    pieces = []
    for m in range(chips):
        start = pl.multiple_of((me ^ (CORES * m)) * group, group)
        pieces.append(ref[pl.ds(start, group)])
    pieces += [ref[q * every : q * every + 1] for q in range(SRC)]
    return jnp.concatenate(pieces, axis=0)


def pack_kernel(group, chips, x_ref, out_ref):
    out_ref[...] = rows_for_here(x_ref, group, chips)


def coded_rows(own, other):
    first_core = lax.rem(lax.axis_index("tm"), CORES) == 0
    x = jnp.concatenate(
        [jnp.where(first_core, own, other), jnp.where(first_core, other, own)], axis=1
    )
    height, length = x.shape
    border = jnp.zeros((height, LANES), jnp.float32)
    magnitude = jnp.concatenate([border, jnp.abs(x), border], axis=1)
    inner = min(256, length)
    band = band_matrix(
        inner + 2 * LANES, inner, lambda p, t: jnp.abs(p - LANES - t) <= W2
    )
    sums = jnp.concatenate(
        banded_sums(
            [
                magnitude[:, start : start + inner + 2 * LANES]
                for start in range(0, length, inner)
            ],
            band,
        ),
        axis=1,
    )
    levels = level(sums)
    normed = x / levels
    left = lax.broadcasted_iota(jnp.int32, (height, LANES), 1) < W2
    tail = length - LANES
    ends = jnp.where(left, normed[:, :LANES], normed[:, tail:])
    end_levels = jnp.where(left, levels[:, :LANES], levels[:, tail:])
    coded = jnp.concatenate([normed, halves(ends)[1], end_levels], axis=1)
    return coded.astype(jnp.bfloat16)


def code_kernel(group, own_ref, other_ref, *outs):
    blocks, sources_ref = outs[:-1], outs[-1]
    coded = coded_rows(own_ref[...], rows_for_here(other_ref, group, len(blocks)))
    for m, block in enumerate(blocks):
        block[...] = coded[m * group : (m + 1) * group]
    sources_ref[...] = coded[len(blocks) * group :]


def gather_kernel(*refs):
    refs[-1][...] = jnp.concatenate(
        [ref[...].astype(jnp.float32) for ref in refs[:-1]], axis=0
    ).astype(jnp.bfloat16)


def finished_shards(runs, held):
    chips, height, width = held.shape
    length = width - 2 * LANES
    chip = lax.div(lax.axis_index("tm"), CORES)
    for m in range(chips):
        held[chip ^ m] = runs[m]
    left = lax.broadcasted_iota(jnp.int32, (height, LANES), 1) < W2
    tail = length - LANES
    end_values, end_levels = [], []

    def lanes(c, first):
        return held[c, :, first : first + LANES].astype(jnp.float32)

    for c in range(chips):
        high = jnp.where(left, lanes(c, 0), lanes(c, tail))
        end_values.append(high + lanes(c, length))
        end_levels.append(lanes(c, length + LANES))

    def meeting(ends, outside):
        outside = [jnp.full((height, LANES), outside, jnp.float32)]
        return [
            jnp.where(left, after, before)
            for before, after in zip(outside + ends, ends + outside)
        ]

    def across(p, t):
        at_p, at_t = jnp.where(p < W2, p, p - LANES), jnp.where(t < W2, t, t - LANES)
        return ((p < W2) != (t < W2)) & (jnp.abs(at_p - at_t) <= W2)

    values, levels = meeting(end_values, 0.0), meeting(end_levels, 1.0)
    added = banded_sums(
        [jnp.abs(v) * l for v, l in zip(values, levels)],
        band_matrix(LANES, LANES, across),
    )
    ends = [
        v * l / (l + a / (2 * W2 + 1)) for v, l, a in zip(values, levels, added)
    ]
    shard = length // CORES
    padding = jnp.zeros((height, PAD), held.dtype)
    for k in range(chips * CORES):
        c, part = k // CORES, k % CORES
        pieces = [held[c, :, part * shard : (part + 1) * shard], padding]
        if part == 0:
            head = jnp.where(left, ends[c], lanes(c, 0)).astype(held.dtype)
            pieces = [head, held[c, :, LANES:shard], padding]
        if part == CORES - 1:
            last = jnp.where(left, lanes(c, tail), ends[c + 1]).astype(held.dtype)
            pieces = [held[c, :, part * shard : tail], last, padding]
        yield jnp.concatenate(pieces, axis=1)


def receiver_kernel(*refs):
    *blocks, out_ref, held = refs
    runs = [ref[...].astype(held.dtype) for ref in blocks]
    for k, wide in enumerate(finished_shards(runs, held)):
        fine = [pltpu.roll(wide, MAXLAG - j, 1) for j in range(FINE)]
        out_ref[k] = jnp.concatenate(fine, axis=0).astype(jnp.bfloat16)


def correlate_kernel(offsets, scale, receivers_ref, own_ref, other_ref, *refs):
    outs, (held, mixed, table) = refs[:offsets], refs[offsets:]
    chips, sources = held.shape[:2]
    group = receivers_ref.shape[1] // FINE
    first_core = lax.rem(lax.axis_index("tm"), CORES) == 0
    own, other = [ref[...].astype(jnp.float32) for ref in (own_ref, other_ref)]
    high, low = jnp.where(first_core, own, other), jnp.where(first_core, other, own)
    half = sources // CORES
    runs = []
    for m in range(chips):
        at = m * half
        rows = [low[at + d : at + d + SRC] for d in range(half - SRC, -1, -SRC)]
        rows.append(high[at : at + half])
        runs.append(jnp.concatenate(rows, axis=0).astype(held.dtype))
    product = None
    for k, wide in enumerate(finished_shards(runs, held)):
        coarse = [pltpu.roll(wide, FINE * i, 1) if i else wide for i in range(COARSE)]
        term = lax.dot_general(
            receivers_ref[k],
            jnp.concatenate(coarse, axis=0).astype(jnp.bfloat16),
            (((1,), (1,)), ((), ())),
            preferred_element_type=jnp.float32,
        )
        product = term if product is None else product + term
    product = product * scale
    for h in range(mixed.shape[0]):
        first, last = h * LANES, min((h + 1) * LANES, COARSE * sources)
        for j in range(FINE):
            mixed[h, pl.ds(j, group, stride=FINE), : last - first] = product[
                j * group : (j + 1) * group, first:last
            ]
        table[h * LANES : (h + 1) * LANES] = mixed[h].T.astype(table.dtype)
    lane = lax.broadcasted_iota(jnp.int32, (sources, LANES), 1)
    width = group * LAGS
    tiles = [None] * -(-width // LANES)

    def place(tile, piece, low, high):
        if tiles[tile] is None:
            tiles[tile] = piece
        elif low == 0:
            tiles[tile] = jnp.where(lane < high, piece, tiles[tile])
        else:
            tiles[tile] = jnp.where(lane >= low, piece, tiles[tile])

    for b in range(group):
        column = b * FINE
        for i in range(COARSE):
            piece = table[
                i * sources : (i + 1) * sources,
                column // LANES * LANES : (column // LANES + 1) * LANES,
            ]
            start = b * LAGS + i * FINE
            shift = (start - column) % LANES
            if shift:
                piece = pltpu.roll(piece, shift, 1)
            count = min(FINE, LAGS - i * FINE)
            tile, low = start // LANES, start % LANES
            place(tile, piece, low, LANES)
            if low + count > LANES:
                tiles[tile + 1] = piece
    for tile, value in enumerate(tiles):
        first = tile * LANES
        last = min(first + LANES, width)
        for o in range(offsets):
            rows = value.astype(jnp.float32)[o * SRC : (o + 1) * SRC, : last - first]
            outs[o][:, first:last] = rows.astype(jnp.bfloat16)


def stack_kernel(*refs):
    out_ref = refs[-1]
    for o, ref in enumerate(refs[:-1]):
        out_ref[:, o, :] = ref[...].astype(jnp.float32)


def call(kernel, out_shape, inputs, scratch=(), flops=0):
    single = not isinstance(out_shape, list)
    spec = pl.BlockSpec(memory_space=pltpu.VMEM)
    moved = sum(v.size * v.dtype.itemsize for v in inputs)
    return pl.pallas_call(
        kernel,
        out_shape=out_shape,
        in_specs=[spec] * len(inputs),
        out_specs=spec if single else [spec] * len(out_shape),
        scratch_shapes=list(scratch),
        compiler_params=pltpu.CompilerParams(vmem_limit_bytes=32 * 1024 * 1024),
        cost_estimate=pl.CostEstimate(
            flops=flops, bytes_accessed=moved, transcendentals=0
        ),
    )(*inputs)


def moved_in(rows):
    return jnp.float32 if rows % 16 else jnp.bfloat16


def swapped(block, axis, m):
    devices = range(lax.axis_size(axis))
    return lax.ppermute(block, axis, [(k, k ^ m) for k in devices])


def to_chips(block, distance, m):
    count, places = lax.axis_size("chan"), lax.axis_size("tm")
    route = []
    for i in range(count):
        for k in range(places):
            turn = distance if k % CORES == 0 else -distance
            target = (i + turn) % count * places + (k ^ (CORES * m))
            route.append((i * places + k, target))
    return lax.ppermute(block, ("chan", "tm"), route)


def body(strain_rate):
    channels, length = strain_rate.shape
    shards = lax.axis_size("tm")
    chips = shards // CORES
    reach = lax.axis_size("chan") // 4
    group = channels // shards
    steps = list(range(-reach, 0)) + list(range(1, reach + 1))
    offsets = len(steps)
    sources = offsets * SRC
    scale = 1.0 / math.sqrt(length * shards)
    run = CORES * length
    coded = run + 2 * LANES

    other = swapped(strain_rate, "tm", 1)
    own = call(
        functools.partial(pack_kernel, group, chips),
        jax.ShapeDtypeStruct((chips * group + SRC, length), jnp.float32),
        [strain_rate],
        flops=8 * channels * length,
    )
    *blocks, own_sources = call(
        functools.partial(code_kernel, group),
        [jax.ShapeDtypeStruct((group, coded), jnp.bfloat16)] * chips
        + [jax.ShapeDtypeStruct((SRC, coded), jnp.bfloat16)],
        [own, other],
        flops=8 * chips * group * run * (256 + 2 * LANES),
    )
    far_first = range(chips - 1, -1, -1)
    arrived = {
        (m, d): to_chips(own_sources, d, m) for m in far_first for d in range(1, reach + 1)
    }
    blocks = [swapped(blocks[m], "tm", CORES * m) if m else blocks[0] for m in range(chips)]
    gathered = call(
        gather_kernel,
        jax.ShapeDtypeStruct((chips * reach * SRC, coded), jnp.bfloat16),
        [arrived[m, d] for m in range(chips) for d in range(1, reach + 1)],
    )
    handed = swapped(gathered, "tm", 1)
    receivers = call(
        receiver_kernel,
        jax.ShapeDtypeStruct((shards, FINE * group, length + PAD), jnp.bfloat16),
        blocks,
        scratch=[pltpu.VMEM((chips, group, coded), moved_in(group))],
        flops=shards * group * 2 * length * length,
    )
    columns = -(-group * FINE // LANES) * LANES
    heights = -(-COARSE * sources // LANES) * LANES
    results = call(
        functools.partial(correlate_kernel, offsets, scale),
        [jax.ShapeDtypeStruct((SRC, group * LAGS), jnp.bfloat16)] * offsets,
        [receivers, gathered, handed],
        scratch=[
            pltpu.VMEM((chips, sources, coded), moved_in(sources)),
            pltpu.VMEM((heights // LANES, columns, LANES), jnp.float32),
            pltpu.VMEM((heights, columns), moved_in(sources)),
        ],
        flops=2 * shards * (length + PAD) * group * FINE * COARSE * sources,
    )
    arrived = [passed_along(r, "chan", -d) for r, d in zip(results, steps)]
    return call(
        stack_kernel,
        jax.ShapeDtypeStruct((SRC, offsets, group * LAGS), jnp.float32),
        arrived,
    )


def solution(mesh):
    placed = (P("chan", "tm"),)
    return jax.shard_map(
        body, mesh=mesh, in_specs=placed, out_specs=P("chan", None, "tm"), check_vma=False
    )
```

```python
import functools
import math

import jax
import jax.numpy as jnp
from jax import lax
from jax.experimental import pallas as pl
from jax.experimental.pallas import tpu as pltpu
from jax.sharding import PartitionSpec as P

SRC = 8
MAXLAG = 25
W2 = 64
LAGS = 51
FINE = 8
COARSE = -(-LAGS // FINE)
LANES = 128
PAD = 128
CORES = 2


def passed_along(block, axis, distance):
    devices = range(lax.axis_size(axis))
    route = [((i - distance) % len(devices), i) for i in devices]
    return lax.ppermute(block, axis, route)


def band_matrix(rows, columns, related):
    p = lax.broadcasted_iota(jnp.int32, (rows, columns), 0)
    t = lax.broadcasted_iota(jnp.int32, (rows, columns), 1)
    return jnp.where(related(p, t), 1.0, 0.0).astype(jnp.bfloat16)


def halves(values):
    high = values.astype(jnp.bfloat16).astype(jnp.float32)
    return high, values - high


def banded_sums(pieces, band):
    height = pieces[0].shape[0]
    parts = [halves(piece) for piece in pieces]
    stacked = jnp.concatenate([p[0] for p in parts] + [p[1] for p in parts], axis=0)
    sums = jnp.dot(
        stacked.astype(jnp.bfloat16), band, preferred_element_type=jnp.float32
    )
    count = len(pieces)
    return [
        sums[c * height : (c + 1) * height]
        + sums[(count + c) * height : (count + c + 1) * height]
        for c in range(count)
    ]


def level(window_sums):
    return window_sums / (2 * W2 + 1) + 1e-05


def partner(m):
    return CORES * m + 1 if m else 0


def rows_for_here(ref, group, chips):
    me = lax.axis_index("tm")
    every = ref.shape[0] // SRC
    pieces = []
    for m in range(chips):
        start = pl.multiple_of((me ^ partner(m)) * group, group)
        pieces.append(ref[pl.ds(start, group)])
    pieces += [ref[q * every : q * every + 1] for q in range(SRC)]
    return jnp.concatenate(pieces, axis=0)


def pack_kernel(group, chips, x_ref, out_ref):
    out_ref[...] = rows_for_here(x_ref, group, chips)


def coded_rows(own, other):
    first_core = lax.rem(lax.axis_index("tm"), CORES) == 0
    x = jnp.concatenate(
        [jnp.where(first_core, own, other), jnp.where(first_core, other, own)], axis=1
    )
    height, length = x.shape
    border = jnp.zeros((height, LANES), jnp.float32)
    magnitude = jnp.concatenate([border, jnp.abs(x), border], axis=1)
    inner = min(256, length)
    band = band_matrix(
        inner + 2 * LANES, inner, lambda p, t: jnp.abs(p - LANES - t) <= W2
    )
    sums = jnp.concatenate(
        banded_sums(
            [
                magnitude[:, start : start + inner + 2 * LANES]
                for start in range(0, length, inner)
            ],
            band,
        ),
        axis=1,
    )
    levels = level(sums)
    normed = x / levels
    left = lax.broadcasted_iota(jnp.int32, (height, LANES), 1) < W2
    tail = length - LANES
    ends = jnp.where(left, normed[:, :LANES], normed[:, tail:])
    end_levels = jnp.where(left, levels[:, :LANES], levels[:, tail:])
    coded = jnp.concatenate([normed, halves(ends)[1], end_levels], axis=1)
    return coded.astype(jnp.bfloat16)


def code_sources_kernel(group, chips, own_ref, other_ref, out_ref):
    first = chips * group
    other = rows_for_here(other_ref, group, chips)
    out_ref[...] = coded_rows(own_ref[first:], other[first:])


def code_receivers_kernel(group, chips, own_ref, other_ref, out_ref):
    last = chips * group
    other = rows_for_here(other_ref, group, chips)
    out_ref[...] = coded_rows(own_ref[:last], other[:last])


def join_kernel(offsets, receivers_ref, *refs):
    given, blocks = refs[:offsets], refs[offsets:]
    group = receivers_ref.shape[0] // len(blocks)
    sources = [ref[...].astype(jnp.float32) for ref in given]
    receivers = receivers_ref[...].astype(jnp.float32)
    for m, block in enumerate(blocks):
        rows = [receivers[m * group : (m + 1) * group]] + sources
        block[...] = jnp.concatenate(rows, axis=0).astype(jnp.bfloat16)


def finished_shards(runs, held):
    chips, height, width = held.shape
    length = width - 2 * LANES
    chip = lax.div(lax.axis_index("tm"), CORES)
    for m in range(chips):
        held[chip ^ m] = runs[m]
    left = lax.broadcasted_iota(jnp.int32, (height, LANES), 1) < W2
    tail = length - LANES
    end_values, end_levels = [], []

    def lanes(c, first):
        return held[c, :, first : first + LANES].astype(jnp.float32)

    for c in range(chips):
        high = jnp.where(left, lanes(c, 0), lanes(c, tail))
        end_values.append(high + lanes(c, length))
        end_levels.append(lanes(c, length + LANES))

    def meeting(ends, outside):
        outside = [jnp.full((height, LANES), outside, jnp.float32)]
        return [
            jnp.where(left, after, before)
            for before, after in zip(outside + ends, ends + outside)
        ]

    def across(p, t):
        at_p, at_t = jnp.where(p < W2, p, p - LANES), jnp.where(t < W2, t, t - LANES)
        return ((p < W2) != (t < W2)) & (jnp.abs(at_p - at_t) <= W2)

    values, levels = meeting(end_values, 0.0), meeting(end_levels, 1.0)
    added = banded_sums(
        [jnp.abs(v) * l for v, l in zip(values, levels)],
        band_matrix(LANES, LANES, across),
    )
    ends = [
        v * l / (l + a / (2 * W2 + 1)) for v, l, a in zip(values, levels, added)
    ]
    shard = length // CORES
    padding = jnp.zeros((height, PAD), held.dtype)
    for k in range(chips * CORES):
        c, part = k // CORES, k % CORES
        pieces = [held[c, :, part * shard : (part + 1) * shard], padding]
        if part == 0:
            head = jnp.where(left, ends[c], lanes(c, 0)).astype(held.dtype)
            pieces = [head, held[c, :, LANES:shard], padding]
        if part == CORES - 1:
            last = jnp.where(left, lanes(c, tail), ends[c + 1]).astype(held.dtype)
            pieces = [held[c, :, part * shard : tail], last, padding]
        yield jnp.concatenate(pieces, axis=1)


def correlate_kernel(offsets, scale, *refs):
    chips = len(refs) - offsets - 3
    blocks, refs = refs[:chips], refs[chips:]
    outs, (held, mixed, table) = refs[:offsets], refs[offsets:]
    sources = offsets * SRC
    group = held.shape[1] - sources
    runs = [ref[...].astype(held.dtype) for ref in blocks[:1] + blocks[:0:-1]]
    product = None
    for wide in finished_shards(runs, held):
        receivers, senders = wide[:group], wide[group:]
        fine = [pltpu.roll(receivers, MAXLAG - j, 1) for j in range(FINE)]
        coarse = [
            pltpu.roll(senders, FINE * i, 1) if i else senders for i in range(COARSE)
        ]
        term = lax.dot_general(
            jnp.concatenate(fine, axis=0).astype(jnp.bfloat16),
            jnp.concatenate(coarse, axis=0).astype(jnp.bfloat16),
            (((1,), (1,)), ((), ())),
            preferred_element_type=jnp.float32,
        )
        product = term if product is None else product + term
    product = product * scale
    for h in range(mixed.shape[0]):
        first, last = h * LANES, min((h + 1) * LANES, COARSE * sources)
        for j in range(FINE):
            mixed[h, pl.ds(j, group, stride=FINE), : last - first] = product[
                j * group : (j + 1) * group, first:last
            ]
        table[h * LANES : (h + 1) * LANES] = mixed[h].T.astype(table.dtype)
    lane = lax.broadcasted_iota(jnp.int32, (sources, LANES), 1)
    width = group * LAGS
    tiles = [None] * -(-width // LANES)

    def place(tile, piece, low, high):
        if tiles[tile] is None:
            tiles[tile] = piece
        elif low == 0:
            tiles[tile] = jnp.where(lane < high, piece, tiles[tile])
        else:
            tiles[tile] = jnp.where(lane >= low, piece, tiles[tile])

    for b in range(group):
        column = b * FINE
        for i in range(COARSE):
            piece = table[
                i * sources : (i + 1) * sources,
                column // LANES * LANES : (column // LANES + 1) * LANES,
            ]
            start = b * LAGS + i * FINE
            shift = (start - column) % LANES
            if shift:
                piece = pltpu.roll(piece, shift, 1)
            count = min(FINE, LAGS - i * FINE)
            tile, low = start // LANES, start % LANES
            place(tile, piece, low, LANES)
            if low + count > LANES:
                tiles[tile + 1] = piece
    for tile, value in enumerate(tiles):
        first = tile * LANES
        last = min(first + LANES, width)
        for o in range(offsets):
            rows = value.astype(jnp.float32)[o * SRC : (o + 1) * SRC, : last - first]
            outs[o][:, first:last] = rows.astype(jnp.bfloat16)


def stack_kernel(*refs):
    out_ref = refs[-1]
    for o, ref in enumerate(refs[:-1]):
        out_ref[:, o, :] = ref[...].astype(jnp.float32)


def call(kernel, out_shape, inputs, scratch=(), flops=0):
    single = not isinstance(out_shape, list)
    spec = pl.BlockSpec(memory_space=pltpu.VMEM)
    moved = sum(v.size * v.dtype.itemsize for v in inputs)
    return pl.pallas_call(
        kernel,
        out_shape=out_shape,
        in_specs=[spec] * len(inputs),
        out_specs=spec if single else [spec] * len(out_shape),
        scratch_shapes=list(scratch),
        compiler_params=pltpu.CompilerParams(vmem_limit_bytes=32 * 1024 * 1024),
        cost_estimate=pl.CostEstimate(
            flops=flops, bytes_accessed=moved, transcendentals=0
        ),
    )(*inputs)


def swapped(block, axis, m):
    devices = range(lax.axis_size(axis))
    return lax.ppermute(block, axis, [(k, k ^ m) for k in devices])


def passed_across(block, distance):
    count, places = lax.axis_size("chan"), lax.axis_size("tm")
    route = [
        ((i - distance) % count * places + (k ^ 1), i * places + k)
        for i in range(count)
        for k in range(places)
    ]
    return lax.ppermute(block, ("chan", "tm"), route)


def body(strain_rate):
    channels, length = strain_rate.shape
    shards = lax.axis_size("tm")
    chips = shards // CORES
    reach = lax.axis_size("chan") // 4
    group = channels // shards
    steps = list(range(-reach, 0)) + list(range(1, reach + 1))
    offsets = len(steps)
    sources = offsets * SRC
    scale = 1.0 / math.sqrt(length * shards)
    run = CORES * length
    coded = run + 2 * LANES

    other = swapped(strain_rate, "tm", 1)
    own = call(
        functools.partial(pack_kernel, group, chips),
        jax.ShapeDtypeStruct((chips * group + SRC, length), jnp.float32),
        [strain_rate],
        flops=8 * channels * length,
    )
    own_sources = call(
        functools.partial(code_sources_kernel, group, chips),
        jax.ShapeDtypeStruct((SRC, coded), jnp.bfloat16),
        [own, other],
    )
    arrived = [passed_across(own_sources, d) for d in steps]
    own_receivers = call(
        functools.partial(code_receivers_kernel, group, chips),
        jax.ShapeDtypeStruct((chips * group, coded), jnp.bfloat16),
        [own, other],
        flops=8 * chips * group * run * (256 + 2 * LANES),
    )
    blocks = call(
        functools.partial(join_kernel, offsets),
        [jax.ShapeDtypeStruct((group + sources, coded), jnp.bfloat16)] * chips,
        [own_receivers] + arrived,
    )
    blocks = list(blocks[:1]) + [
        swapped(blocks[m], "tm", partner(m)) for m in range(chips - 1, 0, -1)
    ]
    columns = -(-group * FINE // LANES) * LANES
    heights = -(-COARSE * sources // LANES) * LANES
    kind = jnp.float32 if group % 16 or sources % 16 else jnp.bfloat16
    results = call(
        functools.partial(correlate_kernel, offsets, scale),
        [jax.ShapeDtypeStruct((SRC, group * LAGS), jnp.bfloat16)] * offsets,
        blocks,
        scratch=[
            pltpu.VMEM((chips, group + sources, coded), kind),
            pltpu.VMEM((heights // LANES, columns, LANES), jnp.float32),
            pltpu.VMEM((heights, columns), kind),
        ],
        flops=2 * shards * (length + PAD) * group * FINE * COARSE * sources,
    )
    arrived = [passed_along(r, "chan", -d) for r, d in zip(results, steps)]
    return call(
        stack_kernel,
        jax.ShapeDtypeStruct((SRC, offsets, group * LAGS), jnp.float32),
        arrived,
    )


def solution(mesh):
    placed = (P("chan", "tm"),)
    return jax.shard_map(
        body, mesh=mesh, in_specs=placed, out_specs=P("chan", None, "tm"), check_vma=False
    )
```

```python
import functools
import math

import jax
import jax.numpy as jnp
from jax import lax
from jax.experimental import pallas as pl
from jax.experimental.pallas import tpu as pltpu
from jax.sharding import PartitionSpec as P

SRC = 8
MAXLAG = 25
W2 = 64
LAGS = 51
FINE = 8
COARSE = -(-LAGS // FINE)
LANES = 128
PAD = 128
CORES = 2


def band_matrix(rows, columns, related):
    p = lax.broadcasted_iota(jnp.int32, (rows, columns), 0)
    t = lax.broadcasted_iota(jnp.int32, (rows, columns), 1)
    return jnp.where(related(p, t), 1.0, 0.0).astype(jnp.bfloat16)


def halves(values):
    high = values.astype(jnp.bfloat16).astype(jnp.float32)
    return high, values - high


def banded_sums(pieces, band):
    height = pieces[0].shape[0]
    parts = [halves(piece) for piece in pieces]
    stacked = jnp.concatenate([p[0] for p in parts] + [p[1] for p in parts], axis=0)
    sums = jnp.dot(
        stacked.astype(jnp.bfloat16), band, preferred_element_type=jnp.float32
    )
    count = len(pieces)
    return [
        sums[c * height : (c + 1) * height]
        + sums[(count + c) * height : (count + c + 1) * height]
        for c in range(count)
    ]


def level(window_sums):
    return window_sums / (2 * W2 + 1) + 1e-05


def rows_for_here(ref, group, chips):
    me = lax.axis_index("tm")
    every = ref.shape[0] // SRC
    pieces = []
    for m in range(chips):
        start = pl.multiple_of((me ^ (CORES * m + 1)) * group, group)
        pieces.append(ref[pl.ds(start, group)])
    pieces += [ref[q * every : q * every + 1] for q in range(SRC)]
    return jnp.concatenate(pieces, axis=0)


def pack_kernel(group, chips, x_ref, out_ref):
    out_ref[...] = rows_for_here(x_ref, group, chips)


def coded_rows(own, other):
    first_core = lax.rem(lax.axis_index("tm"), CORES) == 0
    x = jnp.concatenate(
        [jnp.where(first_core, own, other), jnp.where(first_core, other, own)], axis=1
    )
    height, length = x.shape
    border = jnp.zeros((height, LANES), jnp.float32)
    magnitude = jnp.concatenate([border, jnp.abs(x), border], axis=1)
    inner = min(256, length)
    band = band_matrix(
        inner + 2 * LANES, inner, lambda p, t: jnp.abs(p - LANES - t) <= W2
    )
    sums = jnp.concatenate(
        banded_sums(
            [
                magnitude[:, start : start + inner + 2 * LANES]
                for start in range(0, length, inner)
            ],
            band,
        ),
        axis=1,
    )
    levels = level(sums)
    normed = x / levels
    left = lax.broadcasted_iota(jnp.int32, (height, LANES), 1) < W2
    tail = length - LANES
    ends = jnp.where(left, normed[:, :LANES], normed[:, tail:])
    end_levels = jnp.where(left, levels[:, :LANES], levels[:, tail:])
    coded = jnp.concatenate([normed, halves(ends)[1], end_levels], axis=1)
    return coded.astype(jnp.bfloat16)


def code_sources_kernel(group, chips, own_ref, other_ref, out_ref):
    first = chips * group
    other = rows_for_here(other_ref, group, chips)
    out_ref[...] = coded_rows(own_ref[first:], other[first:])


def code_receivers_kernel(group, chips, own_ref, other_ref, out_ref):
    last = chips * group
    other = rows_for_here(other_ref, group, chips)
    out_ref[...] = coded_rows(own_ref[:last], other[:last])


def join_kernel(offsets, receivers_ref, *refs):
    given, blocks = refs[:offsets], refs[offsets:]
    group = receivers_ref.shape[0] // len(blocks)
    sources = [ref[...].astype(jnp.float32) for ref in given]
    receivers = receivers_ref[...].astype(jnp.float32)
    for m, block in enumerate(blocks):
        rows = [receivers[m * group : (m + 1) * group]] + sources
        block[...] = jnp.concatenate(rows, axis=0).astype(jnp.bfloat16)


def finished_shards(runs, held):
    chips, height, width = held.shape
    length = width - 2 * LANES
    chip = lax.div(lax.axis_index("tm"), CORES)
    for m in range(chips):
        held[chip ^ m] = runs[m]
    left = lax.broadcasted_iota(jnp.int32, (height, LANES), 1) < W2
    tail = length - LANES
    end_values, end_levels = [], []

    def lanes(c, first):
        return held[c, :, first : first + LANES].astype(jnp.float32)

    for c in range(chips):
        high = jnp.where(left, lanes(c, 0), lanes(c, tail))
        end_values.append(high + lanes(c, length))
        end_levels.append(lanes(c, length + LANES))

    def meeting(ends, outside):
        outside = [jnp.full((height, LANES), outside, jnp.float32)]
        return [
            jnp.where(left, after, before)
            for before, after in zip(outside + ends, ends + outside)
        ]

    def across(p, t):
        at_p, at_t = jnp.where(p < W2, p, p - LANES), jnp.where(t < W2, t, t - LANES)
        return ((p < W2) != (t < W2)) & (jnp.abs(at_p - at_t) <= W2)

    values, levels = meeting(end_values, 0.0), meeting(end_levels, 1.0)
    added = banded_sums(
        [jnp.abs(v) * l for v, l in zip(values, levels)],
        band_matrix(LANES, LANES, across),
    )
    ends = [
        v * l / (l + a / (2 * W2 + 1)) for v, l, a in zip(values, levels, added)
    ]
    shard = length // CORES
    padding = jnp.zeros((height, PAD), held.dtype)
    for k in range(chips * CORES):
        c, part = k // CORES, k % CORES
        pieces = [held[c, :, part * shard : (part + 1) * shard], padding]
        if part == 0:
            head = jnp.where(left, ends[c], lanes(c, 0)).astype(held.dtype)
            pieces = [head, held[c, :, LANES:shard], padding]
        if part == CORES - 1:
            last = jnp.where(left, lanes(c, tail), ends[c + 1]).astype(held.dtype)
            pieces = [held[c, :, part * shard : tail], last, padding]
        yield jnp.concatenate(pieces, axis=1)


def correlate_kernel(offsets, scale, *refs):
    chips = len(refs) - offsets - 3
    blocks, refs = refs[:chips], refs[chips:]
    outs, (held, mixed, table) = refs[:offsets], refs[offsets:]
    sources = offsets * SRC
    group = held.shape[1] - sources
    runs = [ref[...].astype(held.dtype) for ref in blocks[:1] + blocks[:0:-1]]
    product = None
    for wide in finished_shards(runs, held):
        receivers, senders = wide[:group], wide[group:]
        fine = [pltpu.roll(receivers, MAXLAG - j, 1) for j in range(FINE)]
        coarse = [
            pltpu.roll(senders, FINE * i, 1) if i else senders for i in range(COARSE)
        ]
        term = lax.dot_general(
            jnp.concatenate(fine, axis=0).astype(jnp.bfloat16),
            jnp.concatenate(coarse, axis=0).astype(jnp.bfloat16),
            (((1,), (1,)), ((), ())),
            preferred_element_type=jnp.float32,
        )
        product = term if product is None else product + term
    product = product * scale
    for h in range(mixed.shape[0]):
        first, last = h * LANES, min((h + 1) * LANES, COARSE * sources)
        for j in range(FINE):
            mixed[h, pl.ds(j, group, stride=FINE), : last - first] = product[
                j * group : (j + 1) * group, first:last
            ]
        table[h * LANES : (h + 1) * LANES] = mixed[h].T.astype(table.dtype)
    lane = lax.broadcasted_iota(jnp.int32, (sources, LANES), 1)
    width = group * LAGS
    tiles = [None] * -(-width // LANES)

    def place(tile, piece, low, high):
        if tiles[tile] is None:
            tiles[tile] = piece
        elif low == 0:
            tiles[tile] = jnp.where(lane < high, piece, tiles[tile])
        else:
            tiles[tile] = jnp.where(lane >= low, piece, tiles[tile])

    for b in range(group):
        column = b * FINE
        for i in range(COARSE):
            piece = table[
                i * sources : (i + 1) * sources,
                column // LANES * LANES : (column // LANES + 1) * LANES,
            ]
            start = b * LAGS + i * FINE
            shift = (start - column) % LANES
            if shift:
                piece = pltpu.roll(piece, shift, 1)
            count = min(FINE, LAGS - i * FINE)
            tile, low = start // LANES, start % LANES
            place(tile, piece, low, LANES)
            if low + count > LANES:
                tiles[tile + 1] = piece
    for tile, value in enumerate(tiles):
        first = tile * LANES
        last = min(first + LANES, width)
        for o in range(offsets):
            rows = value.astype(jnp.float32)[o * SRC : (o + 1) * SRC, : last - first]
            outs[o][:, first:last] = rows.astype(jnp.bfloat16)


def stack_kernel(*refs):
    out_ref = refs[-1]
    for o, ref in enumerate(refs[:-1]):
        out_ref[:, o, :] = ref[...].astype(jnp.float32)


def call(kernel, out_shape, inputs, scratch=(), flops=0):
    single = not isinstance(out_shape, list)
    spec = pl.BlockSpec(memory_space=pltpu.VMEM)
    moved = sum(v.size * v.dtype.itemsize for v in inputs)
    return pl.pallas_call(
        kernel,
        out_shape=out_shape,
        in_specs=[spec] * len(inputs),
        out_specs=spec if single else [spec] * len(out_shape),
        scratch_shapes=list(scratch),
        compiler_params=pltpu.CompilerParams(vmem_limit_bytes=32 * 1024 * 1024),
        cost_estimate=pl.CostEstimate(
            flops=flops, bytes_accessed=moved, transcendentals=0
        ),
    )(*inputs)


def swapped(block, axis, m):
    devices = range(lax.axis_size(axis))
    return lax.ppermute(block, axis, [(k, k ^ m) for k in devices])


def passed_across(block, distance):
    count, places = lax.axis_size("chan"), lax.axis_size("tm")
    route = [
        ((i - distance) % count * places + (k ^ 1), i * places + k)
        for i in range(count)
        for k in range(places)
    ]
    return lax.ppermute(block, ("chan", "tm"), route)


def body(strain_rate):
    channels, length = strain_rate.shape
    shards = lax.axis_size("tm")
    chips = shards // CORES
    reach = lax.axis_size("chan") // 4
    group = channels // shards
    steps = list(range(-reach, 0)) + list(range(1, reach + 1))
    offsets = len(steps)
    sources = offsets * SRC
    scale = 1.0 / math.sqrt(length * shards)
    run = CORES * length
    coded = run + 2 * LANES

    other = swapped(strain_rate, "tm", 1)
    own = call(
        functools.partial(pack_kernel, group, chips),
        jax.ShapeDtypeStruct((chips * group + SRC, length), jnp.float32),
        [strain_rate],
        flops=8 * channels * length,
    )
    own_sources = call(
        functools.partial(code_sources_kernel, group, chips),
        jax.ShapeDtypeStruct((SRC, coded), jnp.bfloat16),
        [own, other],
    )
    arrived = [passed_across(own_sources, d) for d in steps]
    own_receivers = call(
        functools.partial(code_receivers_kernel, group, chips),
        jax.ShapeDtypeStruct((chips * group, coded), jnp.bfloat16),
        [own, other],
        flops=8 * chips * group * run * (256 + 2 * LANES),
    )
    blocks = call(
        functools.partial(join_kernel, offsets),
        [jax.ShapeDtypeStruct((group + sources, coded), jnp.bfloat16)] * chips,
        [own_receivers] + arrived,
    )
    blocks = list(blocks[:1]) + [
        swapped(blocks[m], "tm", CORES * m) for m in range(chips - 1, 0, -1)
    ]
    columns = -(-group * FINE // LANES) * LANES
    heights = -(-COARSE * sources // LANES) * LANES
    kind = jnp.float32 if group % 16 or sources % 16 else jnp.bfloat16
    results = call(
        functools.partial(correlate_kernel, offsets, scale),
        [jax.ShapeDtypeStruct((SRC, group * LAGS), jnp.bfloat16)] * offsets,
        blocks,
        scratch=[
            pltpu.VMEM((chips, group + sources, coded), kind),
            pltpu.VMEM((heights // LANES, columns, LANES), jnp.float32),
            pltpu.VMEM((heights, columns), kind),
        ],
        flops=2 * shards * (length + PAD) * group * FINE * COARSE * sources,
    )
    arrived = [passed_across(r, -d) for r, d in zip(results, steps)]
    return call(
        stack_kernel,
        jax.ShapeDtypeStruct((SRC, offsets, group * LAGS), jnp.float32),
        arrived,
    )


def solution(mesh):
    placed = (P("chan", "tm"),)
    return jax.shard_map(
        body, mesh=mesh, in_specs=placed, out_specs=P("chan", None, "tm"), check_vma=False
    )
```

```python
import functools
import math

import jax
import jax.numpy as jnp
from jax import lax
from jax.experimental import pallas as pl
from jax.experimental.pallas import tpu as pltpu
from jax.sharding import PartitionSpec as P

SRC = 8
MAXLAG = 25
W2 = 64
LAGS = 51
FINE = 8
COARSE = -(-LAGS // FINE)
LANES = 128
PAD = 128
CORES = 2


def band_matrix(rows, columns, related):
    p = lax.broadcasted_iota(jnp.int32, (rows, columns), 0)
    t = lax.broadcasted_iota(jnp.int32, (rows, columns), 1)
    return jnp.where(related(p, t), 1.0, 0.0).astype(jnp.bfloat16)


def halves(values):
    high = values.astype(jnp.bfloat16).astype(jnp.float32)
    return high, values - high


def banded_sums(pieces, band):
    height = pieces[0].shape[0]
    parts = [halves(piece) for piece in pieces]
    stacked = jnp.concatenate([p[0] for p in parts] + [p[1] for p in parts], axis=0)
    sums = jnp.dot(
        stacked.astype(jnp.bfloat16), band, preferred_element_type=jnp.float32
    )
    count = len(pieces)
    return [
        sums[c * height : (c + 1) * height]
        + sums[(count + c) * height : (count + c + 1) * height]
        for c in range(count)
    ]


def level(window_sums):
    return window_sums / (2 * W2 + 1) + 1e-05


def rows_for_here(ref, group, chips):
    me = lax.axis_index("tm")
    every = ref.shape[0] // SRC
    pieces = []
    for m in range(chips):
        start = pl.multiple_of((me ^ (CORES * m + 1)) * group, group)
        pieces.append(ref[pl.ds(start, group)])
    pieces += [ref[q * every : q * every + 1] for q in range(SRC)]
    return jnp.concatenate(pieces, axis=0)


def pack_kernel(group, chips, x_ref, out_ref):
    out_ref[...] = rows_for_here(x_ref, group, chips)


def coded_rows(own, other):
    first_core = lax.rem(lax.axis_index("tm"), CORES) == 0
    x = jnp.concatenate(
        [jnp.where(first_core, own, other), jnp.where(first_core, other, own)], axis=1
    )
    height, length = x.shape
    border = jnp.zeros((height, LANES), jnp.float32)
    magnitude = jnp.concatenate([border, jnp.abs(x), border], axis=1)
    inner = min(256, length)
    band = band_matrix(
        inner + 2 * LANES, inner, lambda p, t: jnp.abs(p - LANES - t) <= W2
    )
    sums = jnp.concatenate(
        banded_sums(
            [
                magnitude[:, start : start + inner + 2 * LANES]
                for start in range(0, length, inner)
            ],
            band,
        ),
        axis=1,
    )
    levels = level(sums)
    normed = x / levels
    left = lax.broadcasted_iota(jnp.int32, (height, LANES), 1) < W2
    tail = length - LANES
    ends = jnp.where(left, normed[:, :LANES], normed[:, tail:])
    end_levels = jnp.where(left, levels[:, :LANES], levels[:, tail:])
    coded = jnp.concatenate([normed, halves(ends)[1], end_levels], axis=1)
    return coded.astype(jnp.bfloat16)


def code_sources_kernel(group, chips, own_ref, other_ref, out_ref):
    first = chips * group
    other = rows_for_here(other_ref, group, chips)
    out_ref[...] = coded_rows(own_ref[first:], other[first:])


def code_receivers_kernel(group, chips, own_ref, other_ref, out_ref):
    last = chips * group
    other = rows_for_here(other_ref, group, chips)
    out_ref[...] = coded_rows(own_ref[:last], other[:last])


def join_kernel(offsets, receivers_ref, *refs):
    given, blocks = refs[:offsets], refs[offsets:]
    group = receivers_ref.shape[0] // len(blocks)
    sources = [ref[...].astype(jnp.float32) for ref in given]
    receivers = receivers_ref[...].astype(jnp.float32)
    for m, block in enumerate(blocks):
        rows = [receivers[m * group : (m + 1) * group]] + sources
        block[...] = jnp.concatenate(rows, axis=0).astype(jnp.bfloat16)


def finished_shards(runs, held):
    chips, height, width = held.shape
    length = width - 2 * LANES
    chip = lax.div(lax.axis_index("tm"), CORES)
    for m in range(chips):
        held[chip ^ m] = runs[m]
    left = lax.broadcasted_iota(jnp.int32, (height, LANES), 1) < W2
    tail = length - LANES
    end_values, end_levels = [], []

    def lanes(c, first):
        return held[c, :, first : first + LANES].astype(jnp.float32)

    for c in range(chips):
        high = jnp.where(left, lanes(c, 0), lanes(c, tail))
        end_values.append(high + lanes(c, length))
        end_levels.append(lanes(c, length + LANES))

    def meeting(ends, outside):
        outside = [jnp.full((height, LANES), outside, jnp.float32)]
        return [
            jnp.where(left, after, before)
            for before, after in zip(outside + ends, ends + outside)
        ]

    def across(p, t):
        at_p, at_t = jnp.where(p < W2, p, p - LANES), jnp.where(t < W2, t, t - LANES)
        return ((p < W2) != (t < W2)) & (jnp.abs(at_p - at_t) <= W2)

    values, levels = meeting(end_values, 0.0), meeting(end_levels, 1.0)
    added = banded_sums(
        [jnp.abs(v) * l for v, l in zip(values, levels)],
        band_matrix(LANES, LANES, across),
    )
    ends = [
        v * l / (l + a / (2 * W2 + 1)) for v, l, a in zip(values, levels, added)
    ]
    shard = length // CORES
    padding = jnp.zeros((height, PAD), held.dtype)
    for k in range(chips * CORES):
        c, part = k // CORES, k % CORES
        pieces = [held[c, :, part * shard : (part + 1) * shard], padding]
        if part == 0:
            head = jnp.where(left, ends[c], lanes(c, 0)).astype(held.dtype)
            pieces = [head, held[c, :, LANES:shard], padding]
        if part == CORES - 1:
            last = jnp.where(left, lanes(c, tail), ends[c + 1]).astype(held.dtype)
            pieces = [held[c, :, part * shard : tail], last, padding]
        yield jnp.concatenate(pieces, axis=1)


def correlate_kernel(offsets, scale, *refs):
    chips = len(refs) - offsets - 3
    blocks, refs = refs[:chips], refs[chips:]
    outs, (held, mixed, table) = refs[:offsets], refs[offsets:]
    sources = offsets * SRC
    group = held.shape[1] - sources
    runs = [ref[...].astype(held.dtype) for ref in blocks[:1] + blocks[:0:-1]]
    product = None
    for wide in finished_shards(runs, held):
        receivers, senders = wide[:group], wide[group:]
        fine = [pltpu.roll(receivers, MAXLAG - j, 1) for j in range(FINE)]
        coarse = [
            pltpu.roll(senders, FINE * i, 1) if i else senders for i in range(COARSE)
        ]
        term = lax.dot_general(
            jnp.concatenate(coarse, axis=0).astype(jnp.bfloat16),
            jnp.concatenate(fine, axis=0).astype(jnp.bfloat16),
            (((1,), (1,)), ((), ())),
            preferred_element_type=jnp.float32,
        )
        product = term if product is None else product + term
    product = (product * scale).T
    for h in range(mixed.shape[0]):
        first, last = h * LANES, min((h + 1) * LANES, COARSE * sources)
        for j in range(FINE):
            mixed[h, pl.ds(j, group, stride=FINE), : last - first] = product[
                j * group : (j + 1) * group, first:last
            ]
        table[h * LANES : (h + 1) * LANES] = mixed[h].T.astype(table.dtype)
    lane = lax.broadcasted_iota(jnp.int32, (sources, LANES), 1)
    width = group * LAGS
    tiles = [None] * -(-width // LANES)

    def place(tile, piece, low, high):
        if tiles[tile] is None:
            tiles[tile] = piece
        elif low == 0:
            tiles[tile] = jnp.where(lane < high, piece, tiles[tile])
        else:
            tiles[tile] = jnp.where(lane >= low, piece, tiles[tile])

    for b in range(group):
        column = b * FINE
        for i in range(COARSE):
            piece = table[
                i * sources : (i + 1) * sources,
                column // LANES * LANES : (column // LANES + 1) * LANES,
            ]
            start = b * LAGS + i * FINE
            shift = (start - column) % LANES
            if shift:
                piece = pltpu.roll(piece, shift, 1)
            count = min(FINE, LAGS - i * FINE)
            tile, low = start // LANES, start % LANES
            place(tile, piece, low, LANES)
            if low + count > LANES:
                tiles[tile + 1] = piece
    for tile, value in enumerate(tiles):
        first = tile * LANES
        last = min(first + LANES, width)
        for o in range(offsets):
            rows = value.astype(jnp.float32)[o * SRC : (o + 1) * SRC, : last - first]
            outs[o][:, first:last] = rows.astype(jnp.bfloat16)


def stack_kernel(*refs):
    out_ref = refs[-1]
    for o, ref in enumerate(refs[:-1]):
        out_ref[:, o, :] = ref[...].astype(jnp.float32)


def call(kernel, out_shape, inputs, scratch=(), flops=0):
    single = not isinstance(out_shape, list)
    spec = pl.BlockSpec(memory_space=pltpu.VMEM)
    moved = sum(v.size * v.dtype.itemsize for v in inputs)
    return pl.pallas_call(
        kernel,
        out_shape=out_shape,
        in_specs=[spec] * len(inputs),
        out_specs=spec if single else [spec] * len(out_shape),
        scratch_shapes=list(scratch),
        compiler_params=pltpu.CompilerParams(vmem_limit_bytes=32 * 1024 * 1024),
        cost_estimate=pl.CostEstimate(
            flops=flops, bytes_accessed=moved, transcendentals=0
        ),
    )(*inputs)


def swapped(block, axis, m):
    devices = range(lax.axis_size(axis))
    return lax.ppermute(block, axis, [(k, k ^ m) for k in devices])


def passed_along(block, distance):
    devices = range(lax.axis_size("chan"))
    route = [((i - distance) % len(devices), i) for i in devices]
    return lax.ppermute(block, "chan", route)


def passed_across(block, distance):
    count, places = lax.axis_size("chan"), lax.axis_size("tm")
    route = [
        ((i - distance) % count * places + (k ^ 1), i * places + k)
        for i in range(count)
        for k in range(places)
    ]
    return lax.ppermute(block, ("chan", "tm"), route)


def body(strain_rate):
    channels, length = strain_rate.shape
    shards = lax.axis_size("tm")
    chips = shards // CORES
    reach = lax.axis_size("chan") // 4
    group = channels // shards
    steps = list(range(-reach, 0)) + list(range(1, reach + 1))
    offsets = len(steps)
    sources = offsets * SRC
    scale = 1.0 / math.sqrt(length * shards)
    run = CORES * length
    coded = run + 2 * LANES

    other = swapped(strain_rate, "tm", 1)
    own = call(
        functools.partial(pack_kernel, group, chips),
        jax.ShapeDtypeStruct((chips * group + SRC, length), jnp.float32),
        [strain_rate],
        flops=8 * channels * length,
    )
    own_sources = call(
        functools.partial(code_sources_kernel, group, chips),
        jax.ShapeDtypeStruct((SRC, coded), jnp.bfloat16),
        [own, other],
    )
    arrived = [passed_along(own_sources, d) for d in steps]
    own_receivers = call(
        functools.partial(code_receivers_kernel, group, chips),
        jax.ShapeDtypeStruct((chips * group, coded), jnp.bfloat16),
        [own, other],
        flops=8 * chips * group * run * (256 + 2 * LANES),
    )
    blocks = call(
        functools.partial(join_kernel, offsets),
        [jax.ShapeDtypeStruct((group + sources, coded), jnp.bfloat16)] * chips,
        [own_receivers] + arrived,
    )
    blocks = list(blocks[:1]) + [
        swapped(blocks[m], "tm", CORES * m) for m in range(chips - 1, 0, -1)
    ]
    columns = -(-group * FINE // LANES) * LANES
    heights = -(-COARSE * sources // LANES) * LANES
    kind = jnp.float32 if group % 16 or sources % 16 else jnp.bfloat16
    results = call(
        functools.partial(correlate_kernel, offsets, scale),
        [jax.ShapeDtypeStruct((SRC, group * LAGS), jnp.bfloat16)] * offsets,
        blocks,
        scratch=[
            pltpu.VMEM((chips, group + sources, coded), kind),
            pltpu.VMEM((heights // LANES, columns, LANES), jnp.float32),
            pltpu.VMEM((heights, columns), kind),
        ],
        flops=2 * shards * (length + PAD) * group * FINE * COARSE * sources,
    )
    arrived = [passed_across(r, -d) for r, d in zip(results, steps)]
    return call(
        stack_kernel,
        jax.ShapeDtypeStruct((SRC, offsets, group * LAGS), jnp.float32),
        arrived,
    )


def solution(mesh):
    placed = (P("chan", "tm"),)
    return jax.shard_map(
        body, mesh=mesh, in_specs=placed, out_specs=P("chan", None, "tm"), check_vma=False
    )
```

```python
import functools
import math

import jax
import jax.numpy as jnp
from jax import lax
from jax.experimental import pallas as pl
from jax.experimental.pallas import tpu as pltpu
from jax.sharding import PartitionSpec as P

SRC = 8
MAXLAG = 25
W2 = 64
LAGS = 51
FINE = 8
COARSE = -(-LAGS // FINE)
LANES = 128
PAD = 128
CORES = 2


def band_matrix(rows, columns, related):
    p = lax.broadcasted_iota(jnp.int32, (rows, columns), 0)
    t = lax.broadcasted_iota(jnp.int32, (rows, columns), 1)
    return jnp.where(related(p, t), 1.0, 0.0).astype(jnp.bfloat16)


def halves(values):
    high = values.astype(jnp.bfloat16).astype(jnp.float32)
    return high, values - high


def banded_sums(pieces, band):
    height = pieces[0].shape[0]
    parts = [halves(piece) for piece in pieces]
    stacked = jnp.concatenate([p[0] for p in parts] + [p[1] for p in parts], axis=0)
    sums = jnp.dot(
        stacked.astype(jnp.bfloat16), band, preferred_element_type=jnp.float32
    )
    count = len(pieces)
    return [
        sums[c * height : (c + 1) * height]
        + sums[(count + c) * height : (count + c + 1) * height]
        for c in range(count)
    ]


def level(window_sums):
    return window_sums / (2 * W2 + 1) + 1e-05


def rows_for_here(ref, group, chips):
    me = lax.axis_index("tm")
    every = ref.shape[0] // SRC
    pieces = []
    for m in range(chips):
        start = pl.multiple_of((me ^ (CORES * m + 1)) * group, group)
        pieces.append(ref[pl.ds(start, group)])
    pieces += [ref[q * every : q * every + 1] for q in range(SRC)]
    return jnp.concatenate(pieces, axis=0)


def pack_kernel(group, chips, x_ref, out_ref):
    out_ref[...] = rows_for_here(x_ref, group, chips)


def coded_rows(own, other):
    first_core = lax.rem(lax.axis_index("tm"), CORES) == 0
    x = jnp.concatenate(
        [jnp.where(first_core, own, other), jnp.where(first_core, other, own)], axis=1
    )
    height, length = x.shape
    border = jnp.zeros((height, LANES), jnp.float32)
    magnitude = jnp.concatenate([border, jnp.abs(x), border], axis=1)
    inner = min(256, length)
    band = band_matrix(
        inner + 2 * LANES, inner, lambda p, t: jnp.abs(p - LANES - t) <= W2
    )
    sums = jnp.concatenate(
        banded_sums(
            [
                magnitude[:, start : start + inner + 2 * LANES]
                for start in range(0, length, inner)
            ],
            band,
        ),
        axis=1,
    )
    levels = level(sums)
    normed = x / levels
    left = lax.broadcasted_iota(jnp.int32, (height, LANES), 1) < W2
    tail = length - LANES
    ends = jnp.where(left, normed[:, :LANES], normed[:, tail:])
    end_levels = jnp.where(left, levels[:, :LANES], levels[:, tail:])
    coded = jnp.concatenate([normed, halves(ends)[1], end_levels], axis=1)
    return coded.astype(jnp.bfloat16)


def code_sources_kernel(group, chips, own_ref, other_ref, out_ref):
    first = chips * group
    other = rows_for_here(other_ref, group, chips)
    out_ref[...] = coded_rows(own_ref[first:], other[first:])


def code_receivers_kernel(group, chips, own_ref, other_ref, out_ref):
    last = chips * group
    other = rows_for_here(other_ref, group, chips)
    out_ref[...] = coded_rows(own_ref[:last], other[:last])


def join_kernel(offsets, receivers_ref, *refs):
    given, blocks = refs[:offsets], refs[offsets:]
    group = receivers_ref.shape[0] // len(blocks)
    sources = [ref[...].astype(jnp.float32) for ref in given]
    receivers = receivers_ref[...].astype(jnp.float32)
    for m, block in enumerate(blocks):
        rows = [receivers[m * group : (m + 1) * group]] + sources
        block[...] = jnp.concatenate(rows, axis=0).astype(jnp.bfloat16)


def finished_runs(runs, held):
    chips, height, width = held.shape
    length = width - 2 * LANES
    chip = lax.div(lax.axis_index("tm"), CORES)
    for m in range(chips):
        held[chip ^ m] = runs[m]
    left = lax.broadcasted_iota(jnp.int32, (height, LANES), 1) < W2
    tail = length - LANES
    end_values, end_levels = [], []

    def lanes(c, first):
        return held[c, :, first : first + LANES].astype(jnp.float32)

    for c in range(chips):
        high = jnp.where(left, lanes(c, 0), lanes(c, tail))
        end_values.append(high + lanes(c, length))
        end_levels.append(lanes(c, length + LANES))

    def meeting(ends, outside):
        outside = [jnp.full((height, LANES), outside, jnp.float32)]
        return [
            jnp.where(left, after, before)
            for before, after in zip(outside + ends, ends + outside)
        ]

    def across(p, t):
        at_p, at_t = jnp.where(p < W2, p, p - LANES), jnp.where(t < W2, t, t - LANES)
        return ((p < W2) != (t < W2)) & (jnp.abs(at_p - at_t) <= W2)

    values, levels = meeting(end_values, 0.0), meeting(end_levels, 1.0)
    added = banded_sums(
        [jnp.abs(v) * l for v, l in zip(values, levels)],
        band_matrix(LANES, LANES, across),
    )
    ends = [
        v * l / (l + a / (2 * W2 + 1)) for v, l, a in zip(values, levels, added)
    ]
    shard = length // CORES
    padding = jnp.zeros((height, PAD), held.dtype)
    for c in range(chips):
        head = jnp.where(left, ends[c], lanes(c, 0)).astype(held.dtype)
        last = jnp.where(left, lanes(c, tail), ends[c + 1]).astype(held.dtype)
        pieces = [head, held[c, :, LANES:shard], padding]
        for start in range(shard, length - shard, shard):
            pieces += [held[c, :, start : start + shard], padding]
        pieces += [held[c, :, length - shard : tail], last, padding]
        yield jnp.concatenate(pieces, axis=1)


def correlate_kernel(offsets, scale, *refs):
    chips = len(refs) - offsets - 3
    blocks, refs = refs[:chips], refs[chips:]
    outs, (held, mixed, table) = refs[:offsets], refs[offsets:]
    sources = offsets * SRC
    group = held.shape[1] - sources
    runs = [ref[...].astype(held.dtype) for ref in blocks[:1] + blocks[:0:-1]]
    product = None
    for wide in finished_runs(runs, held):
        receivers, senders = wide[:group], wide[group:]
        fine = [pltpu.roll(receivers, MAXLAG - j, 1) for j in range(FINE)]
        coarse = [
            pltpu.roll(senders, FINE * i, 1) if i else senders for i in range(COARSE)
        ]
        term = lax.dot_general(
            jnp.concatenate(fine, axis=0).astype(jnp.bfloat16),
            jnp.concatenate(coarse, axis=0).astype(jnp.bfloat16),
            (((1,), (1,)), ((), ())),
            preferred_element_type=jnp.float32,
        )
        product = term if product is None else product + term
    product = product * scale
    for h in range(mixed.shape[0]):
        first, last = h * LANES, min((h + 1) * LANES, COARSE * sources)
        for j in range(FINE):
            mixed[h, pl.ds(j, group, stride=FINE), : last - first] = product[
                j * group : (j + 1) * group, first:last
            ]
        table[h * LANES : (h + 1) * LANES] = mixed[h].T.astype(table.dtype)
    lane = lax.broadcasted_iota(jnp.int32, (sources, LANES), 1)
    width = group * LAGS
    tiles = [None] * -(-width // LANES)

    def place(tile, piece, low, high):
        if tiles[tile] is None:
            tiles[tile] = piece
        elif low == 0:
            tiles[tile] = jnp.where(lane < high, piece, tiles[tile])
        else:
            tiles[tile] = jnp.where(lane >= low, piece, tiles[tile])

    for b in range(group):
        column = b * FINE
        for i in range(COARSE):
            piece = table[
                i * sources : (i + 1) * sources,
                column // LANES * LANES : (column // LANES + 1) * LANES,
            ]
            start = b * LAGS + i * FINE
            shift = (start - column) % LANES
            if shift:
                piece = pltpu.roll(piece, shift, 1)
            count = min(FINE, LAGS - i * FINE)
            tile, low = start // LANES, start % LANES
            place(tile, piece, low, LANES)
            if low + count > LANES:
                tiles[tile + 1] = piece
    for tile, value in enumerate(tiles):
        first = tile * LANES
        last = min(first + LANES, width)
        for o in range(offsets):
            rows = value.astype(jnp.float32)[o * SRC : (o + 1) * SRC, : last - first]
            outs[o][:, first:last] = rows.astype(jnp.bfloat16)


def stack_kernel(*refs):
    out_ref = refs[-1]
    for o, ref in enumerate(refs[:-1]):
        out_ref[:, o, :] = ref[...].astype(jnp.float32)


def call(kernel, out_shape, inputs, scratch=(), flops=0):
    single = not isinstance(out_shape, list)
    spec = pl.BlockSpec(memory_space=pltpu.VMEM)
    moved = sum(v.size * v.dtype.itemsize for v in inputs)
    return pl.pallas_call(
        kernel,
        out_shape=out_shape,
        in_specs=[spec] * len(inputs),
        out_specs=spec if single else [spec] * len(out_shape),
        scratch_shapes=list(scratch),
        compiler_params=pltpu.CompilerParams(vmem_limit_bytes=32 * 1024 * 1024),
        cost_estimate=pl.CostEstimate(
            flops=flops, bytes_accessed=moved, transcendentals=0
        ),
    )(*inputs)


def swapped(block, axis, m):
    devices = range(lax.axis_size(axis))
    return lax.ppermute(block, axis, [(k, k ^ m) for k in devices])


def passed_along(block, distance):
    devices = range(lax.axis_size("chan"))
    route = [((i - distance) % len(devices), i) for i in devices]
    return lax.ppermute(block, "chan", route)


def passed_across(block, distance):
    count, places = lax.axis_size("chan"), lax.axis_size("tm")
    route = [
        ((i - distance) % count * places + (k ^ 1), i * places + k)
        for i in range(count)
        for k in range(places)
    ]
    return lax.ppermute(block, ("chan", "tm"), route)


def body(strain_rate):
    channels, length = strain_rate.shape
    shards = lax.axis_size("tm")
    chips = shards // CORES
    reach = lax.axis_size("chan") // 4
    group = channels // shards
    steps = list(range(-reach, 0)) + list(range(1, reach + 1))
    offsets = len(steps)
    sources = offsets * SRC
    scale = 1.0 / math.sqrt(length * shards)
    run = CORES * length
    coded = run + 2 * LANES

    other = swapped(strain_rate, "tm", 1)
    own = call(
        functools.partial(pack_kernel, group, chips),
        jax.ShapeDtypeStruct((chips * group + SRC, length), jnp.float32),
        [strain_rate],
        flops=8 * channels * length,
    )
    own_sources = call(
        functools.partial(code_sources_kernel, group, chips),
        jax.ShapeDtypeStruct((SRC, coded), jnp.bfloat16),
        [own, other],
    )
    arrived = [passed_along(own_sources, d) for d in steps]
    own_receivers = call(
        functools.partial(code_receivers_kernel, group, chips),
        jax.ShapeDtypeStruct((chips * group, coded), jnp.bfloat16),
        [own, other],
        flops=8 * chips * group * run * (256 + 2 * LANES),
    )
    blocks = call(
        functools.partial(join_kernel, offsets),
        [jax.ShapeDtypeStruct((group + sources, coded), jnp.bfloat16)] * chips,
        [own_receivers] + arrived,
    )
    blocks = list(blocks[:1]) + [
        swapped(blocks[m], "tm", CORES * m) for m in range(chips - 1, 0, -1)
    ]
    columns = -(-group * FINE // LANES) * LANES
    heights = -(-COARSE * sources // LANES) * LANES
    kind = jnp.float32 if group % 16 or sources % 16 else jnp.bfloat16
    results = call(
        functools.partial(correlate_kernel, offsets, scale),
        [jax.ShapeDtypeStruct((SRC, group * LAGS), jnp.bfloat16)] * offsets,
        blocks,
        scratch=[
            pltpu.VMEM((chips, group + sources, coded), kind),
            pltpu.VMEM((heights // LANES, columns, LANES), jnp.float32),
            pltpu.VMEM((heights, columns), kind),
        ],
        flops=2 * shards * (length + PAD) * group * FINE * COARSE * sources,
    )
    arrived = [passed_across(r, -d) for r, d in zip(results, steps)]
    return call(
        stack_kernel,
        jax.ShapeDtypeStruct((SRC, offsets, group * LAGS), jnp.float32),
        arrived,
    )


def solution(mesh):
    placed = (P("chan", "tm"),)
    return jax.shard_map(
        body, mesh=mesh, in_specs=placed, out_specs=P("chan", None, "tm"), check_vma=False
    )
```

```python
import functools
import math

import jax
import jax.numpy as jnp
from jax import lax
from jax.experimental import pallas as pl
from jax.experimental.pallas import tpu as pltpu
from jax.sharding import PartitionSpec as P

SRC = 8
MAXLAG = 25
W2 = 64
LAGS = 51
FINE = 4
COARSE = -(-LAGS // FINE)
LANES = 128
PAD = 128
CORES = 2


def band_matrix(rows, columns, related):
    p = lax.broadcasted_iota(jnp.int32, (rows, columns), 0)
    t = lax.broadcasted_iota(jnp.int32, (rows, columns), 1)
    return jnp.where(related(p, t), 1.0, 0.0).astype(jnp.bfloat16)


def halves(values):
    high = values.astype(jnp.bfloat16).astype(jnp.float32)
    return high, values - high


def banded_sums(pieces, band):
    height = pieces[0].shape[0]
    parts = [halves(piece) for piece in pieces]
    stacked = jnp.concatenate([p[0] for p in parts] + [p[1] for p in parts], axis=0)
    sums = jnp.dot(
        stacked.astype(jnp.bfloat16), band, preferred_element_type=jnp.float32
    )
    count = len(pieces)
    return [
        sums[c * height : (c + 1) * height]
        + sums[(count + c) * height : (count + c + 1) * height]
        for c in range(count)
    ]


def level(window_sums):
    return window_sums / (2 * W2 + 1) + 1e-05


def rows_for_here(ref, group, chips):
    me = lax.axis_index("tm")
    every = ref.shape[0] // SRC
    pieces = []
    for m in range(chips):
        start = pl.multiple_of((me ^ (CORES * m + 1)) * group, group)
        pieces.append(ref[pl.ds(start, group)])
    pieces += [ref[q * every : q * every + 1] for q in range(SRC)]
    return jnp.concatenate(pieces, axis=0)


def pack_kernel(group, chips, x_ref, out_ref):
    out_ref[...] = rows_for_here(x_ref, group, chips)


def coded_rows(own, other):
    first_core = lax.rem(lax.axis_index("tm"), CORES) == 0
    x = jnp.concatenate(
        [jnp.where(first_core, own, other), jnp.where(first_core, other, own)], axis=1
    )
    height, length = x.shape
    border = jnp.zeros((height, LANES), jnp.float32)
    magnitude = jnp.concatenate([border, jnp.abs(x), border], axis=1)
    inner = min(256, length)
    band = band_matrix(
        inner + 2 * LANES, inner, lambda p, t: jnp.abs(p - LANES - t) <= W2
    )
    sums = jnp.concatenate(
        banded_sums(
            [
                magnitude[:, start : start + inner + 2 * LANES]
                for start in range(0, length, inner)
            ],
            band,
        ),
        axis=1,
    )
    levels = level(sums)
    normed = x / levels
    left = lax.broadcasted_iota(jnp.int32, (height, LANES), 1) < W2
    tail = length - LANES
    ends = jnp.where(left, normed[:, :LANES], normed[:, tail:])
    end_levels = jnp.where(left, levels[:, :LANES], levels[:, tail:])
    coded = jnp.concatenate([normed, halves(ends)[1], end_levels], axis=1)
    return coded.astype(jnp.bfloat16)


def code_sources_kernel(group, chips, own_ref, other_ref, out_ref):
    first = chips * group
    other = rows_for_here(other_ref, group, chips)
    out_ref[...] = coded_rows(own_ref[first:], other[first:])


def code_receivers_kernel(group, chips, own_ref, other_ref, out_ref):
    last = chips * group
    other = rows_for_here(other_ref, group, chips)
    out_ref[...] = coded_rows(own_ref[:last], other[:last])


def join_kernel(offsets, receivers_ref, *refs):
    given, blocks = refs[:offsets], refs[offsets:]
    group = receivers_ref.shape[0] // len(blocks)
    sources = [ref[...].astype(jnp.float32) for ref in given]
    receivers = receivers_ref[...].astype(jnp.float32)
    for m, block in enumerate(blocks):
        rows = [receivers[m * group : (m + 1) * group]] + sources
        block[...] = jnp.concatenate(rows, axis=0).astype(jnp.bfloat16)


def finished_shards(runs, held):
    chips, height, width = held.shape
    length = width - 2 * LANES
    chip = lax.div(lax.axis_index("tm"), CORES)
    for m in range(chips):
        held[chip ^ m] = runs[m]
    left = lax.broadcasted_iota(jnp.int32, (height, LANES), 1) < W2
    tail = length - LANES
    end_values, end_levels = [], []

    def lanes(c, first):
        return held[c, :, first : first + LANES].astype(jnp.float32)

    for c in range(chips):
        high = jnp.where(left, lanes(c, 0), lanes(c, tail))
        end_values.append(high + lanes(c, length))
        end_levels.append(lanes(c, length + LANES))

    def meeting(ends, outside):
        outside = [jnp.full((height, LANES), outside, jnp.float32)]
        return [
            jnp.where(left, after, before)
            for before, after in zip(outside + ends, ends + outside)
        ]

    def across(p, t):
        at_p, at_t = jnp.where(p < W2, p, p - LANES), jnp.where(t < W2, t, t - LANES)
        return ((p < W2) != (t < W2)) & (jnp.abs(at_p - at_t) <= W2)

    values, levels = meeting(end_values, 0.0), meeting(end_levels, 1.0)
    added = banded_sums(
        [jnp.abs(v) * l for v, l in zip(values, levels)],
        band_matrix(LANES, LANES, across),
    )
    ends = [
        v * l / (l + a / (2 * W2 + 1)) for v, l, a in zip(values, levels, added)
    ]
    shard = length // CORES
    padding = jnp.zeros((height, PAD), held.dtype)
    for k in range(chips * CORES):
        c, part = k // CORES, k % CORES
        pieces = [held[c, :, part * shard : (part + 1) * shard], padding]
        if part == 0:
            head = jnp.where(left, ends[c], lanes(c, 0)).astype(held.dtype)
            pieces = [head, held[c, :, LANES:shard], padding]
        if part == CORES - 1:
            last = jnp.where(left, lanes(c, tail), ends[c + 1]).astype(held.dtype)
            pieces = [held[c, :, part * shard : tail], last, padding]
        yield jnp.concatenate(pieces, axis=1)


def correlate_kernel(offsets, scale, *refs):
    chips = len(refs) - offsets - 3
    blocks, refs = refs[:chips], refs[chips:]
    outs, (held, mixed, table) = refs[:offsets], refs[offsets:]
    sources = offsets * SRC
    group = held.shape[1] - sources
    runs = [ref[...].astype(held.dtype) for ref in blocks[:1] + blocks[:0:-1]]
    product = None
    for wide in finished_shards(runs, held):
        receivers, senders = wide[:group], wide[group:]
        fine = [pltpu.roll(receivers, MAXLAG - j, 1) for j in range(FINE)]
        coarse = [
            pltpu.roll(senders, FINE * i, 1) if i else senders for i in range(COARSE)
        ]
        term = lax.dot_general(
            jnp.concatenate(fine, axis=0).astype(jnp.bfloat16),
            jnp.concatenate(coarse, axis=0).astype(jnp.bfloat16),
            (((1,), (1,)), ((), ())),
            preferred_element_type=jnp.float32,
        )
        product = term if product is None else product + term
    product = product * scale
    for h in range(mixed.shape[0]):
        first, last = h * LANES, min((h + 1) * LANES, COARSE * sources)
        for j in range(FINE):
            mixed[h, pl.ds(j, group, stride=FINE), : last - first] = product[
                j * group : (j + 1) * group, first:last
            ]
        table[h * LANES : (h + 1) * LANES] = mixed[h].T.astype(table.dtype)
    lane = lax.broadcasted_iota(jnp.int32, (sources, LANES), 1)
    width = group * LAGS
    tiles = [None] * -(-width // LANES)

    def place(tile, piece, low, high):
        if tiles[tile] is None:
            tiles[tile] = piece
        elif low == 0:
            tiles[tile] = jnp.where(lane < high, piece, tiles[tile])
        else:
            tiles[tile] = jnp.where(lane >= low, piece, tiles[tile])

    for b in range(group):
        column = b * FINE
        for i in range(COARSE):
            piece = table[
                i * sources : (i + 1) * sources,
                column // LANES * LANES : (column // LANES + 1) * LANES,
            ]
            start = b * LAGS + i * FINE
            shift = (start - column) % LANES
            if shift:
                piece = pltpu.roll(piece, shift, 1)
            count = min(FINE, LAGS - i * FINE)
            tile, low = start // LANES, start % LANES
            place(tile, piece, low, LANES)
            if low + count > LANES:
                tiles[tile + 1] = piece
    for tile, value in enumerate(tiles):
        first = tile * LANES
        last = min(first + LANES, width)
        for o in range(offsets):
            rows = value.astype(jnp.float32)[o * SRC : (o + 1) * SRC, : last - first]
            outs[o][:, first:last] = rows.astype(jnp.bfloat16)


def stack_kernel(*refs):
    out_ref = refs[-1]
    for o, ref in enumerate(refs[:-1]):
        out_ref[:, o, :] = ref[...].astype(jnp.float32)


def call(kernel, out_shape, inputs, scratch=(), flops=0):
    single = not isinstance(out_shape, list)
    spec = pl.BlockSpec(memory_space=pltpu.VMEM)
    moved = sum(v.size * v.dtype.itemsize for v in inputs)
    return pl.pallas_call(
        kernel,
        out_shape=out_shape,
        in_specs=[spec] * len(inputs),
        out_specs=spec if single else [spec] * len(out_shape),
        scratch_shapes=list(scratch),
        compiler_params=pltpu.CompilerParams(vmem_limit_bytes=32 * 1024 * 1024),
        cost_estimate=pl.CostEstimate(
            flops=flops, bytes_accessed=moved, transcendentals=0
        ),
    )(*inputs)


def swapped(block, axis, m):
    devices = range(lax.axis_size(axis))
    return lax.ppermute(block, axis, [(k, k ^ m) for k in devices])


def passed_along(block, distance):
    devices = range(lax.axis_size("chan"))
    route = [((i - distance) % len(devices), i) for i in devices]
    return lax.ppermute(block, "chan", route)


def passed_across(block, distance):
    count, places = lax.axis_size("chan"), lax.axis_size("tm")
    route = [
        ((i - distance) % count * places + (k ^ 1), i * places + k)
        for i in range(count)
        for k in range(places)
    ]
    return lax.ppermute(block, ("chan", "tm"), route)


def body(strain_rate):
    channels, length = strain_rate.shape
    shards = lax.axis_size("tm")
    chips = shards // CORES
    reach = lax.axis_size("chan") // 4
    group = channels // shards
    steps = list(range(-reach, 0)) + list(range(1, reach + 1))
    offsets = len(steps)
    sources = offsets * SRC
    scale = 1.0 / math.sqrt(length * shards)
    run = CORES * length
    coded = run + 2 * LANES

    other = swapped(strain_rate, "tm", 1)
    own = call(
        functools.partial(pack_kernel, group, chips),
        jax.ShapeDtypeStruct((chips * group + SRC, length), jnp.float32),
        [strain_rate],
        flops=8 * channels * length,
    )
    own_sources = call(
        functools.partial(code_sources_kernel, group, chips),
        jax.ShapeDtypeStruct((SRC, coded), jnp.bfloat16),
        [own, other],
    )
    arrived = [passed_along(own_sources, d) for d in steps]
    own_receivers = call(
        functools.partial(code_receivers_kernel, group, chips),
        jax.ShapeDtypeStruct((chips * group, coded), jnp.bfloat16),
        [own, other],
        flops=8 * chips * group * run * (256 + 2 * LANES),
    )
    blocks = call(
        functools.partial(join_kernel, offsets),
        [jax.ShapeDtypeStruct((group + sources, coded), jnp.bfloat16)] * chips,
        [own_receivers] + arrived,
    )
    blocks = list(blocks[:1]) + [
        swapped(blocks[m], "tm", CORES * m) for m in range(chips - 1, 0, -1)
    ]
    columns = -(-group * FINE // LANES) * LANES
    heights = -(-COARSE * sources // LANES) * LANES
    kind = jnp.float32 if group % 16 or sources % 16 else jnp.bfloat16
    results = call(
        functools.partial(correlate_kernel, offsets, scale),
        [jax.ShapeDtypeStruct((SRC, group * LAGS), jnp.bfloat16)] * offsets,
        blocks,
        scratch=[
            pltpu.VMEM((chips, group + sources, coded), kind),
            pltpu.VMEM((heights // LANES, columns, LANES), jnp.float32),
            pltpu.VMEM((heights, columns), kind),
        ],
        flops=2 * shards * (length + PAD) * group * FINE * COARSE * sources,
    )
    arrived = [passed_across(r, -d) for r, d in zip(results, steps)]
    return call(
        stack_kernel,
        jax.ShapeDtypeStruct((SRC, offsets, group * LAGS), jnp.float32),
        arrived,
    )


def solution(mesh):
    placed = (P("chan", "tm"),)
    return jax.shard_map(
        body, mesh=mesh, in_specs=placed, out_specs=P("chan", None, "tm"), check_vma=False
    )
```

```python
import functools
import math

import jax
import jax.numpy as jnp
from jax import lax
from jax.experimental import pallas as pl
from jax.experimental.pallas import tpu as pltpu
from jax.sharding import PartitionSpec as P

SRC = 8
MAXLAG = 25
W2 = 64
LAGS = 51
FINE = 8
COARSE = -(-LAGS // FINE)
LANES = 128
PAD = 128
CORES = 2


def band_matrix(rows, columns, related):
    p = lax.broadcasted_iota(jnp.int32, (rows, columns), 0)
    t = lax.broadcasted_iota(jnp.int32, (rows, columns), 1)
    return jnp.where(related(p, t), 1.0, 0.0).astype(jnp.bfloat16)


def halves(values):
    high = values.astype(jnp.bfloat16).astype(jnp.float32)
    return high, values - high


def banded_sums(pieces, band):
    height = pieces[0].shape[0]
    parts = [halves(piece) for piece in pieces]
    stacked = jnp.concatenate([p[0] for p in parts] + [p[1] for p in parts], axis=0)
    sums = jnp.dot(
        stacked.astype(jnp.bfloat16), band, preferred_element_type=jnp.float32
    )
    count = len(pieces)
    return [
        sums[c * height : (c + 1) * height]
        + sums[(count + c) * height : (count + c + 1) * height]
        for c in range(count)
    ]


def level(window_sums):
    return window_sums / (2 * W2 + 1) + 1e-05


def rows_for_here(ref, group, chips):
    me = lax.axis_index("tm")
    every = ref.shape[0] // SRC
    pieces = []
    for m in range(chips):
        start = pl.multiple_of((me ^ (CORES * m + 1)) * group, group)
        pieces.append(ref[pl.ds(start, group)])
    pieces += [ref[q * every : q * every + 1] for q in range(SRC)]
    return jnp.concatenate(pieces, axis=0)


def pack_kernel(group, chips, x_ref, out_ref):
    out_ref[...] = rows_for_here(x_ref, group, chips)


def coded_rows(own, other):
    first_core = lax.rem(lax.axis_index("tm"), CORES) == 0
    x = jnp.concatenate(
        [jnp.where(first_core, own, other), jnp.where(first_core, other, own)], axis=1
    )
    height, length = x.shape
    border = jnp.zeros((height, LANES), jnp.float32)
    magnitude = jnp.concatenate([border, jnp.abs(x), border], axis=1)
    inner = min(256, length)
    band = band_matrix(
        inner + 2 * LANES, inner, lambda p, t: jnp.abs(p - LANES - t) <= W2
    )
    sums = jnp.concatenate(
        banded_sums(
            [
                magnitude[:, start : start + inner + 2 * LANES]
                for start in range(0, length, inner)
            ],
            band,
        ),
        axis=1,
    )
    levels = level(sums)
    normed = x / levels
    left = lax.broadcasted_iota(jnp.int32, (height, LANES), 1) < W2
    tail = length - LANES
    ends = jnp.where(left, normed[:, :LANES], normed[:, tail:])
    end_levels = jnp.where(left, levels[:, :LANES], levels[:, tail:])
    coded = jnp.concatenate([normed, halves(ends)[1], end_levels], axis=1)
    return coded.astype(jnp.bfloat16)


def code_sources_kernel(group, chips, own_ref, other_ref, out_ref):
    first = chips * group
    other = rows_for_here(other_ref, group, chips)
    out_ref[...] = coded_rows(own_ref[first:], other[first:])


def code_receivers_kernel(group, chips, own_ref, other_ref, out_ref):
    last = chips * group
    other = rows_for_here(other_ref, group, chips)
    out_ref[...] = coded_rows(own_ref[:last], other[:last])


def join_kernel(offsets, receivers_ref, *refs):
    given, blocks = refs[:offsets], refs[offsets:]
    group = receivers_ref.shape[0] // len(blocks)
    sources = [ref[...].astype(jnp.float32) for ref in given]
    receivers = receivers_ref[...].astype(jnp.float32)
    for m, block in enumerate(blocks):
        rows = [receivers[m * group : (m + 1) * group]] + sources
        block[...] = jnp.concatenate(rows, axis=0).astype(jnp.bfloat16)


def finished_shards(runs, held):
    chips, height, width = held.shape
    length = width - 2 * LANES
    chip = lax.div(lax.axis_index("tm"), CORES)
    for m in range(chips):
        held[chip ^ m] = runs[m]
    left = lax.broadcasted_iota(jnp.int32, (height, LANES), 1) < W2
    tail = length - LANES
    end_values, end_levels = [], []

    def lanes(c, first):
        return held[c, :, first : first + LANES].astype(jnp.float32)

    for c in range(chips):
        high = jnp.where(left, lanes(c, 0), lanes(c, tail))
        end_values.append(high + lanes(c, length))
        end_levels.append(lanes(c, length + LANES))

    def meeting(ends, outside):
        outside = [jnp.full((height, LANES), outside, jnp.float32)]
        return [
            jnp.where(left, after, before)
            for before, after in zip(outside + ends, ends + outside)
        ]

    def across(p, t):
        at_p, at_t = jnp.where(p < W2, p, p - LANES), jnp.where(t < W2, t, t - LANES)
        return ((p < W2) != (t < W2)) & (jnp.abs(at_p - at_t) <= W2)

    values, levels = meeting(end_values, 0.0), meeting(end_levels, 1.0)
    added = banded_sums(
        [jnp.abs(v) * l for v, l in zip(values, levels)],
        band_matrix(LANES, LANES, across),
    )
    ends = [
        v * l / (l + a / (2 * W2 + 1)) for v, l, a in zip(values, levels, added)
    ]
    shard = length // CORES
    padding = jnp.zeros((height, PAD), held.dtype)
    for k in range(chips * CORES):
        c, part = k // CORES, k % CORES
        pieces = [held[c, :, part * shard : (part + 1) * shard], padding]
        if part == 0:
            head = jnp.where(left, ends[c], lanes(c, 0)).astype(held.dtype)
            pieces = [head, held[c, :, LANES:shard], padding]
        if part == CORES - 1:
            last = jnp.where(left, lanes(c, tail), ends[c + 1]).astype(held.dtype)
            pieces = [held[c, :, part * shard : tail], last, padding]
        yield jnp.concatenate(pieces, axis=1)


def correlate_kernel(offsets, scale, *refs):
    chips = len(refs) - offsets - 3
    blocks, refs = refs[:chips], refs[chips:]
    outs, (held, mixed, table) = refs[:offsets], refs[offsets:]
    sources = offsets * SRC
    group = held.shape[1] - sources
    runs = [ref[...].astype(held.dtype) for ref in blocks[:1] + blocks[:0:-1]]
    product = None
    for wide in finished_shards(runs, held):
        receivers, senders = wide[:group], wide[group:]
        fine = [pltpu.roll(receivers, MAXLAG - j, 1) for j in range(FINE)]
        coarse = [
            pltpu.roll(senders, FINE * i, 1) if i else senders for i in range(COARSE)
        ]
        term = lax.dot_general(
            jnp.concatenate(fine, axis=0).astype(jnp.bfloat16),
            jnp.concatenate(coarse, axis=0).astype(jnp.bfloat16),
            (((1,), (1,)), ((), ())),
            preferred_element_type=jnp.float32,
        )
        product = term if product is None else product + term
    product = product * scale
    for h in range(mixed.shape[0]):
        first, last = h * LANES, min((h + 1) * LANES, COARSE * sources)
        for j in range(FINE):
            mixed[h, pl.ds(j, group, stride=FINE), : last - first] = product[
                j * group : (j + 1) * group, first:last
            ]
        table[h * LANES : (h + 1) * LANES] = mixed[h].T.astype(table.dtype)
    lane = lax.broadcasted_iota(jnp.int32, (sources, LANES), 1).astype(table.dtype)
    width = group * LAGS
    tiles = [None] * -(-width // LANES)

    def place(tile, piece, low):
        if low and tiles[tile] is not None:
            piece = jnp.where(lane >= low, piece, tiles[tile])
        tiles[tile] = piece

    for b in range(group):
        column = b * FINE
        for i in range(COARSE):
            piece = table[
                i * sources : (i + 1) * sources,
                column // LANES * LANES : (column // LANES + 1) * LANES,
            ]
            start = b * LAGS + i * FINE
            shift = (start - column) % LANES
            if shift:
                piece = pltpu.roll(piece, shift, 1)
            count = min(FINE, LAGS - i * FINE)
            tile, low = start // LANES, start % LANES
            place(tile, piece, low)
            if low + count > LANES:
                tiles[tile + 1] = piece
    for tile, value in enumerate(tiles):
        first = tile * LANES
        last = min(first + LANES, width)
        for o in range(offsets):
            rows = value.astype(jnp.float32)[o * SRC : (o + 1) * SRC, : last - first]
            outs[o][:, first:last] = rows.astype(jnp.bfloat16)


def stack_kernel(*refs):
    out_ref = refs[-1]
    for o, ref in enumerate(refs[:-1]):
        out_ref[:, o, :] = ref[...].astype(jnp.float32)


def call(kernel, out_shape, inputs, scratch=(), flops=0):
    single = not isinstance(out_shape, list)
    spec = pl.BlockSpec(memory_space=pltpu.VMEM)
    moved = sum(v.size * v.dtype.itemsize for v in inputs)
    return pl.pallas_call(
        kernel,
        out_shape=out_shape,
        in_specs=[spec] * len(inputs),
        out_specs=spec if single else [spec] * len(out_shape),
        scratch_shapes=list(scratch),
        compiler_params=pltpu.CompilerParams(vmem_limit_bytes=32 * 1024 * 1024),
        cost_estimate=pl.CostEstimate(
            flops=flops, bytes_accessed=moved, transcendentals=0
        ),
    )(*inputs)


def swapped(block, axis, m):
    devices = range(lax.axis_size(axis))
    return lax.ppermute(block, axis, [(k, k ^ m) for k in devices])


def passed_along(block, distance):
    devices = range(lax.axis_size("chan"))
    route = [((i - distance) % len(devices), i) for i in devices]
    return lax.ppermute(block, "chan", route)


def passed_across(block, distance):
    count, places = lax.axis_size("chan"), lax.axis_size("tm")
    route = [
        ((i - distance) % count * places + (k ^ 1), i * places + k)
        for i in range(count)
        for k in range(places)
    ]
    return lax.ppermute(block, ("chan", "tm"), route)


def body(strain_rate):
    channels, length = strain_rate.shape
    shards = lax.axis_size("tm")
    chips = shards // CORES
    reach = lax.axis_size("chan") // 4
    group = channels // shards
    steps = list(range(-reach, 0)) + list(range(1, reach + 1))
    offsets = len(steps)
    sources = offsets * SRC
    scale = 1.0 / math.sqrt(length * shards)
    run = CORES * length
    coded = run + 2 * LANES

    other = swapped(strain_rate, "tm", 1)
    own = call(
        functools.partial(pack_kernel, group, chips),
        jax.ShapeDtypeStruct((chips * group + SRC, length), jnp.float32),
        [strain_rate],
        flops=8 * channels * length,
    )
    own_sources = call(
        functools.partial(code_sources_kernel, group, chips),
        jax.ShapeDtypeStruct((SRC, coded), jnp.bfloat16),
        [own, other],
    )
    arrived = [passed_along(own_sources, d) for d in steps]
    own_receivers = call(
        functools.partial(code_receivers_kernel, group, chips),
        jax.ShapeDtypeStruct((chips * group, coded), jnp.bfloat16),
        [own, other],
        flops=8 * chips * group * run * (256 + 2 * LANES),
    )
    blocks = call(
        functools.partial(join_kernel, offsets),
        [jax.ShapeDtypeStruct((group + sources, coded), jnp.bfloat16)] * chips,
        [own_receivers] + arrived,
    )
    blocks = list(blocks[:1]) + [
        swapped(blocks[m], "tm", CORES * m) for m in range(chips - 1, 0, -1)
    ]
    columns = -(-group * FINE // LANES) * LANES
    heights = -(-COARSE * sources // LANES) * LANES
    kind = jnp.float32 if group % 16 or sources % 16 else jnp.bfloat16
    results = call(
        functools.partial(correlate_kernel, offsets, scale),
        [jax.ShapeDtypeStruct((SRC, group * LAGS), jnp.bfloat16)] * offsets,
        blocks,
        scratch=[
            pltpu.VMEM((chips, group + sources, coded), kind),
            pltpu.VMEM((heights // LANES, columns, LANES), jnp.float32),
            pltpu.VMEM((heights, columns), kind),
        ],
        flops=2 * shards * (length + PAD) * group * FINE * COARSE * sources,
    )
    arrived = [passed_across(r, -d) for r, d in zip(results, steps)]
    return call(
        stack_kernel,
        jax.ShapeDtypeStruct((SRC, offsets, group * LAGS), jnp.float32),
        arrived,
    )


def solution(mesh):
    placed = (P("chan", "tm"),)
    return jax.shard_map(
        body, mesh=mesh, in_specs=placed, out_specs=P("chan", None, "tm"), check_vma=False
    )
```

```python
import functools
import math

import jax
import jax.numpy as jnp
from jax import lax
from jax.experimental import pallas as pl
from jax.experimental.pallas import tpu as pltpu
from jax.sharding import PartitionSpec as P

SRC = 8
MAXLAG = 25
W2 = 64
LAGS = 51
FINE = 8
COARSE = -(-LAGS // FINE)
LANES = 128
CORES = 2


def band_matrix(rows, columns, related):
    p = lax.broadcasted_iota(jnp.int32, (rows, columns), 0)
    t = lax.broadcasted_iota(jnp.int32, (rows, columns), 1)
    return jnp.where(related(p, t), 1.0, 0.0).astype(jnp.bfloat16)


def halves(values):
    high = values.astype(jnp.bfloat16).astype(jnp.float32)
    return high, values - high


def banded_sums(pieces, band):
    height = pieces[0].shape[0]
    parts = [halves(piece) for piece in pieces]
    stacked = jnp.concatenate([p[0] for p in parts] + [p[1] for p in parts], axis=0)
    sums = jnp.dot(
        stacked.astype(jnp.bfloat16), band, preferred_element_type=jnp.float32
    )
    count = len(pieces)
    return [
        sums[c * height : (c + 1) * height]
        + sums[(count + c) * height : (count + c + 1) * height]
        for c in range(count)
    ]


def level(window_sums):
    return window_sums / (2 * W2 + 1) + 1e-05


def rows_for_here(ref, group, chips):
    me = lax.axis_index("tm")
    every = ref.shape[0] // SRC
    pieces = []
    for m in range(chips):
        start = pl.multiple_of((me ^ (CORES * m + 1)) * group, group)
        pieces.append(ref[pl.ds(start, group)])
    pieces += [ref[q * every : q * every + 1] for q in range(SRC)]
    return jnp.concatenate(pieces, axis=0)


def pack_kernel(group, chips, x_ref, out_ref):
    out_ref[...] = rows_for_here(x_ref, group, chips)


def coded_rows(own, other):
    first_core = lax.rem(lax.axis_index("tm"), CORES) == 0
    x = jnp.concatenate(
        [jnp.where(first_core, own, other), jnp.where(first_core, other, own)], axis=1
    )
    height, length = x.shape
    border = jnp.zeros((height, LANES), jnp.float32)
    magnitude = jnp.concatenate([border, jnp.abs(x), border], axis=1)
    inner = min(256, length)
    band = band_matrix(
        inner + 2 * LANES, inner, lambda p, t: jnp.abs(p - LANES - t) <= W2
    )
    sums = jnp.concatenate(
        banded_sums(
            [
                magnitude[:, start : start + inner + 2 * LANES]
                for start in range(0, length, inner)
            ],
            band,
        ),
        axis=1,
    )
    levels = level(sums)
    normed = x / levels
    left = lax.broadcasted_iota(jnp.int32, (height, LANES), 1) < W2
    tail = length - LANES
    ends = jnp.where(left, normed[:, :LANES], normed[:, tail:])
    end_levels = jnp.where(left, levels[:, :LANES], levels[:, tail:])
    coded = jnp.concatenate([normed, halves(ends)[1], end_levels], axis=1)
    return coded.astype(jnp.bfloat16)


def code_sources_kernel(group, chips, own_ref, other_ref, out_ref):
    first = chips * group
    other = rows_for_here(other_ref, group, chips)
    out_ref[...] = coded_rows(own_ref[first:], other[first:])


def code_receivers_kernel(group, chips, own_ref, other_ref, out_ref):
    last = chips * group
    other = rows_for_here(other_ref, group, chips)
    out_ref[...] = coded_rows(own_ref[:last], other[:last])


def join_kernel(offsets, receivers_ref, *refs):
    given, blocks = refs[:offsets], refs[offsets:]
    group = receivers_ref.shape[0] // len(blocks)
    sources = [ref[...].astype(jnp.float32) for ref in given]
    receivers = receivers_ref[...].astype(jnp.float32)
    for m, block in enumerate(blocks):
        rows = [receivers[m * group : (m + 1) * group]] + sources
        block[...] = jnp.concatenate(rows, axis=0).astype(jnp.bfloat16)


def finished_shards(runs, held):
    chips, height, width = held.shape
    length = width - 2 * LANES
    chip = lax.div(lax.axis_index("tm"), CORES)
    for m in range(chips):
        held[chip ^ m] = runs[m]
    left = lax.broadcasted_iota(jnp.int32, (height, LANES), 1) < W2
    tail = length - LANES
    end_values, end_levels = [], []

    def lanes(c, first):
        return held[c, :, first : first + LANES].astype(jnp.float32)

    for c in range(chips):
        high = jnp.where(left, lanes(c, 0), lanes(c, tail))
        end_values.append(high + lanes(c, length))
        end_levels.append(lanes(c, length + LANES))

    def meeting(ends, outside):
        outside = [jnp.full((height, LANES), outside, jnp.float32)]
        return [
            jnp.where(left, after, before)
            for before, after in zip(outside + ends, ends + outside)
        ]

    def across(p, t):
        at_p, at_t = jnp.where(p < W2, p, p - LANES), jnp.where(t < W2, t, t - LANES)
        return ((p < W2) != (t < W2)) & (jnp.abs(at_p - at_t) <= W2)

    values, levels = meeting(end_values, 0.0), meeting(end_levels, 1.0)
    added = banded_sums(
        [jnp.abs(v) * l for v, l in zip(values, levels)],
        band_matrix(LANES, LANES, across),
    )
    ends = [
        v * l / (l + a / (2 * W2 + 1)) for v, l, a in zip(values, levels, added)
    ]
    shard = length // CORES
    for k in range(chips * CORES):
        c, part = k // CORES, k % CORES
        pieces = [held[c, :, part * shard : (part + 1) * shard]]
        if part == 0:
            head = jnp.where(left, ends[c], lanes(c, 0)).astype(held.dtype)
            pieces = [head, held[c, :, LANES:shard]]
        if part == CORES - 1:
            last = jnp.where(left, lanes(c, tail), ends[c + 1]).astype(held.dtype)
            pieces = [held[c, :, part * shard : tail], last]
        yield jnp.concatenate(pieces, axis=1)


def lane_numbers(rows, dtype):
    return lax.broadcasted_iota(jnp.int32, (rows, LANES), 1).astype(dtype)


def shifted(rows, shift):
    height, length = rows.shape
    nothing = jnp.zeros((height, LANES), rows.dtype)
    if not shift:
        return jnp.concatenate([rows, nothing], axis=1)
    turned = [
        pltpu.roll(rows[:, first : first + LANES], shift, 1)
        for first in range(0, length, LANES)
    ]
    behind = lane_numbers(height, rows.dtype) >= shift
    return jnp.concatenate(
        [
            jnp.where(behind, here, before)
            for before, here in zip([nothing] + turned, turned + [nothing])
        ],
        axis=1,
    )


def correlate_kernel(offsets, scale, *refs):
    chips = len(refs) - offsets - 3
    blocks, refs = refs[:chips], refs[chips:]
    outs, (held, mixed, table) = refs[:offsets], refs[offsets:]
    sources = offsets * SRC
    group = held.shape[1] - sources
    runs = [ref[...].astype(held.dtype) for ref in blocks[:1] + blocks[:0:-1]]
    product = None
    for wide in finished_shards(runs, held):
        receivers, senders = wide[:group], wide[group:]
        fine = [shifted(receivers, MAXLAG - j) for j in range(FINE)]
        coarse = [shifted(senders, FINE * i) for i in range(COARSE)]
        term = lax.dot_general(
            jnp.concatenate(fine, axis=0).astype(jnp.bfloat16),
            jnp.concatenate(coarse, axis=0).astype(jnp.bfloat16),
            (((1,), (1,)), ((), ())),
            preferred_element_type=jnp.float32,
        )
        product = term if product is None else product + term
    product = product * scale
    for h in range(mixed.shape[0]):
        first, last = h * LANES, min((h + 1) * LANES, COARSE * sources)
        for j in range(FINE):
            mixed[h, pl.ds(j, group, stride=FINE), : last - first] = product[
                j * group : (j + 1) * group, first:last
            ]
        table[h * LANES : (h + 1) * LANES] = mixed[h].T.astype(table.dtype)
    columns = table.shape[1]
    turned = []
    for i in range(COARSE):
        block = table[i * sources : (i + 1) * sources]
        turned.append(pltpu.roll(block, FINE * i, 1) if i else block)
    lane = lane_numbers(sources, table.dtype)
    width = group * LAGS

    def place(tiles, tile, piece, low):
        if low and tile in tiles:
            piece = jnp.where(lane >= low, piece, tiles[tile])
        tiles[tile] = piece

    tiles = {}
    for b in range(group):
        joined = {}
        for i in range(COARSE):
            tile, low = divmod((b + i) * FINE % columns, LANES)
            piece = turned[i][:, tile * LANES : (tile + 1) * LANES]
            place(joined, tile, piece, low)
        turn = b * (LAGS - FINE) % LANES
        if turn:
            joined = {tile: pltpu.roll(v, turn, 1) for tile, v in joined.items()}
        for lag in range(LAGS):
            at, to = (b * FINE + lag) % columns, b * LAGS + lag
            if lag == 0 or at % LANES == 0 or to % LANES == 0:
                place(tiles, to // LANES, joined[at // LANES], to % LANES)
    for tile, value in tiles.items():
        first = tile * LANES
        last = min(first + LANES, width)
        for o in range(offsets):
            rows = value.astype(jnp.float32)[o * SRC : (o + 1) * SRC, : last - first]
            outs[o][:, first:last] = rows.astype(jnp.bfloat16)


def stack_kernel(*refs):
    out_ref = refs[-1]
    for o, ref in enumerate(refs[:-1]):
        out_ref[:, o, :] = ref[...].astype(jnp.float32)


def call(kernel, out_shape, inputs, scratch=(), flops=0):
    single = not isinstance(out_shape, list)
    spec = pl.BlockSpec(memory_space=pltpu.VMEM)
    moved = sum(v.size * v.dtype.itemsize for v in inputs)
    return pl.pallas_call(
        kernel,
        out_shape=out_shape,
        in_specs=[spec] * len(inputs),
        out_specs=spec if single else [spec] * len(out_shape),
        scratch_shapes=list(scratch),
        compiler_params=pltpu.CompilerParams(vmem_limit_bytes=32 * 1024 * 1024),
        cost_estimate=pl.CostEstimate(
            flops=flops, bytes_accessed=moved, transcendentals=0
        ),
    )(*inputs)


def swapped(block, axis, m):
    devices = range(lax.axis_size(axis))
    return lax.ppermute(block, axis, [(k, k ^ m) for k in devices])


def passed_along(block, distance):
    devices = range(lax.axis_size("chan"))
    route = [((i - distance) % len(devices), i) for i in devices]
    return lax.ppermute(block, "chan", route)


def passed_across(block, distance):
    count, places = lax.axis_size("chan"), lax.axis_size("tm")
    route = [
        ((i - distance) % count * places + (k ^ 1), i * places + k)
        for i in range(count)
        for k in range(places)
    ]
    return lax.ppermute(block, ("chan", "tm"), route)


def body(strain_rate):
    channels, length = strain_rate.shape
    shards = lax.axis_size("tm")
    chips = shards // CORES
    reach = lax.axis_size("chan") // 4
    group = channels // shards
    steps = list(range(-reach, 0)) + list(range(1, reach + 1))
    offsets = len(steps)
    sources = offsets * SRC
    scale = 1.0 / math.sqrt(length * shards)
    run = CORES * length
    coded = run + 2 * LANES

    other = swapped(strain_rate, "tm", 1)
    own = call(
        functools.partial(pack_kernel, group, chips),
        jax.ShapeDtypeStruct((chips * group + SRC, length), jnp.float32),
        [strain_rate],
        flops=8 * channels * length,
    )
    own_sources = call(
        functools.partial(code_sources_kernel, group, chips),
        jax.ShapeDtypeStruct((SRC, coded), jnp.bfloat16),
        [own, other],
    )
    arrived = [passed_along(own_sources, d) for d in steps]
    own_receivers = call(
        functools.partial(code_receivers_kernel, group, chips),
        jax.ShapeDtypeStruct((chips * group, coded), jnp.bfloat16),
        [own, other],
        flops=8 * chips * group * run * (256 + 2 * LANES),
    )
    blocks = call(
        functools.partial(join_kernel, offsets),
        [jax.ShapeDtypeStruct((group + sources, coded), jnp.bfloat16)] * chips,
        [own_receivers] + arrived,
    )
    blocks = list(blocks[:1]) + [
        swapped(blocks[m], "tm", CORES * m) for m in range(chips - 1, 0, -1)
    ]
    columns = -(-group * FINE // LANES) * LANES
    heights = -(-COARSE * sources // LANES) * LANES
    kind = jnp.float32 if group % 16 or sources % 16 else jnp.bfloat16
    results = call(
        functools.partial(correlate_kernel, offsets, scale),
        [jax.ShapeDtypeStruct((SRC, group * LAGS), jnp.bfloat16)] * offsets,
        blocks,
        scratch=[
            pltpu.VMEM((chips, group + sources, coded), kind),
            pltpu.VMEM((heights // LANES, columns, LANES), jnp.float32),
            pltpu.VMEM((heights, columns), kind),
        ],
        flops=2 * shards * (length + LANES) * group * FINE * COARSE * sources,
    )
    arrived = [passed_across(r, -d) for r, d in zip(results, steps)]
    return call(
        stack_kernel,
        jax.ShapeDtypeStruct((SRC, offsets, group * LAGS), jnp.float32),
        arrived,
    )


def solution(mesh):
    placed = (P("chan", "tm"),)
    return jax.shard_map(
        body, mesh=mesh, in_specs=placed, out_specs=P("chan", None, "tm"), check_vma=False
    )
```

```python
import functools
import math

import jax
import jax.numpy as jnp
from jax import lax
from jax.experimental import pallas as pl
from jax.experimental.pallas import tpu as pltpu
from jax.sharding import PartitionSpec as P

SRC = 8
MAXLAG = 25
W2 = 64
LAGS = 51
FINE = 8
COARSE = -(-LAGS // FINE)
LANES = 128
CORES = 2


def band_matrix(rows, columns, related):
    p = lax.broadcasted_iota(jnp.int32, (rows, columns), 0)
    t = lax.broadcasted_iota(jnp.int32, (rows, columns), 1)
    return jnp.where(related(p, t), 1.0, 0.0).astype(jnp.bfloat16)


def halves(values):
    high = values.astype(jnp.bfloat16).astype(jnp.float32)
    return high, values - high


def banded_sums(pieces, band):
    height = pieces[0].shape[0]
    parts = [halves(piece) for piece in pieces]
    stacked = jnp.concatenate([p[0] for p in parts] + [p[1] for p in parts], axis=0)
    sums = jnp.dot(
        stacked.astype(jnp.bfloat16), band, preferred_element_type=jnp.float32
    )
    count = len(pieces)
    return [
        sums[c * height : (c + 1) * height]
        + sums[(count + c) * height : (count + c + 1) * height]
        for c in range(count)
    ]


def level(window_sums):
    return window_sums / (2 * W2 + 1) + 1e-05


def rows_for_here(ref, group, chips):
    me = lax.axis_index("tm")
    every = ref.shape[0] // SRC
    pieces = []
    for m in range(chips):
        start = pl.multiple_of((me ^ (CORES * m + 1)) * group, group)
        pieces.append(ref[pl.ds(start, group)])
    pieces += [ref[q * every : q * every + 1] for q in range(SRC)]
    return jnp.concatenate(pieces, axis=0)


def pack_kernel(group, chips, x_ref, out_ref):
    out_ref[...] = rows_for_here(x_ref, group, chips)


def coded_rows(own, other, exact):
    first_core = lax.rem(lax.axis_index("tm"), CORES) == 0
    x = jnp.concatenate(
        [jnp.where(first_core, own, other), jnp.where(first_core, other, own)], axis=1
    )
    height, length = x.shape
    border = jnp.zeros((height, LANES), jnp.float32)
    magnitude = jnp.concatenate([border, jnp.abs(x), border], axis=1)
    inner = min(256, length)
    band = band_matrix(
        inner + 2 * LANES, inner, lambda p, t: jnp.abs(p - LANES - t) <= W2
    )
    sums = jnp.concatenate(
        banded_sums(
            [
                magnitude[:, start : start + inner + 2 * LANES]
                for start in range(0, length, inner)
            ],
            band,
        ),
        axis=1,
    )
    levels = level(sums)
    normed = x / levels
    left = lax.broadcasted_iota(jnp.int32, (height, LANES), 1) < W2
    tail = length - LANES
    ends = jnp.where(left, normed[:, :LANES], normed[:, tail:])
    end_levels = jnp.where(left, levels[:, :LANES], levels[:, tail:])
    errors = [halves(ends)[1]] if exact else []
    coded = jnp.concatenate([normed, end_levels] + errors, axis=1)
    return coded.astype(jnp.bfloat16)


def code_sources_kernel(group, chips, own_ref, other_ref, out_ref):
    first = chips * group
    other = rows_for_here(other_ref, group, chips)
    out_ref[...] = coded_rows(own_ref[first:], other[first:], True)


def code_receivers_kernel(group, chips, own_ref, other_ref, out_ref):
    last = chips * group
    other = rows_for_here(other_ref, group, chips)
    out_ref[...] = coded_rows(own_ref[:last], other[:last], False)


def join_kernel(offsets, receivers_ref, *refs):
    given, blocks = refs[:offsets], refs[offsets:]
    group = receivers_ref.shape[0] // len(blocks)
    sources = [ref[...].astype(jnp.float32) for ref in given]
    receivers = receivers_ref[...].astype(jnp.float32)
    sources = jnp.concatenate(sources, axis=0)
    width = receivers.shape[1]
    for m, block in enumerate(blocks):
        rows = jnp.concatenate(
            [receivers[m * group : (m + 1) * group], sources[:, :width]], axis=0
        )
        pieces = [rows[:, first : first + LANES] for first in range(0, width, LANES)]
        pieces.append(sources[:, width:])
        block[...] = jnp.concatenate(pieces, axis=0).astype(jnp.bfloat16)


def finished_shards(runs, held, sources, tiles):
    chips, depth, _ = held.shape
    height = (depth - sources) // (tiles + 1)
    chip = lax.div(lax.axis_index("tm"), CORES)
    for m in range(chips):
        held[chip ^ m] = runs[m]
    left = lax.broadcasted_iota(jnp.int32, (height, LANES), 1) < W2

    def tile(c, t):
        return held[c, t * height : (t + 1) * height]

    end_values, end_levels = [], []
    for c in range(chips):
        high = jnp.where(
            left, tile(c, 0).astype(jnp.float32), tile(c, tiles - 1).astype(jnp.float32)
        )
        errors = held[c, (tiles + 1) * height :].astype(jnp.float32)
        first = height - sources
        end_values.append(
            jnp.concatenate([high[:first], high[first:] + errors], axis=0)
        )
        end_levels.append(tile(c, tiles).astype(jnp.float32))

    def meeting(ends, outside):
        outside = [jnp.full((height, LANES), outside, jnp.float32)]
        return [
            jnp.where(left, after, before)
            for before, after in zip(outside + ends, ends + outside)
        ]

    def across(p, t):
        at_p, at_t = jnp.where(p < W2, p, p - LANES), jnp.where(t < W2, t, t - LANES)
        return ((p < W2) != (t < W2)) & (jnp.abs(at_p - at_t) <= W2)

    values, levels = meeting(end_values, 0.0), meeting(end_levels, 1.0)
    added = banded_sums(
        [jnp.abs(v) * l for v, l in zip(values, levels)],
        band_matrix(LANES, LANES, across),
    )
    ends = [
        v * l / (l + a / (2 * W2 + 1)) for v, l, a in zip(values, levels, added)
    ]
    for c in range(chips):
        row = [tile(c, t) for t in range(tiles)]
        head = jnp.where(left, ends[c], row[0].astype(jnp.float32))
        last = jnp.where(left, row[-1].astype(jnp.float32), ends[c + 1])
        row = [head.astype(held.dtype)] + row[1:-1] + [last.astype(held.dtype)]
        shard = tiles // CORES
        for first in range(0, tiles, shard):
            yield jnp.concatenate(row[first : first + shard], axis=1)


def lane_numbers(rows, dtype):
    return lax.broadcasted_iota(jnp.int32, (rows, LANES), 1).astype(dtype)


def shifted(rows, shift):
    height, length = rows.shape
    nothing = jnp.zeros((height, LANES), rows.dtype)
    if not shift:
        return jnp.concatenate([rows, nothing], axis=1)
    turned = [
        pltpu.roll(rows[:, first : first + LANES], shift, 1)
        for first in range(0, length, LANES)
    ]
    behind = lane_numbers(height, rows.dtype) >= shift
    return jnp.concatenate(
        [
            jnp.where(behind, here, before)
            for before, here in zip([nothing] + turned, turned + [nothing])
        ],
        axis=1,
    )


def correlate_kernel(offsets, group, tiles, scale, *refs):
    chips = len(refs) - offsets - 3
    blocks, refs = refs[:chips], refs[chips:]
    outs, (held, mixed, table) = refs[:offsets], refs[offsets:]
    sources = offsets * SRC
    runs = [ref[...].astype(held.dtype) for ref in blocks[:1] + blocks[:0:-1]]
    product = None
    for wide in finished_shards(runs, held, sources, tiles):
        receivers, senders = wide[:group], wide[group:]
        fine = [shifted(receivers, MAXLAG - j) for j in range(FINE)]
        coarse = [shifted(senders, FINE * i) for i in range(COARSE)]
        term = lax.dot_general(
            jnp.concatenate(fine, axis=0).astype(jnp.bfloat16),
            jnp.concatenate(coarse, axis=0).astype(jnp.bfloat16),
            (((1,), (1,)), ((), ())),
            preferred_element_type=jnp.float32,
        )
        product = term if product is None else product + term
    product = product * scale
    for h in range(mixed.shape[0]):
        first, last = h * LANES, min((h + 1) * LANES, COARSE * sources)
        for j in range(FINE):
            mixed[h, pl.ds(j, group, stride=FINE), : last - first] = product[
                j * group : (j + 1) * group, first:last
            ]
        table[h * LANES : (h + 1) * LANES] = mixed[h].T.astype(table.dtype)
    columns = table.shape[1]
    turned = []
    for i in range(COARSE):
        block = table[i * sources : (i + 1) * sources]
        turned.append(pltpu.roll(block, FINE * i, 1) if i else block)
    lane = lane_numbers(sources, table.dtype)
    width = group * LAGS

    def place(tiles, tile, piece, low):
        if low and tile in tiles:
            piece = jnp.where(lane >= low, piece, tiles[tile])
        tiles[tile] = piece

    tiles = {}
    for b in range(group):
        joined = {}
        for i in range(COARSE):
            tile, low = divmod((b + i) * FINE % columns, LANES)
            piece = turned[i][:, tile * LANES : (tile + 1) * LANES]
            place(joined, tile, piece, low)
        turn = b * (LAGS - FINE) % LANES
        if turn:
            joined = {tile: pltpu.roll(v, turn, 1) for tile, v in joined.items()}
        for lag in range(LAGS):
            at, to = (b * FINE + lag) % columns, b * LAGS + lag
            if lag == 0 or at % LANES == 0 or to % LANES == 0:
                place(tiles, to // LANES, joined[at // LANES], to % LANES)
    for tile, value in tiles.items():
        first = tile * LANES
        last = min(first + LANES, width)
        for o in range(offsets):
            rows = value.astype(jnp.float32)[o * SRC : (o + 1) * SRC, : last - first]
            outs[o][:, first:last] = rows.astype(jnp.bfloat16)


def stack_kernel(*refs):
    out_ref = refs[-1]
    for o, ref in enumerate(refs[:-1]):
        out_ref[:, o, :] = ref[...].astype(jnp.float32)


def call(kernel, out_shape, inputs, scratch=(), flops=0):
    single = not isinstance(out_shape, list)
    spec = pl.BlockSpec(memory_space=pltpu.VMEM)
    moved = sum(v.size * v.dtype.itemsize for v in inputs)
    return pl.pallas_call(
        kernel,
        out_shape=out_shape,
        in_specs=[spec] * len(inputs),
        out_specs=spec if single else [spec] * len(out_shape),
        scratch_shapes=list(scratch),
        compiler_params=pltpu.CompilerParams(vmem_limit_bytes=32 * 1024 * 1024),
        cost_estimate=pl.CostEstimate(
            flops=flops, bytes_accessed=moved, transcendentals=0
        ),
    )(*inputs)


def swapped(block, axis, m):
    devices = range(lax.axis_size(axis))
    return lax.ppermute(block, axis, [(k, k ^ m) for k in devices])


def passed_along(block, distance):
    devices = range(lax.axis_size("chan"))
    route = [((i - distance) % len(devices), i) for i in devices]
    return lax.ppermute(block, "chan", route)


def passed_across(block, distance):
    count, places = lax.axis_size("chan"), lax.axis_size("tm")
    route = [
        ((i - distance) % count * places + (k ^ 1), i * places + k)
        for i in range(count)
        for k in range(places)
    ]
    return lax.ppermute(block, ("chan", "tm"), route)


def body(strain_rate):
    channels, length = strain_rate.shape
    shards = lax.axis_size("tm")
    chips = shards // CORES
    reach = lax.axis_size("chan") // 4
    group = channels // shards
    steps = list(range(-reach, 0)) + list(range(1, reach + 1))
    offsets = len(steps)
    sources = offsets * SRC
    scale = 1.0 / math.sqrt(length * shards)
    run = CORES * length
    tiles = run // LANES
    depth = (group + sources) * (tiles + 1) + sources

    other = swapped(strain_rate, "tm", 1)
    own = call(
        functools.partial(pack_kernel, group, chips),
        jax.ShapeDtypeStruct((chips * group + SRC, length), jnp.float32),
        [strain_rate],
        flops=8 * channels * length,
    )
    own_sources = call(
        functools.partial(code_sources_kernel, group, chips),
        jax.ShapeDtypeStruct((SRC, run + 2 * LANES), jnp.bfloat16),
        [own, other],
    )
    arrived = [passed_along(own_sources, d) for d in steps]
    own_receivers = call(
        functools.partial(code_receivers_kernel, group, chips),
        jax.ShapeDtypeStruct((chips * group, run + LANES), jnp.bfloat16),
        [own, other],
        flops=8 * chips * group * run * (256 + 2 * LANES),
    )
    blocks = call(
        functools.partial(join_kernel, offsets),
        [jax.ShapeDtypeStruct((depth, LANES), jnp.bfloat16)] * chips,
        [own_receivers] + arrived,
    )
    blocks = list(blocks[:1]) + [
        swapped(blocks[m], "tm", CORES * m) for m in range(chips - 1, 0, -1)
    ]
    columns = -(-group * FINE // LANES) * LANES
    heights = -(-COARSE * sources // LANES) * LANES
    kind = jnp.float32 if group % 16 or sources % 16 else jnp.bfloat16
    results = call(
        functools.partial(correlate_kernel, offsets, group, tiles, scale),
        [jax.ShapeDtypeStruct((SRC, group * LAGS), jnp.bfloat16)] * offsets,
        blocks,
        scratch=[
            pltpu.VMEM((chips, depth, LANES), kind),
            pltpu.VMEM((heights // LANES, columns, LANES), jnp.float32),
            pltpu.VMEM((heights, columns), kind),
        ],
        flops=2 * shards * (length + LANES) * group * FINE * COARSE * sources,
    )
    arrived = [passed_across(r, -d) for r, d in zip(results, steps)]
    return call(
        stack_kernel,
        jax.ShapeDtypeStruct((SRC, offsets, group * LAGS), jnp.float32),
        arrived,
    )


def solution(mesh):
    placed = (P("chan", "tm"),)
    return jax.shard_map(
        body, mesh=mesh, in_specs=placed, out_specs=P("chan", None, "tm"), check_vma=False
    )
```

```python
import functools
import math

import jax
import jax.numpy as jnp
from jax import lax
from jax.experimental import pallas as pl
from jax.experimental.pallas import tpu as pltpu
from jax.sharding import PartitionSpec as P

SRC = 8
MAXLAG = 25
W2 = 64
LAGS = 51
FINE = 8
COARSE = -(-LAGS // FINE)
LANES = 128
CORES = 2


def band_matrix(rows, columns, related):
    p = lax.broadcasted_iota(jnp.int32, (rows, columns), 0)
    t = lax.broadcasted_iota(jnp.int32, (rows, columns), 1)
    return jnp.where(related(p, t), 1.0, 0.0).astype(jnp.bfloat16)


def halves(values):
    high = values.astype(jnp.bfloat16).astype(jnp.float32)
    return high, values - high


def banded_sums(pieces, band):
    height = pieces[0].shape[0]
    parts = [halves(piece) for piece in pieces]
    stacked = jnp.concatenate([p[0] for p in parts] + [p[1] for p in parts], axis=0)
    sums = jnp.dot(
        stacked.astype(jnp.bfloat16), band, preferred_element_type=jnp.float32
    )
    count = len(pieces)
    return [
        sums[c * height : (c + 1) * height]
        + sums[(count + c) * height : (count + c + 1) * height]
        for c in range(count)
    ]


def level(window_sums):
    return window_sums / (2 * W2 + 1) + 1e-05


def rows_for_here(ref, group, chips):
    me = lax.axis_index("tm")
    every = ref.shape[0] // SRC
    pieces = []
    for m in range(chips):
        start = pl.multiple_of((me ^ (CORES * m + 1)) * group, group)
        pieces.append(ref[pl.ds(start, group)])
    pieces += [ref[q * every : q * every + 1] for q in range(SRC)]
    return jnp.concatenate(pieces, axis=0)


def pack_kernel(group, chips, x_ref, out_ref):
    out_ref[...] = rows_for_here(x_ref, group, chips)


def coded_rows(own, other):
    first_core = lax.rem(lax.axis_index("tm"), CORES) == 0
    x = jnp.concatenate(
        [jnp.where(first_core, own, other), jnp.where(first_core, other, own)], axis=1
    )
    height, length = x.shape
    border = jnp.zeros((height, LANES), jnp.float32)
    magnitude = jnp.concatenate([border, jnp.abs(x), border], axis=1)
    inner = min(256, length)
    band = band_matrix(
        inner + 2 * LANES, inner, lambda p, t: jnp.abs(p - LANES - t) <= W2
    )
    sums = jnp.concatenate(
        banded_sums(
            [
                magnitude[:, start : start + inner + 2 * LANES]
                for start in range(0, length, inner)
            ],
            band,
        ),
        axis=1,
    )
    levels = level(sums)
    normed = x / levels
    left = lax.broadcasted_iota(jnp.int32, (height, LANES), 1) < W2
    tail = length - LANES
    ends = jnp.where(left, normed[:, :LANES], normed[:, tail:])
    end_levels = jnp.where(left, levels[:, :LANES], levels[:, tail:])
    coded = jnp.concatenate([normed, halves(ends)[1], end_levels], axis=1)
    return coded.astype(jnp.bfloat16)


def code_sources_kernel(group, chips, own_ref, other_ref, out_ref):
    first = chips * group
    other = rows_for_here(other_ref, group, chips)
    out_ref[...] = coded_rows(own_ref[first:], other[first:])


def code_receivers_kernel(group, chips, own_ref, other_ref, out_ref):
    last = chips * group
    other = rows_for_here(other_ref, group, chips)
    out_ref[...] = coded_rows(own_ref[:last], other[:last])


def join_kernel(offsets, receivers_ref, *refs):
    given, blocks = refs[:offsets], refs[offsets:]
    group = receivers_ref.shape[0] // len(blocks)
    sources = [ref[...].astype(jnp.float32) for ref in given]
    receivers = receivers_ref[...].astype(jnp.float32)
    for m, block in enumerate(blocks):
        rows = [receivers[m * group : (m + 1) * group]] + sources
        block[...] = jnp.concatenate(rows, axis=0).astype(jnp.bfloat16)


def finished_shards(runs, held):
    chips, height, width = held.shape
    length = width - 2 * LANES
    chip = lax.div(lax.axis_index("tm"), CORES)
    for m in range(chips):
        held[chip ^ m] = runs[m]
    left = lax.broadcasted_iota(jnp.int32, (height, LANES), 1) < W2
    tail = length - LANES
    end_values, end_levels = [], []

    def lanes(c, first):
        return held[c, :, first : first + LANES].astype(jnp.float32)

    for c in range(chips):
        high = jnp.where(left, lanes(c, 0), lanes(c, tail))
        end_values.append(high + lanes(c, length))
        end_levels.append(lanes(c, length + LANES))

    def meeting(ends, outside):
        outside = [jnp.full((height, LANES), outside, jnp.float32)]
        return [
            jnp.where(left, after, before)
            for before, after in zip(outside + ends, ends + outside)
        ]

    def across(p, t):
        at_p, at_t = jnp.where(p < W2, p, p - LANES), jnp.where(t < W2, t, t - LANES)
        return ((p < W2) != (t < W2)) & (jnp.abs(at_p - at_t) <= W2)

    values, levels = meeting(end_values, 0.0), meeting(end_levels, 1.0)
    added = banded_sums(
        [jnp.abs(v) * l for v, l in zip(values, levels)],
        band_matrix(LANES, LANES, across),
    )
    ends = [
        v * l / (l + a / (2 * W2 + 1)) for v, l, a in zip(values, levels, added)
    ]
    shard = length // CORES
    for k in range(chips * CORES):
        c, part = k // CORES, k % CORES
        pieces = [held[c, :, part * shard : (part + 1) * shard]]
        if part == 0:
            head = jnp.where(left, ends[c], lanes(c, 0)).astype(held.dtype)
            pieces = [head, held[c, :, LANES:shard]]
        if part == CORES - 1:
            last = jnp.where(left, lanes(c, tail), ends[c + 1]).astype(held.dtype)
            pieces = [held[c, :, part * shard : tail], last]
        yield jnp.concatenate(pieces, axis=1)


def lane_numbers(rows, dtype):
    return lax.broadcasted_iota(jnp.int32, (rows, LANES), 1).astype(dtype)


def shifted(rows, shift):
    height, length = rows.shape
    nothing = jnp.zeros((height, LANES), rows.dtype)
    if not shift:
        return jnp.concatenate([rows, nothing], axis=1)
    turned = [
        pltpu.roll(rows[:, first : first + LANES], shift, 1)
        for first in range(0, length, LANES)
    ]
    behind = lane_numbers(height, rows.dtype) >= shift
    return jnp.concatenate(
        [
            jnp.where(behind, here, before)
            for before, here in zip([nothing] + turned, turned + [nothing])
        ],
        axis=1,
    )


def correlate_kernel(offsets, scale, *refs):
    chips = len(refs) - offsets - 3
    blocks, refs = refs[:chips], refs[chips:]
    outs, (held, mixed, table) = refs[:offsets], refs[offsets:]
    sources = offsets * SRC
    group = held.shape[1] - sources
    runs = {m: ref[...].astype(held.dtype) for m, ref in zip(chip_order(chips), blocks)}
    product = None
    for wide in finished_shards(runs, held):
        receivers, senders = wide[:group], wide[group:]
        fine = [shifted(receivers, MAXLAG - j) for j in range(FINE)]
        coarse = [shifted(senders, FINE * i) for i in range(COARSE)]
        term = lax.dot_general(
            jnp.concatenate(fine, axis=0).astype(jnp.bfloat16),
            jnp.concatenate(coarse, axis=0).astype(jnp.bfloat16),
            (((1,), (1,)), ((), ())),
            preferred_element_type=jnp.float32,
        )
        product = term if product is None else product + term
    product = product * scale
    for h in range(mixed.shape[0]):
        first, last = h * LANES, min((h + 1) * LANES, COARSE * sources)
        for j in range(FINE):
            mixed[h, pl.ds(j, group, stride=FINE), : last - first] = product[
                j * group : (j + 1) * group, first:last
            ]
        table[h * LANES : (h + 1) * LANES] = mixed[h].T.astype(table.dtype)
    columns = table.shape[1]
    turned = []
    for i in range(COARSE):
        block = table[i * sources : (i + 1) * sources]
        turned.append(pltpu.roll(block, FINE * i, 1) if i else block)
    lane = lane_numbers(sources, table.dtype)
    width = group * LAGS

    def place(tiles, tile, piece, low):
        if low and tile in tiles:
            piece = jnp.where(lane >= low, piece, tiles[tile])
        tiles[tile] = piece

    tiles = {}
    for b in range(group):
        joined = {}
        for i in range(COARSE):
            tile, low = divmod((b + i) * FINE % columns, LANES)
            piece = turned[i][:, tile * LANES : (tile + 1) * LANES]
            place(joined, tile, piece, low)
        turn = b * (LAGS - FINE) % LANES
        if turn:
            joined = {tile: pltpu.roll(v, turn, 1) for tile, v in joined.items()}
        for lag in range(LAGS):
            at, to = (b * FINE + lag) % columns, b * LAGS + lag
            if lag == 0 or at % LANES == 0 or to % LANES == 0:
                place(tiles, to // LANES, joined[at // LANES], to % LANES)
    for tile, value in tiles.items():
        first = tile * LANES
        last = min(first + LANES, width)
        for o in range(offsets):
            rows = value.astype(jnp.float32)[o * SRC : (o + 1) * SRC, : last - first]
            outs[o][:, first:last] = rows.astype(jnp.bfloat16)


def stack_kernel(*refs):
    out_ref = refs[-1]
    for o, ref in enumerate(refs[:-1]):
        out_ref[:, o, :] = ref[...].astype(jnp.float32)


def call(kernel, out_shape, inputs, scratch=(), flops=0):
    single = not isinstance(out_shape, list)
    spec = pl.BlockSpec(memory_space=pltpu.VMEM)
    moved = sum(v.size * v.dtype.itemsize for v in inputs)
    return pl.pallas_call(
        kernel,
        out_shape=out_shape,
        in_specs=[spec] * len(inputs),
        out_specs=spec if single else [spec] * len(out_shape),
        scratch_shapes=list(scratch),
        compiler_params=pltpu.CompilerParams(vmem_limit_bytes=32 * 1024 * 1024),
        cost_estimate=pl.CostEstimate(
            flops=flops, bytes_accessed=moved, transcendentals=0
        ),
    )(*inputs)


def chip_order(chips):
    return [m for m in (0, 2, 3, 1) if m < chips] + list(range(4, chips))


def swapped(block, axis, m):
    devices = range(lax.axis_size(axis))
    return lax.ppermute(block, axis, [(k, k ^ m) for k in devices])


def passed_along(block, distance):
    devices = range(lax.axis_size("chan"))
    route = [((i - distance) % len(devices), i) for i in devices]
    return lax.ppermute(block, "chan", route)


def passed_across(block, distance):
    count, places = lax.axis_size("chan"), lax.axis_size("tm")
    route = [
        ((i - distance) % count * places + (k ^ 1), i * places + k)
        for i in range(count)
        for k in range(places)
    ]
    return lax.ppermute(block, ("chan", "tm"), route)


def body(strain_rate):
    channels, length = strain_rate.shape
    shards = lax.axis_size("tm")
    chips = shards // CORES
    reach = lax.axis_size("chan") // 4
    group = channels // shards
    steps = list(range(-reach, 0)) + list(range(1, reach + 1))
    offsets = len(steps)
    sources = offsets * SRC
    scale = 1.0 / math.sqrt(length * shards)
    run = CORES * length
    coded = run + 2 * LANES

    other = swapped(strain_rate, "tm", 1)
    own = call(
        functools.partial(pack_kernel, group, chips),
        jax.ShapeDtypeStruct((chips * group + SRC, length), jnp.float32),
        [strain_rate],
        flops=8 * channels * length,
    )
    own_sources = call(
        functools.partial(code_sources_kernel, group, chips),
        jax.ShapeDtypeStruct((SRC, coded), jnp.bfloat16),
        [own, other],
    )
    arrived = [passed_along(own_sources, d) for d in steps]
    own_receivers = call(
        functools.partial(code_receivers_kernel, group, chips),
        jax.ShapeDtypeStruct((chips * group, coded), jnp.bfloat16),
        [own, other],
        flops=8 * chips * group * run * (256 + 2 * LANES),
    )
    blocks = call(
        functools.partial(join_kernel, offsets),
        [jax.ShapeDtypeStruct((group + sources, coded), jnp.bfloat16)] * chips,
        [own_receivers] + arrived,
    )
    blocks = list(blocks[:1]) + [
        swapped(blocks[m], "tm", CORES * m) for m in chip_order(chips)[1:]
    ]
    columns = -(-group * FINE // LANES) * LANES
    heights = -(-COARSE * sources // LANES) * LANES
    kind = jnp.float32 if group % 16 or sources % 16 else jnp.bfloat16
    results = call(
        functools.partial(correlate_kernel, offsets, scale),
        [jax.ShapeDtypeStruct((SRC, group * LAGS), jnp.bfloat16)] * offsets,
        blocks,
        scratch=[
            pltpu.VMEM((chips, group + sources, coded), kind),
            pltpu.VMEM((heights // LANES, columns, LANES), jnp.float32),
            pltpu.VMEM((heights, columns), kind),
        ],
        flops=2 * shards * (length + LANES) * group * FINE * COARSE * sources,
    )
    arrived = [passed_across(r, -d) for r, d in zip(results, steps)]
    return call(
        stack_kernel,
        jax.ShapeDtypeStruct((SRC, offsets, group * LAGS), jnp.float32),
        arrived,
    )


def solution(mesh):
    placed = (P("chan", "tm"),)
    return jax.shard_map(
        body, mesh=mesh, in_specs=placed, out_specs=P("chan", None, "tm"), check_vma=False
    )
```

```python
import functools
import math

import jax
import jax.numpy as jnp
from jax import lax
from jax.experimental import pallas as pl
from jax.experimental.pallas import tpu as pltpu
from jax.sharding import PartitionSpec as P

SRC = 8
MAXLAG = 25
W2 = 64
LAGS = 51
FINE = 8
COARSE = -(-LAGS // FINE)
LANES = 128
CORES = 2


def band_matrix(rows, columns, related):
    p = lax.broadcasted_iota(jnp.int32, (rows, columns), 0)
    t = lax.broadcasted_iota(jnp.int32, (rows, columns), 1)
    return jnp.where(related(p, t), 1.0, 0.0).astype(jnp.bfloat16)


def halves(values):
    high = values.astype(jnp.bfloat16).astype(jnp.float32)
    return high, values - high


def banded_sums(pieces, band):
    height = pieces[0].shape[0]
    parts = [halves(piece) for piece in pieces]
    stacked = jnp.concatenate([p[0] for p in parts] + [p[1] for p in parts], axis=0)
    sums = jnp.dot(
        stacked.astype(jnp.bfloat16), band, preferred_element_type=jnp.float32
    )
    count = len(pieces)
    return [
        sums[c * height : (c + 1) * height]
        + sums[(count + c) * height : (count + c + 1) * height]
        for c in range(count)
    ]


def level(window_sums):
    return window_sums / (2 * W2 + 1) + 1e-05


def rows_for_here(ref, group, chips):
    me = lax.axis_index("tm")
    every = ref.shape[0] // SRC
    pieces = []
    for m in range(chips):
        start = pl.multiple_of((me ^ (CORES * m + 1)) * group, group)
        pieces.append(ref[pl.ds(start, group)])
    pieces += [ref[q * every : q * every + 1] for q in range(SRC)]
    return jnp.concatenate(pieces, axis=0)


def pack_kernel(group, chips, x_ref, out_ref):
    out_ref[...] = rows_for_here(x_ref, group, chips)


def coded_rows(own, other):
    first_core = lax.rem(lax.axis_index("tm"), CORES) == 0
    x = jnp.concatenate(
        [jnp.where(first_core, own, other), jnp.where(first_core, other, own)], axis=1
    )
    height, length = x.shape
    border = jnp.zeros((height, LANES), jnp.float32)
    magnitude = jnp.concatenate([border, jnp.abs(x), border], axis=1)
    inner = min(256, length)
    band = band_matrix(
        inner + 2 * LANES, inner, lambda p, t: jnp.abs(p - LANES - t) <= W2
    )
    sums = jnp.concatenate(
        banded_sums(
            [
                magnitude[:, start : start + inner + 2 * LANES]
                for start in range(0, length, inner)
            ],
            band,
        ),
        axis=1,
    )
    levels = level(sums)
    normed = x / levels
    left = lax.broadcasted_iota(jnp.int32, (height, LANES), 1) < W2
    tail = length - LANES
    ends = jnp.where(left, normed[:, :LANES], normed[:, tail:])
    end_levels = jnp.where(left, levels[:, :LANES], levels[:, tail:])
    coded = jnp.concatenate([normed, halves(ends)[1], end_levels], axis=1)
    return coded.astype(jnp.bfloat16)


def code_sources_kernel(group, chips, own_ref, other_ref, out_ref):
    first = chips * group
    other = rows_for_here(other_ref, group, chips)
    out_ref[...] = coded_rows(own_ref[first:], other[first:])


def code_receivers_kernel(group, chips, own_ref, other_ref, out_ref):
    last = chips * group
    other = rows_for_here(other_ref, group, chips)
    out_ref[...] = coded_rows(own_ref[:last], other[:last])


def join_kernel(offsets, receivers_ref, *refs):
    given, blocks = refs[:offsets], refs[offsets:]
    group = receivers_ref.shape[0] // len(blocks)
    sources = [ref[...].astype(jnp.float32) for ref in given]
    receivers = receivers_ref[...].astype(jnp.float32)
    for m, block in enumerate(blocks):
        rows = [receivers[m * group : (m + 1) * group]] + sources
        block[...] = jnp.concatenate(rows, axis=0).astype(jnp.bfloat16)


def finished_shards(runs, held):
    chips, height, width = held.shape
    length = width - 2 * LANES
    chip = lax.div(lax.axis_index("tm"), CORES)
    for m in range(chips):
        held[chip ^ m] = runs[m]
    left = lax.broadcasted_iota(jnp.int32, (height, LANES), 1) < W2
    tail = length - LANES
    end_values, end_levels = [], []

    def lanes(c, first):
        return held[c, :, first : first + LANES].astype(jnp.float32)

    for c in range(chips):
        high = jnp.where(left, lanes(c, 0), lanes(c, tail))
        end_values.append(high + lanes(c, length))
        end_levels.append(lanes(c, length + LANES))

    def meeting(ends, outside):
        outside = [jnp.full((height, LANES), outside, jnp.float32)]
        return [
            jnp.where(left, after, before)
            for before, after in zip(outside + ends, ends + outside)
        ]

    def across(p, t):
        at_p, at_t = jnp.where(p < W2, p, p - LANES), jnp.where(t < W2, t, t - LANES)
        return ((p < W2) != (t < W2)) & (jnp.abs(at_p - at_t) <= W2)

    values, levels = meeting(end_values, 0.0), meeting(end_levels, 1.0)
    added = banded_sums(
        [jnp.abs(v) * l for v, l in zip(values, levels)],
        band_matrix(LANES, LANES, across),
    )
    ends = [
        v * l / (l + a / (2 * W2 + 1)) for v, l, a in zip(values, levels, added)
    ]
    shard = length // CORES
    for k in range(chips * CORES):
        c, part = k // CORES, k % CORES
        pieces = [held[c, :, part * shard : (part + 1) * shard]]
        if part == 0:
            head = jnp.where(left, ends[c], lanes(c, 0)).astype(held.dtype)
            pieces = [head, held[c, :, LANES:shard]]
        if part == CORES - 1:
            last = jnp.where(left, lanes(c, tail), ends[c + 1]).astype(held.dtype)
            pieces = [held[c, :, part * shard : tail], last]
        yield jnp.concatenate(pieces, axis=1)


def lane_numbers(rows, dtype):
    return lax.broadcasted_iota(jnp.int32, (rows, LANES), 1).astype(dtype)


def shifted(rows, shift):
    height, length = rows.shape
    nothing = jnp.zeros((height, LANES), rows.dtype)
    if not shift:
        return jnp.concatenate([rows, nothing], axis=1)
    turned = [
        pltpu.roll(rows[:, first : first + LANES], shift, 1)
        for first in range(0, length, LANES)
    ]
    behind = lane_numbers(height, rows.dtype) >= shift
    return jnp.concatenate(
        [
            jnp.where(behind, here, before)
            for before, here in zip([nothing] + turned, turned + [nothing])
        ],
        axis=1,
    )


def correlate_kernel(offsets, scale, *refs):
    chips = len(refs) - offsets - 3
    blocks, refs = refs[:chips], refs[chips:]
    outs, (held, mixed, table) = refs[:offsets], refs[offsets:]
    sources = offsets * SRC
    group = held.shape[1] - sources
    runs = {m: ref[...].astype(held.dtype) for m, ref in zip(chip_order(chips), blocks)}
    product = None
    for wide in finished_shards(runs, held):
        receivers, senders = wide[:group], wide[group:]
        fine = [shifted(receivers, MAXLAG - j) for j in range(FINE)]
        coarse = [shifted(senders, FINE * i) for i in range(COARSE)]
        term = lax.dot_general(
            jnp.concatenate(fine, axis=0).astype(jnp.bfloat16),
            jnp.concatenate(coarse, axis=0).astype(jnp.bfloat16),
            (((1,), (1,)), ((), ())),
            preferred_element_type=jnp.float32,
        )
        product = term if product is None else product + term
    product = product * scale
    for h in range(mixed.shape[0]):
        first, last = h * LANES, min((h + 1) * LANES, COARSE * sources)
        for j in range(FINE):
            mixed[h, pl.ds(j, group, stride=FINE), : last - first] = product[
                j * group : (j + 1) * group, first:last
            ]
        table[h * LANES : (h + 1) * LANES] = mixed[h].T.astype(table.dtype)
    columns = table.shape[1]
    turned = []
    for i in range(COARSE):
        block = table[i * sources : (i + 1) * sources]
        turned.append(pltpu.roll(block, FINE * i, 1) if i else block)
    lane = lane_numbers(sources, table.dtype)
    width = group * LAGS

    def place(tiles, tile, piece, low):
        if low and tile in tiles:
            piece = jnp.where(lane >= low, piece, tiles[tile])
        tiles[tile] = piece

    tiles = {}
    for b in range(group):
        joined = {}
        for i in range(COARSE):
            tile, low = divmod((b + i) * FINE % columns, LANES)
            piece = turned[i][:, tile * LANES : (tile + 1) * LANES]
            place(joined, tile, piece, low)
        turn = b * (LAGS - FINE) % LANES
        if turn:
            joined = {tile: pltpu.roll(v, turn, 1) for tile, v in joined.items()}
        for lag in range(LAGS):
            at, to = (b * FINE + lag) % columns, b * LAGS + lag
            if lag == 0 or at % LANES == 0 or to % LANES == 0:
                place(tiles, to // LANES, joined[at // LANES], to % LANES)
    for tile, value in tiles.items():
        first = tile * LANES
        last = min(first + LANES, width)
        for o in range(offsets):
            rows = value.astype(jnp.float32)[o * SRC : (o + 1) * SRC, : last - first]
            outs[o][:, first:last] = rows.astype(jnp.bfloat16)


def stack_kernel(*refs):
    out_ref = refs[-1]
    for o, ref in enumerate(refs[:-1]):
        out_ref[:, o, :] = ref[...].astype(jnp.float32)


def call(kernel, out_shape, inputs, scratch=(), flops=0):
    single = not isinstance(out_shape, list)
    spec = pl.BlockSpec(memory_space=pltpu.VMEM)
    moved = sum(v.size * v.dtype.itemsize for v in inputs)
    return pl.pallas_call(
        kernel,
        out_shape=out_shape,
        in_specs=[spec] * len(inputs),
        out_specs=spec if single else [spec] * len(out_shape),
        scratch_shapes=list(scratch),
        compiler_params=pltpu.CompilerParams(vmem_limit_bytes=32 * 1024 * 1024),
        cost_estimate=pl.CostEstimate(
            flops=flops, bytes_accessed=moved, transcendentals=0
        ),
    )(*inputs)


def chip_order(chips):
    return [m for m in (0, 3, 1, 2) if m < chips] + list(range(4, chips))


def swapped(block, axis, m):
    devices = range(lax.axis_size(axis))
    return lax.ppermute(block, axis, [(k, k ^ m) for k in devices])


def passed_along(block, distance):
    devices = range(lax.axis_size("chan"))
    route = [((i - distance) % len(devices), i) for i in devices]
    return lax.ppermute(block, "chan", route)


def passed_across(block, distance):
    count, places = lax.axis_size("chan"), lax.axis_size("tm")
    route = [
        ((i - distance) % count * places + (k ^ 1), i * places + k)
        for i in range(count)
        for k in range(places)
    ]
    return lax.ppermute(block, ("chan", "tm"), route)


def body(strain_rate):
    channels, length = strain_rate.shape
    shards = lax.axis_size("tm")
    chips = shards // CORES
    reach = lax.axis_size("chan") // 4
    group = channels // shards
    steps = list(range(-reach, 0)) + list(range(1, reach + 1))
    offsets = len(steps)
    sources = offsets * SRC
    scale = 1.0 / math.sqrt(length * shards)
    run = CORES * length
    coded = run + 2 * LANES

    other = swapped(strain_rate, "tm", 1)
    own = call(
        functools.partial(pack_kernel, group, chips),
        jax.ShapeDtypeStruct((chips * group + SRC, length), jnp.float32),
        [strain_rate],
        flops=8 * channels * length,
    )
    own_sources = call(
        functools.partial(code_sources_kernel, group, chips),
        jax.ShapeDtypeStruct((SRC, coded), jnp.bfloat16),
        [own, other],
    )
    arrived = [passed_along(own_sources, d) for d in steps]
    own_receivers = call(
        functools.partial(code_receivers_kernel, group, chips),
        jax.ShapeDtypeStruct((chips * group, coded), jnp.bfloat16),
        [own, other],
        flops=8 * chips * group * run * (256 + 2 * LANES),
    )
    blocks = call(
        functools.partial(join_kernel, offsets),
        [jax.ShapeDtypeStruct((group + sources, coded), jnp.bfloat16)] * chips,
        [own_receivers] + arrived,
    )
    blocks = list(blocks[:1]) + [
        swapped(blocks[m], "tm", CORES * m) for m in chip_order(chips)[1:]
    ]
    columns = -(-group * FINE // LANES) * LANES
    heights = -(-COARSE * sources // LANES) * LANES
    kind = jnp.float32 if group % 16 or sources % 16 else jnp.bfloat16
    results = call(
        functools.partial(correlate_kernel, offsets, scale),
        [jax.ShapeDtypeStruct((SRC, group * LAGS), jnp.bfloat16)] * offsets,
        blocks,
        scratch=[
            pltpu.VMEM((chips, group + sources, coded), kind),
            pltpu.VMEM((heights // LANES, columns, LANES), jnp.float32),
            pltpu.VMEM((heights, columns), kind),
        ],
        flops=2 * shards * (length + LANES) * group * FINE * COARSE * sources,
    )
    arrived = [passed_across(r, -d) for r, d in zip(results, steps)]
    return call(
        stack_kernel,
        jax.ShapeDtypeStruct((SRC, offsets, group * LAGS), jnp.float32),
        arrived,
    )


def solution(mesh):
    placed = (P("chan", "tm"),)
    return jax.shard_map(
        body, mesh=mesh, in_specs=placed, out_specs=P("chan", None, "tm"), check_vma=False
    )
```

```python
import functools
import math

import jax
import jax.numpy as jnp
from jax import lax
from jax.experimental import pallas as pl
from jax.experimental.pallas import tpu as pltpu
from jax.sharding import PartitionSpec as P

SRC = 8
MAXLAG = 25
W2 = 64
LAGS = 51
FINE = 8
COARSE = -(-LAGS // FINE)
MIDDLE = MAXLAG // FINE * FINE
LANES = 128
CORES = 2


def band_matrix(rows, columns, related):
    p = lax.broadcasted_iota(jnp.int32, (rows, columns), 0)
    t = lax.broadcasted_iota(jnp.int32, (rows, columns), 1)
    return jnp.where(related(p, t), 1.0, 0.0).astype(jnp.bfloat16)


def halves(values):
    high = values.astype(jnp.bfloat16).astype(jnp.float32)
    return high, values - high


def banded_sums(pieces, band):
    height = pieces[0].shape[0]
    parts = [halves(piece) for piece in pieces]
    stacked = jnp.concatenate([p[0] for p in parts] + [p[1] for p in parts], axis=0)
    sums = jnp.dot(
        stacked.astype(jnp.bfloat16), band, preferred_element_type=jnp.float32
    )
    count = len(pieces)
    return [
        sums[c * height : (c + 1) * height]
        + sums[(count + c) * height : (count + c + 1) * height]
        for c in range(count)
    ]


def level(window_sums):
    return window_sums / (2 * W2 + 1) + 1e-05


def rows_for_here(ref, group, chips):
    me = lax.axis_index("tm")
    every = ref.shape[0] // SRC
    pieces = []
    for m in range(chips):
        start = pl.multiple_of((me ^ (CORES * m + 1)) * group, group)
        pieces.append(ref[pl.ds(start, group)])
    pieces += [ref[q * every : q * every + 1] for q in range(SRC)]
    return jnp.concatenate(pieces, axis=0)


def pack_kernel(group, chips, x_ref, out_ref):
    out_ref[...] = rows_for_here(x_ref, group, chips)


def coded_rows(own, other):
    first_core = lax.rem(lax.axis_index("tm"), CORES) == 0
    x = jnp.concatenate(
        [jnp.where(first_core, own, other), jnp.where(first_core, other, own)], axis=1
    )
    height, length = x.shape
    border = jnp.zeros((height, LANES), jnp.float32)
    magnitude = jnp.concatenate([border, jnp.abs(x), border], axis=1)
    inner = min(256, length)
    band = band_matrix(
        inner + 2 * LANES, inner, lambda p, t: jnp.abs(p - LANES - t) <= W2
    )
    sums = jnp.concatenate(
        banded_sums(
            [
                magnitude[:, start : start + inner + 2 * LANES]
                for start in range(0, length, inner)
            ],
            band,
        ),
        axis=1,
    )
    levels = level(sums)
    normed = x / levels
    left = lax.broadcasted_iota(jnp.int32, (height, LANES), 1) < W2
    tail = length - LANES
    ends = jnp.where(left, normed[:, :LANES], normed[:, tail:])
    end_levels = jnp.where(left, levels[:, :LANES], levels[:, tail:])
    coded = jnp.concatenate([normed, halves(ends)[1], end_levels], axis=1)
    return coded.astype(jnp.bfloat16)


def code_sources_kernel(group, chips, own_ref, other_ref, out_ref):
    first = chips * group
    other = rows_for_here(other_ref, group, chips)
    out_ref[...] = coded_rows(own_ref[first:], other[first:])


def code_receivers_kernel(group, chips, own_ref, other_ref, out_ref):
    last = chips * group
    other = rows_for_here(other_ref, group, chips)
    out_ref[...] = coded_rows(own_ref[:last], other[:last])


def join_kernel(offsets, receivers_ref, *refs):
    given, blocks = refs[:offsets], refs[offsets:]
    group = receivers_ref.shape[0] // len(blocks)
    sources = [ref[...].astype(jnp.float32) for ref in given]
    receivers = receivers_ref[...].astype(jnp.float32)
    for m, block in enumerate(blocks):
        rows = [receivers[m * group : (m + 1) * group]] + sources
        block[...] = jnp.concatenate(rows, axis=0).astype(jnp.bfloat16)


def finished_shards(runs, held):
    chips, height, width = held.shape
    length = width - 2 * LANES
    chip = lax.div(lax.axis_index("tm"), CORES)
    for m in range(chips):
        held[chip ^ m] = runs[m]
    left = lax.broadcasted_iota(jnp.int32, (height, LANES), 1) < W2
    tail = length - LANES
    end_values, end_levels = [], []

    def lanes(c, first):
        return held[c, :, first : first + LANES].astype(jnp.float32)

    for c in range(chips):
        high = jnp.where(left, lanes(c, 0), lanes(c, tail))
        end_values.append(high + lanes(c, length))
        end_levels.append(lanes(c, length + LANES))

    def meeting(ends, outside):
        outside = [jnp.full((height, LANES), outside, jnp.float32)]
        return [
            jnp.where(left, after, before)
            for before, after in zip(outside + ends, ends + outside)
        ]

    def across(p, t):
        at_p, at_t = jnp.where(p < W2, p, p - LANES), jnp.where(t < W2, t, t - LANES)
        return ((p < W2) != (t < W2)) & (jnp.abs(at_p - at_t) <= W2)

    values, levels = meeting(end_values, 0.0), meeting(end_levels, 1.0)
    added = banded_sums(
        [jnp.abs(v) * l for v, l in zip(values, levels)],
        band_matrix(LANES, LANES, across),
    )
    ends = [
        v * l / (l + a / (2 * W2 + 1)) for v, l, a in zip(values, levels, added)
    ]
    shard = length // CORES
    for k in range(chips * CORES):
        c, part = k // CORES, k % CORES
        pieces = [held[c, :, part * shard : (part + 1) * shard]]
        if part == 0:
            head = jnp.where(left, ends[c], lanes(c, 0)).astype(held.dtype)
            pieces = [head, held[c, :, LANES:shard]]
        if part == CORES - 1:
            last = jnp.where(left, lanes(c, tail), ends[c + 1]).astype(held.dtype)
            pieces = [held[c, :, part * shard : tail], last]
        yield jnp.concatenate(pieces, axis=1)


def lane_numbers(rows, dtype):
    return lax.broadcasted_iota(jnp.int32, (rows, LANES), 1).astype(dtype)


def shifted(rows, shift):
    height, length = rows.shape
    nothing = jnp.zeros((height, LANES), rows.dtype)
    if not shift:
        return jnp.concatenate([rows, nothing], axis=1)
    amount = shift % LANES
    turned = [
        pltpu.roll(rows[:, first : first + LANES], amount, 1)
        for first in range(0, length, LANES)
    ]
    if shift > 0:
        low, high = [nothing] + turned, turned + [nothing]
    else:
        low, high = turned + [nothing], turned[1:] + [nothing, turned[0]]
    behind = lane_numbers(height, rows.dtype) >= amount
    return jnp.concatenate(
        [jnp.where(behind, h, l) for l, h in zip(low, high)], axis=1
    )


def correlate_kernel(offsets, scale, *refs):
    chips = len(refs) - offsets - 3
    blocks, refs = refs[:chips], refs[chips:]
    outs, (held, mixed, table) = refs[:offsets], refs[offsets:]
    sources = offsets * SRC
    group = held.shape[1] - sources
    runs = [ref[...].astype(held.dtype) for ref in blocks[:1] + blocks[:0:-1]]
    product = None
    for wide in finished_shards(runs, held):
        receivers, senders = wide[:group], wide[group:]
        fine = [shifted(receivers, MAXLAG - MIDDLE - j) for j in range(FINE)]
        coarse = [shifted(senders, FINE * i - MIDDLE) for i in range(COARSE)]
        term = lax.dot_general(
            jnp.concatenate(fine, axis=0).astype(jnp.bfloat16),
            jnp.concatenate(coarse, axis=0).astype(jnp.bfloat16),
            (((1,), (1,)), ((), ())),
            preferred_element_type=jnp.float32,
        )
        product = term if product is None else product + term
    product = product * scale
    for h in range(mixed.shape[0]):
        first, last = h * LANES, min((h + 1) * LANES, COARSE * sources)
        for j in range(FINE):
            mixed[h, pl.ds(j, group, stride=FINE), : last - first] = product[
                j * group : (j + 1) * group, first:last
            ]
        table[h * LANES : (h + 1) * LANES] = mixed[h].T.astype(table.dtype)
    columns = table.shape[1]
    turned = []
    for i in range(COARSE):
        block = table[i * sources : (i + 1) * sources]
        turned.append(pltpu.roll(block, FINE * i, 1) if i else block)
    lane = lane_numbers(sources, table.dtype)
    width = group * LAGS

    def place(tiles, tile, piece, low):
        if low and tile in tiles:
            piece = jnp.where(lane >= low, piece, tiles[tile])
        tiles[tile] = piece

    tiles = {}
    for b in range(group):
        joined = {}
        for i in range(COARSE):
            tile, low = divmod((b + i) * FINE % columns, LANES)
            piece = turned[i][:, tile * LANES : (tile + 1) * LANES]
            place(joined, tile, piece, low)
        turn = b * (LAGS - FINE) % LANES
        if turn:
            joined = {tile: pltpu.roll(v, turn, 1) for tile, v in joined.items()}
        for lag in range(LAGS):
            at, to = (b * FINE + lag) % columns, b * LAGS + lag
            if lag == 0 or at % LANES == 0 or to % LANES == 0:
                place(tiles, to // LANES, joined[at // LANES], to % LANES)
    for tile, value in tiles.items():
        first = tile * LANES
        last = min(first + LANES, width)
        for o in range(offsets):
            rows = value.astype(jnp.float32)[o * SRC : (o + 1) * SRC, : last - first]
            outs[o][:, first:last] = rows.astype(jnp.bfloat16)


def stack_kernel(*refs):
    out_ref = refs[-1]
    for o, ref in enumerate(refs[:-1]):
        out_ref[:, o, :] = ref[...].astype(jnp.float32)


def call(kernel, out_shape, inputs, scratch=(), flops=0):
    single = not isinstance(out_shape, list)
    spec = pl.BlockSpec(memory_space=pltpu.VMEM)
    moved = sum(v.size * v.dtype.itemsize for v in inputs)
    return pl.pallas_call(
        kernel,
        out_shape=out_shape,
        in_specs=[spec] * len(inputs),
        out_specs=spec if single else [spec] * len(out_shape),
        scratch_shapes=list(scratch),
        compiler_params=pltpu.CompilerParams(vmem_limit_bytes=32 * 1024 * 1024),
        cost_estimate=pl.CostEstimate(
            flops=flops, bytes_accessed=moved, transcendentals=0
        ),
    )(*inputs)


def swapped(block, axis, m):
    devices = range(lax.axis_size(axis))
    return lax.ppermute(block, axis, [(k, k ^ m) for k in devices])


def passed_along(block, distance):
    devices = range(lax.axis_size("chan"))
    route = [((i - distance) % len(devices), i) for i in devices]
    return lax.ppermute(block, "chan", route)


def passed_across(block, distance):
    count, places = lax.axis_size("chan"), lax.axis_size("tm")
    route = [
        ((i - distance) % count * places + (k ^ 1), i * places + k)
        for i in range(count)
        for k in range(places)
    ]
    return lax.ppermute(block, ("chan", "tm"), route)


def body(strain_rate):
    channels, length = strain_rate.shape
    shards = lax.axis_size("tm")
    chips = shards // CORES
    reach = lax.axis_size("chan") // 4
    group = channels // shards
    steps = list(range(-reach, 0)) + list(range(1, reach + 1))
    offsets = len(steps)
    sources = offsets * SRC
    scale = 1.0 / math.sqrt(length * shards)
    run = CORES * length
    coded = run + 2 * LANES

    other = swapped(strain_rate, "tm", 1)
    own = call(
        functools.partial(pack_kernel, group, chips),
        jax.ShapeDtypeStruct((chips * group + SRC, length), jnp.float32),
        [strain_rate],
        flops=8 * channels * length,
    )
    own_sources = call(
        functools.partial(code_sources_kernel, group, chips),
        jax.ShapeDtypeStruct((SRC, coded), jnp.bfloat16),
        [own, other],
    )
    arrived = [passed_along(own_sources, d) for d in steps]
    own_receivers = call(
        functools.partial(code_receivers_kernel, group, chips),
        jax.ShapeDtypeStruct((chips * group, coded), jnp.bfloat16),
        [own, other],
        flops=8 * chips * group * run * (256 + 2 * LANES),
    )
    blocks = call(
        functools.partial(join_kernel, offsets),
        [jax.ShapeDtypeStruct((group + sources, coded), jnp.bfloat16)] * chips,
        [own_receivers] + arrived,
    )
    blocks = list(blocks[:1]) + [
        swapped(blocks[m], "tm", CORES * m) for m in range(chips - 1, 0, -1)
    ]
    columns = -(-group * FINE // LANES) * LANES
    heights = -(-COARSE * sources // LANES) * LANES
    kind = jnp.float32 if group % 16 or sources % 16 else jnp.bfloat16
    results = call(
        functools.partial(correlate_kernel, offsets, scale),
        [jax.ShapeDtypeStruct((SRC, group * LAGS), jnp.bfloat16)] * offsets,
        blocks,
        scratch=[
            pltpu.VMEM((chips, group + sources, coded), kind),
            pltpu.VMEM((heights // LANES, columns, LANES), jnp.float32),
            pltpu.VMEM((heights, columns), kind),
        ],
        flops=2 * shards * (length + LANES) * group * FINE * COARSE * sources,
    )
    arrived = [passed_across(r, -d) for r, d in zip(results, steps)]
    return call(
        stack_kernel,
        jax.ShapeDtypeStruct((SRC, offsets, group * LAGS), jnp.float32),
        arrived,
    )


def solution(mesh):
    placed = (P("chan", "tm"),)
    return jax.shard_map(
        body, mesh=mesh, in_specs=placed, out_specs=P("chan", None, "tm"), check_vma=False
    )
```

```python
import functools
import math

import jax
import jax.numpy as jnp
from jax import lax
from jax.experimental import pallas as pl
from jax.experimental.pallas import tpu as pltpu
from jax.sharding import PartitionSpec as P

SRC = 8
MAXLAG = 25
W2 = 64
LAGS = 51
FINE = 8
COARSE = -(-LAGS // FINE)
LANES = 128
CORES = 2


def band_matrix(rows, columns, related):
    p = lax.broadcasted_iota(jnp.int32, (rows, columns), 0)
    t = lax.broadcasted_iota(jnp.int32, (rows, columns), 1)
    return jnp.where(related(p, t), 1.0, 0.0).astype(jnp.bfloat16)


def halves(values):
    high = values.astype(jnp.bfloat16).astype(jnp.float32)
    return high, values - high


def banded_sums(pieces, band):
    height = pieces[0].shape[0]
    parts = [halves(piece) for piece in pieces]
    stacked = jnp.concatenate([p[0] for p in parts] + [p[1] for p in parts], axis=0)
    sums = jnp.dot(
        stacked.astype(jnp.bfloat16), band, preferred_element_type=jnp.float32
    )
    count = len(pieces)
    return [
        sums[c * height : (c + 1) * height]
        + sums[(count + c) * height : (count + c + 1) * height]
        for c in range(count)
    ]


def level(window_sums):
    return window_sums / (2 * W2 + 1) + 1e-05


def rows_for_here(ref, group, chips):
    me = lax.axis_index("tm")
    every = ref.shape[0] // SRC
    pieces = []
    for m in range(chips):
        start = pl.multiple_of((me ^ (CORES * m + 1)) * group, group)
        pieces.append(ref[pl.ds(start, group)])
    pieces += [ref[q * every : q * every + 1] for q in range(SRC)]
    return jnp.concatenate(pieces, axis=0)


def pack_kernel(group, chips, x_ref, out_ref):
    out_ref[...] = rows_for_here(x_ref, group, chips)


def coded_rows(own, other):
    first_core = lax.rem(lax.axis_index("tm"), CORES) == 0
    x = jnp.concatenate(
        [jnp.where(first_core, own, other), jnp.where(first_core, other, own)], axis=1
    )
    height, length = x.shape
    border = jnp.zeros((height, LANES), jnp.float32)
    magnitude = jnp.concatenate([border, jnp.abs(x), border], axis=1)
    inner = min(256, length)
    band = band_matrix(
        inner + 2 * LANES, inner, lambda p, t: jnp.abs(p - LANES - t) <= W2
    )
    sums = jnp.concatenate(
        banded_sums(
            [
                magnitude[:, start : start + inner + 2 * LANES]
                for start in range(0, length, inner)
            ],
            band,
        ),
        axis=1,
    )
    levels = level(sums)
    normed = x / levels
    left = lax.broadcasted_iota(jnp.int32, (height, LANES), 1) < W2
    tail = length - LANES
    ends = jnp.where(left, normed[:, :LANES], normed[:, tail:])
    end_levels = jnp.where(left, levels[:, :LANES], levels[:, tail:])
    coded = jnp.concatenate([normed, halves(ends)[1], end_levels], axis=1)
    return coded.astype(jnp.bfloat16)


def code_sources_kernel(group, chips, own_ref, other_ref, out_ref):
    first = chips * group
    other = rows_for_here(other_ref, group, chips)
    out_ref[...] = coded_rows(own_ref[first:], other[first:])


def code_receivers_kernel(group, chips, own_ref, other_ref, out_ref):
    last = chips * group
    other = rows_for_here(other_ref, group, chips)
    out_ref[...] = coded_rows(own_ref[:last], other[:last])


def join_kernel(offsets, receivers_ref, *refs):
    given, blocks = refs[:offsets], refs[offsets:]
    group = receivers_ref.shape[0] // len(blocks)
    sources = [ref[...].astype(jnp.float32) for ref in given]
    receivers = receivers_ref[...].astype(jnp.float32)
    for m, block in enumerate(blocks):
        rows = [receivers[m * group : (m + 1) * group]] + sources
        block[...] = jnp.concatenate(rows, axis=0).astype(jnp.bfloat16)


def finished_shards(runs, held):
    chips, height, width = held.shape
    length = width - 2 * LANES
    chip = lax.div(lax.axis_index("tm"), CORES)
    for m in range(chips):
        held[chip ^ m] = runs[m]
    left = lax.broadcasted_iota(jnp.int32, (height, LANES), 1) < W2
    tail = length - LANES
    end_values, end_levels = [], []

    def lanes(c, first):
        return held[c, :, first : first + LANES].astype(jnp.float32)

    for c in range(chips):
        high = jnp.where(left, lanes(c, 0), lanes(c, tail))
        end_values.append(high + lanes(c, length))
        end_levels.append(lanes(c, length + LANES))

    def meeting(ends, outside):
        outside = [jnp.full((height, LANES), outside, jnp.float32)]
        return [
            jnp.where(left, after, before)
            for before, after in zip(outside + ends, ends + outside)
        ]

    def across(p, t):
        at_p, at_t = jnp.where(p < W2, p, p - LANES), jnp.where(t < W2, t, t - LANES)
        return ((p < W2) != (t < W2)) & (jnp.abs(at_p - at_t) <= W2)

    values, levels = meeting(end_values, 0.0), meeting(end_levels, 1.0)
    added = banded_sums(
        [jnp.abs(v) * l for v, l in zip(values, levels)],
        band_matrix(LANES, LANES, across),
    )
    ends = [
        v * l / (l + a / (2 * W2 + 1)) for v, l, a in zip(values, levels, added)
    ]
    shard = length // CORES
    for k in range(chips * CORES):
        c, part = k // CORES, k % CORES
        pieces = [held[c, :, part * shard : (part + 1) * shard]]
        if part == 0:
            head = jnp.where(left, ends[c], lanes(c, 0)).astype(held.dtype)
            pieces = [head, held[c, :, LANES:shard]]
        if part == CORES - 1:
            last = jnp.where(left, lanes(c, tail), ends[c + 1]).astype(held.dtype)
            pieces = [held[c, :, part * shard : tail], last]
        yield jnp.concatenate(pieces, axis=1)


def lane_numbers(rows, dtype):
    return lax.broadcasted_iota(jnp.int32, (rows, LANES), 1).astype(dtype)


def shifted(rows, shift):
    height, length = rows.shape
    nothing = jnp.zeros((height, LANES), rows.dtype)
    if not shift:
        return jnp.concatenate([rows, nothing], axis=1)
    turned = [
        pltpu.roll(rows[:, first : first + LANES], shift, 1)
        for first in range(0, length, LANES)
    ]
    behind = lane_numbers(height, rows.dtype) >= shift
    return jnp.concatenate(
        [
            jnp.where(behind, here, before)
            for before, here in zip([nothing] + turned, turned + [nothing])
        ],
        axis=1,
    )


def correlate_kernel(offsets, scale, *refs):
    chips = len(refs) - offsets - 3
    blocks, refs = refs[:chips], refs[chips:]
    outs, (held, mixed, table) = refs[:offsets], refs[offsets:]
    sources = offsets * SRC
    group = held.shape[1] - sources
    runs = [ref[...].astype(held.dtype) for ref in blocks[:1] + blocks[:0:-1]]
    product = None
    for wide in finished_shards(runs, held):
        receivers, senders = wide[:group], wide[group:]
        fine = [shifted(receivers, MAXLAG - j) for j in range(FINE)]
        coarse = [shifted(senders, FINE * i) for i in range(COARSE)]
        term = lax.dot_general(
            jnp.concatenate(fine, axis=0).astype(jnp.bfloat16),
            jnp.concatenate(coarse, axis=0).astype(jnp.bfloat16),
            (((1,), (1,)), ((), ())),
            preferred_element_type=jnp.float32,
        )
        product = term if product is None else product + term
    product = product * scale
    for h in range(mixed.shape[0]):
        first, last = h * LANES, min((h + 1) * LANES, COARSE * sources)
        for j in range(FINE):
            mixed[h, pl.ds(j, group, stride=FINE), : last - first] = product[
                j * group : (j + 1) * group, first:last
            ]
        table[h * LANES : (h + 1) * LANES] = mixed[h].T.astype(table.dtype)
    columns = table.shape[1]
    turned = []
    for i in range(COARSE):
        block = table[i * sources : (i + 1) * sources]
        turned.append(pltpu.roll(block, FINE * i, 1) if i else block)
    lane = lane_numbers(sources, table.dtype)
    width = group * LAGS

    def place(tiles, tile, piece, low):
        if low and tile in tiles:
            piece = jnp.where(lane >= low, piece, tiles[tile])
        tiles[tile] = piece

    tiles = {}
    for b in range(group):
        joined = {}
        for i in range(COARSE):
            tile, low = divmod((b + i) * FINE % columns, LANES)
            piece = turned[i][:, tile * LANES : (tile + 1) * LANES]
            place(joined, tile, piece, low)
        turn = b * (LAGS - FINE) % LANES
        if turn:
            joined = {tile: pltpu.roll(v, turn, 1) for tile, v in joined.items()}
        for lag in range(LAGS):
            at, to = (b * FINE + lag) % columns, b * LAGS + lag
            if lag == 0 or at % LANES == 0 or to % LANES == 0:
                place(tiles, to // LANES, joined[at // LANES], to % LANES)
    first_core = lax.rem(lax.axis_index("tm"), CORES) == 0
    for tile, value in tiles.items():
        first = tile * LANES
        last = min(first + LANES, width)
        for o in range(offsets):
            wide = value.astype(jnp.float32)[:, : last - first]
            rows = [wide[p * SRC : (p + 1) * SRC] for p in (o, offsets - 1 - o)]
            rows = jnp.where(first_core, rows[0], rows[1])
            outs[o][:, first:last] = rows.astype(jnp.bfloat16)


def stack_kernel(*refs):
    *given, out_ref = refs
    first_core = lax.rem(lax.axis_index("tm"), CORES) == 0
    values = [ref[...].astype(jnp.float32) for ref in given]
    for o, value in enumerate(values):
        out_ref[:, o, :] = jnp.where(first_core, values[len(values) - 1 - o], value)


def call(kernel, out_shape, inputs, scratch=(), flops=0):
    single = not isinstance(out_shape, list)
    spec = pl.BlockSpec(memory_space=pltpu.VMEM)
    moved = sum(v.size * v.dtype.itemsize for v in inputs)
    return pl.pallas_call(
        kernel,
        out_shape=out_shape,
        in_specs=[spec] * len(inputs),
        out_specs=spec if single else [spec] * len(out_shape),
        scratch_shapes=list(scratch),
        compiler_params=pltpu.CompilerParams(vmem_limit_bytes=32 * 1024 * 1024),
        cost_estimate=pl.CostEstimate(
            flops=flops, bytes_accessed=moved, transcendentals=0
        ),
    )(*inputs)


def swapped(block, axis, m):
    devices = range(lax.axis_size(axis))
    return lax.ppermute(block, axis, [(k, k ^ m) for k in devices])


def passed_along(block, distance):
    devices = range(lax.axis_size("chan"))
    route = [((i - distance) % len(devices), i) for i in devices]
    return lax.ppermute(block, "chan", route)


def exchanged(block, distance):
    count, places = lax.axis_size("chan"), lax.axis_size("tm")
    route = []
    for i in range(count):
        for k in range(places):
            turn = distance if k % CORES == 0 else -distance
            route.append((i * places + k, (i + turn) % count * places + (k ^ 1)))
    return lax.ppermute(block, ("chan", "tm"), route)


def body(strain_rate):
    channels, length = strain_rate.shape
    shards = lax.axis_size("tm")
    chips = shards // CORES
    reach = lax.axis_size("chan") // 4
    group = channels // shards
    steps = list(range(-reach, 0)) + list(range(1, reach + 1))
    offsets = len(steps)
    sources = offsets * SRC
    scale = 1.0 / math.sqrt(length * shards)
    run = CORES * length
    coded = run + 2 * LANES

    other = swapped(strain_rate, "tm", 1)
    own = call(
        functools.partial(pack_kernel, group, chips),
        jax.ShapeDtypeStruct((chips * group + SRC, length), jnp.float32),
        [strain_rate],
        flops=8 * channels * length,
    )
    own_sources = call(
        functools.partial(code_sources_kernel, group, chips),
        jax.ShapeDtypeStruct((SRC, coded), jnp.bfloat16),
        [own, other],
    )
    arrived = [passed_along(own_sources, d) for d in steps]
    own_receivers = call(
        functools.partial(code_receivers_kernel, group, chips),
        jax.ShapeDtypeStruct((chips * group, coded), jnp.bfloat16),
        [own, other],
        flops=8 * chips * group * run * (256 + 2 * LANES),
    )
    blocks = call(
        functools.partial(join_kernel, offsets),
        [jax.ShapeDtypeStruct((group + sources, coded), jnp.bfloat16)] * chips,
        [own_receivers] + arrived,
    )
    blocks = list(blocks[:1]) + [
        swapped(blocks[m], "tm", CORES * m) for m in range(chips - 1, 0, -1)
    ]
    columns = -(-group * FINE // LANES) * LANES
    heights = -(-COARSE * sources // LANES) * LANES
    kind = jnp.float32 if group % 16 or sources % 16 else jnp.bfloat16
    results = call(
        functools.partial(correlate_kernel, offsets, scale),
        [jax.ShapeDtypeStruct((SRC, group * LAGS), jnp.bfloat16)] * offsets,
        blocks,
        scratch=[
            pltpu.VMEM((chips, group + sources, coded), kind),
            pltpu.VMEM((heights // LANES, columns, LANES), jnp.float32),
            pltpu.VMEM((heights, columns), kind),
        ],
        flops=2 * shards * (length + LANES) * group * FINE * COARSE * sources,
    )
    arrived = [exchanged(r, -d) for r, d in zip(results, steps)]
    return call(
        stack_kernel,
        jax.ShapeDtypeStruct((SRC, offsets, group * LAGS), jnp.float32),
        arrived,
    )


def solution(mesh):
    placed = (P("chan", "tm"),)
    return jax.shard_map(
        body, mesh=mesh, in_specs=placed, out_specs=P("chan", None, "tm"), check_vma=False
    )
```

```python
import functools
import math

import jax
import jax.numpy as jnp
from jax import lax
from jax.experimental import pallas as pl
from jax.experimental.pallas import tpu as pltpu
from jax.sharding import PartitionSpec as P

SRC = 8
MAXLAG = 25
W2 = 64
LAGS = 51
FINE = 8
COARSE = -(-LAGS // FINE)
LANES = 128
CORES = 2


def band_matrix(rows, columns, related):
    p = lax.broadcasted_iota(jnp.int32, (rows, columns), 0)
    t = lax.broadcasted_iota(jnp.int32, (rows, columns), 1)
    return jnp.where(related(p, t), 1.0, 0.0).astype(jnp.bfloat16)


def halves(values):
    high = values.astype(jnp.bfloat16).astype(jnp.float32)
    return high, values - high


def banded_sums(pieces, band):
    height = pieces[0].shape[0]
    parts = [halves(piece) for piece in pieces]
    stacked = jnp.concatenate([p[0] for p in parts] + [p[1] for p in parts], axis=0)
    sums = jnp.dot(
        stacked.astype(jnp.bfloat16), band, preferred_element_type=jnp.float32
    )
    count = len(pieces)
    return [
        sums[c * height : (c + 1) * height]
        + sums[(count + c) * height : (count + c + 1) * height]
        for c in range(count)
    ]


def level(window_sums):
    return window_sums / (2 * W2 + 1) + 1e-05


def rows_for_here(ref, group, chips):
    me = lax.axis_index("tm")
    every = ref.shape[0] // SRC
    pieces = []
    for m in range(chips):
        start = pl.multiple_of((me ^ (CORES * m + 1)) * group, group)
        pieces.append(ref[pl.ds(start, group)])
    pieces += [ref[q * every : q * every + 1] for q in range(SRC)]
    return jnp.concatenate(pieces, axis=0)


def pack_kernel(group, chips, x_ref, out_ref):
    out_ref[...] = rows_for_here(x_ref, group, chips)


def coded_rows(own, other):
    first_core = lax.rem(lax.axis_index("tm"), CORES) == 0
    x = jnp.concatenate(
        [jnp.where(first_core, own, other), jnp.where(first_core, other, own)], axis=1
    )
    height, length = x.shape
    border = jnp.zeros((height, LANES), jnp.float32)
    magnitude = jnp.concatenate([border, jnp.abs(x), border], axis=1)
    inner = min(256, length)
    band = band_matrix(
        inner + 2 * LANES, inner, lambda p, t: jnp.abs(p - LANES - t) <= W2
    )
    sums = jnp.concatenate(
        banded_sums(
            [
                magnitude[:, start : start + inner + 2 * LANES]
                for start in range(0, length, inner)
            ],
            band,
        ),
        axis=1,
    )
    levels = level(sums)
    normed = x / levels
    left = lax.broadcasted_iota(jnp.int32, (height, LANES), 1) < W2
    tail = length - LANES
    ends = jnp.where(left, normed[:, :LANES], normed[:, tail:])
    end_levels = jnp.where(left, levels[:, :LANES], levels[:, tail:])
    coded = jnp.concatenate([normed, halves(ends)[1], end_levels], axis=1)
    return coded.astype(jnp.bfloat16)


def code_sources_kernel(group, chips, own_ref, other_ref, out_ref):
    first = chips * group
    other = rows_for_here(other_ref, group, chips)
    out_ref[...] = coded_rows(own_ref[first:], other[first:])


def code_receivers_kernel(group, chips, own_ref, other_ref, out_ref):
    last = chips * group
    other = rows_for_here(other_ref, group, chips)
    out_ref[...] = coded_rows(own_ref[:last], other[:last])


def join_kernel(offsets, receivers_ref, *refs):
    given, blocks = refs[:offsets], refs[offsets:]
    group = receivers_ref.shape[0] // len(blocks)
    sources = [ref[...].astype(jnp.float32) for ref in given]
    receivers = receivers_ref[...].astype(jnp.float32)
    for m, block in enumerate(blocks):
        rows = [receivers[m * group : (m + 1) * group]] + sources
        block[...] = jnp.concatenate(rows, axis=0).astype(jnp.bfloat16)


def finished_shards(runs, held):
    chips, height, width = held.shape
    length = width - 2 * LANES
    chip = lax.div(lax.axis_index("tm"), CORES)
    for m in range(chips):
        held[chip ^ m] = runs[m]
    left = lax.broadcasted_iota(jnp.int32, (height, LANES), 1) < W2
    tail = length - LANES
    end_values, end_levels = [], []

    def lanes(c, first):
        return held[c, :, first : first + LANES].astype(jnp.float32)

    for c in range(chips):
        high = jnp.where(left, lanes(c, 0), lanes(c, tail))
        end_values.append(high + lanes(c, length))
        end_levels.append(lanes(c, length + LANES))

    def meeting(ends, outside):
        outside = [jnp.full((height, LANES), outside, jnp.float32)]
        return [
            jnp.where(left, after, before)
            for before, after in zip(outside + ends, ends + outside)
        ]

    def across(p, t):
        at_p, at_t = jnp.where(p < W2, p, p - LANES), jnp.where(t < W2, t, t - LANES)
        return ((p < W2) != (t < W2)) & (jnp.abs(at_p - at_t) <= W2)

    values, levels = meeting(end_values, 0.0), meeting(end_levels, 1.0)
    added = banded_sums(
        [jnp.abs(v) * l for v, l in zip(values, levels)],
        band_matrix(LANES, LANES, across),
    )
    ends = [
        v * l / (l + a / (2 * W2 + 1)) for v, l, a in zip(values, levels, added)
    ]
    shard = length // CORES
    for k in range(chips * CORES):
        c, part = k // CORES, k % CORES
        pieces = [held[c, :, part * shard : (part + 1) * shard]]
        if part == 0:
            head = jnp.where(left, ends[c], lanes(c, 0)).astype(held.dtype)
            pieces = [head, held[c, :, LANES:shard]]
        if part == CORES - 1:
            last = jnp.where(left, lanes(c, tail), ends[c + 1]).astype(held.dtype)
            pieces = [held[c, :, part * shard : tail], last]
        yield jnp.concatenate(pieces, axis=1)


def lane_numbers(rows, dtype):
    return lax.broadcasted_iota(jnp.int32, (rows, LANES), 1).astype(dtype)


def shifted(rows, shift):
    height, length = rows.shape
    nothing = jnp.zeros((height, LANES), rows.dtype)
    if not shift:
        return jnp.concatenate([rows, nothing], axis=1)
    turned = [
        pltpu.roll(rows[:, first : first + LANES], shift, 1)
        for first in range(0, length, LANES)
    ]
    behind = lane_numbers(height, rows.dtype) >= shift
    return jnp.concatenate(
        [
            jnp.where(behind, here, before)
            for before, here in zip([nothing] + turned, turned + [nothing])
        ],
        axis=1,
    )


def correlate_kernel(offsets, scale, *refs):
    chips = len(refs) - offsets - 3
    blocks, refs = refs[:chips], refs[chips:]
    outs, (held, mixed, table) = refs[:offsets], refs[offsets:]
    sources = offsets * SRC
    group = held.shape[1] - sources
    runs = [ref[...].astype(held.dtype) for ref in blocks[:1] + blocks[:0:-1]]
    product = None
    for wide in finished_shards(runs, held):
        receivers, senders = wide[:group], wide[group:]
        fine = [shifted(receivers, MAXLAG - j) for j in range(FINE)]
        coarse = [shifted(senders, FINE * i) for i in range(COARSE)]
        term = lax.dot_general(
            jnp.concatenate(fine, axis=0).astype(jnp.bfloat16),
            jnp.concatenate(coarse, axis=0).astype(jnp.bfloat16),
            (((1,), (1,)), ((), ())),
            preferred_element_type=jnp.float32,
        )
        product = term if product is None else product + term
    product = product * scale
    for h in range(mixed.shape[0]):
        first, last = h * LANES, min((h + 1) * LANES, COARSE * sources)
        for j in range(FINE):
            mixed[h, pl.ds(j, group, stride=FINE), : last - first] = product[
                j * group : (j + 1) * group, first:last
            ]
        table[h * LANES : (h + 1) * LANES] = mixed[h].T.astype(table.dtype)
    columns = table.shape[1]
    turned = []
    for i in range(COARSE):
        block = table[i * sources : (i + 1) * sources]
        turned.append(pltpu.roll(block, FINE * i, 1) if i else block)
    lane = lane_numbers(sources, table.dtype)
    width = group * LAGS

    def place(tiles, tile, piece, low):
        if low and tile in tiles:
            piece = jnp.where(lane >= low, piece, tiles[tile])
        tiles[tile] = piece

    tiles = {}
    for b in range(group):
        joined = {}
        for i in range(COARSE):
            tile, low = divmod((b + i) * FINE % columns, LANES)
            piece = turned[i][:, tile * LANES : (tile + 1) * LANES]
            place(joined, tile, piece, low)
        turn = b * (LAGS - FINE) % LANES
        if turn:
            joined = {tile: pltpu.roll(v, turn, 1) for tile, v in joined.items()}
        for lag in range(LAGS):
            at, to = (b * FINE + lag) % columns, b * LAGS + lag
            if lag == 0 or at % LANES == 0 or to % LANES == 0:
                place(tiles, to // LANES, joined[at // LANES], to % LANES)
    first_core = lax.rem(lax.axis_index("tm"), CORES) == 0
    for tile, value in tiles.items():
        first = tile * LANES
        last = min(first + LANES, width)
        for o in range(offsets):
            wide = value.astype(jnp.float32)[:, : last - first]
            rows = [wide[p * SRC : (p + 1) * SRC] for p in (o, offsets - 1 - o)]
            rows = jnp.where(first_core, rows[0], rows[1])
            outs[o][:, first:last] = rows.astype(jnp.bfloat16)


def stack_kernel(*refs):
    given, out_ref = refs[:-1][::-1], refs[-1]
    first_core = lax.rem(lax.axis_index("tm"), CORES) == 0
    values = [ref[...].astype(jnp.float32) for ref in given]
    for o, value in enumerate(values):
        out_ref[:, o, :] = jnp.where(first_core, values[len(values) - 1 - o], value)


def call(kernel, out_shape, inputs, scratch=(), flops=0):
    single = not isinstance(out_shape, list)
    spec = pl.BlockSpec(memory_space=pltpu.VMEM)
    moved = sum(v.size * v.dtype.itemsize for v in inputs)
    return pl.pallas_call(
        kernel,
        out_shape=out_shape,
        in_specs=[spec] * len(inputs),
        out_specs=spec if single else [spec] * len(out_shape),
        scratch_shapes=list(scratch),
        compiler_params=pltpu.CompilerParams(vmem_limit_bytes=32 * 1024 * 1024),
        cost_estimate=pl.CostEstimate(
            flops=flops, bytes_accessed=moved, transcendentals=0
        ),
    )(*inputs)


def swapped(block, axis, m):
    devices = range(lax.axis_size(axis))
    return lax.ppermute(block, axis, [(k, k ^ m) for k in devices])


def passed_along(block, distance):
    devices = range(lax.axis_size("chan"))
    route = [((i - distance) % len(devices), i) for i in devices]
    return lax.ppermute(block, "chan", route)


def exchanged(block, distance):
    count, places = lax.axis_size("chan"), lax.axis_size("tm")
    route = []
    for i in range(count):
        for k in range(places):
            turn = distance if k % CORES == 0 else -distance
            route.append((i * places + k, (i + turn) % count * places + (k ^ 1)))
    return lax.ppermute(block, ("chan", "tm"), route)


def body(strain_rate):
    channels, length = strain_rate.shape
    shards = lax.axis_size("tm")
    chips = shards // CORES
    reach = lax.axis_size("chan") // 4
    group = channels // shards
    steps = list(range(-reach, 0)) + list(range(1, reach + 1))
    offsets = len(steps)
    sources = offsets * SRC
    scale = 1.0 / math.sqrt(length * shards)
    run = CORES * length
    coded = run + 2 * LANES

    other = swapped(strain_rate, "tm", 1)
    own = call(
        functools.partial(pack_kernel, group, chips),
        jax.ShapeDtypeStruct((chips * group + SRC, length), jnp.float32),
        [strain_rate],
        flops=8 * channels * length,
    )
    own_sources = call(
        functools.partial(code_sources_kernel, group, chips),
        jax.ShapeDtypeStruct((SRC, coded), jnp.bfloat16),
        [own, other],
    )
    arrived = [passed_along(own_sources, d) for d in steps]
    own_receivers = call(
        functools.partial(code_receivers_kernel, group, chips),
        jax.ShapeDtypeStruct((chips * group, coded), jnp.bfloat16),
        [own, other],
        flops=8 * chips * group * run * (256 + 2 * LANES),
    )
    blocks = call(
        functools.partial(join_kernel, offsets),
        [jax.ShapeDtypeStruct((group + sources, coded), jnp.bfloat16)] * chips,
        [own_receivers] + arrived,
    )
    blocks = list(blocks[:1]) + [
        swapped(blocks[m], "tm", CORES * m) for m in range(chips - 1, 0, -1)
    ]
    columns = -(-group * FINE // LANES) * LANES
    heights = -(-COARSE * sources // LANES) * LANES
    kind = jnp.float32 if group % 16 or sources % 16 else jnp.bfloat16
    results = call(
        functools.partial(correlate_kernel, offsets, scale),
        [jax.ShapeDtypeStruct((SRC, group * LAGS), jnp.bfloat16)] * offsets,
        blocks,
        scratch=[
            pltpu.VMEM((chips, group + sources, coded), kind),
            pltpu.VMEM((heights // LANES, columns, LANES), jnp.float32),
            pltpu.VMEM((heights, columns), kind),
        ],
        flops=2 * shards * (length + LANES) * group * FINE * COARSE * sources,
    )
    arrived = [exchanged(r, -d) for r, d in zip(results, steps)]
    return call(
        stack_kernel,
        jax.ShapeDtypeStruct((SRC, offsets, group * LAGS), jnp.float32),
        arrived[::-1],
    )


def solution(mesh):
    placed = (P("chan", "tm"),)
    return jax.shard_map(
        body, mesh=mesh, in_specs=placed, out_specs=P("chan", None, "tm"), check_vma=False
    )
```
